32 devices in a mesh: runs: 2 (over y), sec: 4 (over z), mpo: 4 (over x, core), rep: 1.
Axes of the slice: x: 2, y: 2, z: 4, core: 2. Of those that a mesh axis runs over, the one named last changes fastest.
Arguments:
- wavefunction: float32 [8192, 256], P(('runs', 'sec'), 'rep'), parts along dimension 0, may hold values from -18 to 18
- left_blocks: float32 [64, 32, 128, 128], P(('runs', 'sec'), 'mpo'), parts along dimension 0, may hold values from -2 to 5
- right_blocks: float32 [64, 256, 256], P(('runs', 'mpo'), None, 'rep'), parts along dimension 0, may hold values from -2 to 5
- block_rows: int32 [64], P(('runs', 'sec')), parts along dimension 0, may hold values from 16 to 128, as said below
- term_charge: int32 [32], P('mpo'), may hold values from 0 to 4, as said below
Outputs:
- applied: float32 [8192, 256], P(('runs', 'sec'), 'rep'), parts along dimension 0
- correction: float32 [8192, 256], P(('runs', 'sec'), 'rep'), parts along dimension 0
The draws below stay inside these ranges and needn't reach their ends.
There are 2 independent parts, one for each index of `runs`. The reference program is written for one: setup_inputs(seed, part) draws one part's arguments, and reference() takes and returns one part's arrays. A program takes and returns all parts, laid end to end along the dimension named above; an argument that names none is the same for every part. Nothing has to cross between parts.
Inputs may be any that keep to these rules, and one draw needn't show every extreme that they name: `block_rows`: some sector is full and some has the fewest rows. `term_charge`: every class occurs.
All inputs are finite; a program needn't handle non-finite values.
Results may differ from the reference program's by a relative error of at most 0.0003.
Values sent between devices are 32-bit elements; how exact they have to be, the bound alone decides.
No kernel may reach another device: no remote copies, remote signals or barrier semaphores. Data moves between devices by JAX's collectives and lax.ppermute only.
A program may use at most 64 MiB of HBM per device.

```python
import jax
import jax.numpy as jnp
from jax import lax

BS = 128
CB = 256
W = 32
NSEC = 32
QD = 16
ROWS = 4096


def draw_wavefunction(key, part):
    key = jax.random.fold_in(key, 1)
    sector_of = (jnp.arange(ROWS, dtype=jnp.int32) // BS).astype(jnp.float32)
    ramp = sector_of / (NSEC - 1)
    values = jnp.clip(jax.random.normal(key, (ROWS, CB), jnp.float32), -6.0, 6.0)
    factor = jnp.exp(jnp.log(3.0) * ramp)
    return values * factor[:, None]


def dominant(key, shape, order, lead, gain_lo, gain_hi, scale):
    first, second = jax.random.split(key)
    noise = jnp.clip(jax.random.normal(first, shape, jnp.float32), -5.0, 5.0)
    gains = jax.random.uniform(second, shape[:lead] + (order, 1), jnp.float32, gain_lo, gain_hi)
    eye = jnp.eye(order, dtype=jnp.float32)
    return (noise / jnp.sqrt(float(order)) + eye * gains) * scale


def draw_left_blocks(key, part):
    key = jax.random.fold_in(key, 2)
    return dominant(key, (NSEC, W, BS, BS), BS, 2, 1.0, 2.0, 1.0)


def draw_right_blocks(key, part):
    key = jax.random.fold_in(key, 3)
    return dominant(key, (W, CB, CB), CB, 1, 1.0, 2.0, 1.0 / jnp.sqrt(float(W)))


def draw_block_rows(key, part):
    key = jax.random.fold_in(key, 4)
    first, second, third = jax.random.split(key, 3)
    fewest = max(1, BS // 8)
    values = jax.random.randint(first, (NSEC,), fewest, BS + 1, jnp.int32)
    full_at = jax.random.randint(second, (), 0, NSEC, jnp.int32)
    small_at = (full_at + 1 + jax.random.randint(third, (), 0, NSEC - 1, jnp.int32)) % NSEC
    index = jnp.arange(NSEC, dtype=jnp.int32)
    values = jnp.where(index == full_at, BS, values)
    values = jnp.where(index == small_at, fewest, values)
    return values.astype(jnp.int32)


def draw_term_charge(key, part):
    key = jax.random.fold_in(key, 5)
    classes = jnp.arange(W, dtype=jnp.int32) % 5
    return jax.random.permutation(key, classes).astype(jnp.int32)


def setup_inputs(seed: int = 0, part: int = 0) -> dict:
    seeds = jax.random.split(jax.random.key(seed), 6)
    part_splits = jax.random.split(jax.random.fold_in(seeds[5], part), 6)
    return {
        "wavefunction": draw_wavefunction(jax.random.fold_in(jax.random.fold_in(seeds[5], part), 71), part),
        "left_blocks": draw_left_blocks(jax.random.fold_in(jax.random.fold_in(seeds[5], part), 71), part),
        "right_blocks": draw_right_blocks(jax.random.fold_in(jax.random.fold_in(seeds[5], part), 71), part),
        "block_rows": draw_block_rows(jax.random.fold_in(jax.random.fold_in(seeds[5], part), 71), part),
        "term_charge": draw_term_charge(jax.random.fold_in(seeds[5], 71), part),
    }


def reference(wavefunction, left_blocks, right_blocks, block_rows, term_charge):
    row_index = jnp.arange(BS, dtype=jnp.int32)
    row_live = (row_index[None, :] < block_rows[:, None]).astype(jnp.float32)
    blocks = wavefunction.reshape(NSEC, BS, CB) * row_live[:, :, None]
    empty_far = jnp.zeros((QD, BS, CB), jnp.float32)
    empty_one = jnp.zeros((1, BS, CB), jnp.float32)
    above_blocks = jnp.concatenate([blocks[QD:], empty_far], axis=0)
    below_blocks = jnp.concatenate([empty_far, blocks[:-QD]], axis=0)
    next_blocks = jnp.concatenate([blocks[1:], empty_one], axis=0)
    prev_blocks = jnp.concatenate([empty_one, blocks[:-1]], axis=0)
    sources = jnp.stack([blocks, above_blocks, below_blocks, next_blocks, prev_blocks])

    def one_term(partial_sum, term):
        left_term = lax.dynamic_index_in_dim(left_blocks, term, 1, keepdims=False)
        right_term = lax.dynamic_index_in_dim(right_blocks, term, 0, keepdims=False)
        charge = lax.dynamic_index_in_dim(term_charge, term, 0, keepdims=False)
        source = lax.dynamic_index_in_dim(sources, charge, 0, keepdims=False)
        mixed = jnp.einsum('abc,acd->abd', left_term, source, precision=lax.Precision.HIGHEST)
        partial_sum = partial_sum + jnp.einsum('abd,de->abe', mixed, right_term, precision=lax.Precision.HIGHEST)
        return partial_sum, None

    start_sum = jnp.zeros((NSEC, BS, CB), jnp.float32)
    term_total, _ = lax.scan(one_term, start_sum, jnp.arange(W, dtype=jnp.int32))
    applied = term_total * row_live[:, :, None]
    rayleigh = jnp.sum(blocks * applied) / jnp.sum(blocks * blocks)
    correction = applied - rayleigh * blocks
    return applied.reshape(ROWS, CB), correction.reshape(ROWS, CB)
```

```python
import functools

import jax
import jax.numpy as jnp
from jax import lax
from jax.experimental import pallas as pl
from jax.experimental.pallas import tpu as pltpu
from jax.sharding import PartitionSpec as P

QD = 16
F32 = jnp.float32
BF16 = jnp.bfloat16
VMEM = pl.BlockSpec(memory_space=pltpu.VMEM)
SMEM = pl.BlockSpec(memory_space=pltpu.SMEM)
ANY = pl.BlockSpec(memory_space=pl.ANY)


def split(x):
    high = x.astype(BF16)
    return high, (x - high.astype(F32)).astype(BF16)


def dot3(a_high, a_low, b_high, b_low):
    dot = functools.partial(jnp.dot, preferred_element_type=F32)
    return dot(a_high, b_high) + (dot(a_low, b_high) + dot(a_high, b_low))


def masked(rows, live):
    index = lax.broadcasted_iota(jnp.int32, rows.shape, 0)
    return jnp.where(index < live, rows, 0.0)


def add_term(acc, src_high, src_low, offset, left, right, t_high, t_low):
    block = left.shape[-1]
    rows = acc.shape[0]
    r_high, r_low = split(right[...])
    window = pl.ds(pl.multiple_of(offset, block), rows)
    t_high[...], t_low[...] = split(dot3(src_high[window, :], src_low[window, :], r_high, r_low))
    for s in range(rows // block):
        here = pl.ds(s * block, block)
        l_high, l_low = split(left[s])
        acc[here, :] += dot3(l_high, l_low, t_high[here, :], t_low[here, :])


def copies(left, right, first, count, term, slot, lbuf, rbuf, sem):
    return (
        pltpu.make_async_copy(left.at[pl.ds(first, count), term], lbuf.at[slot], sem.at[0, slot]),
        pltpu.make_async_copy(right.at[term], rbuf.at[slot], sem.at[1, slot]),
    )


def near_kernel(half, first_at, info, rows_ref, cls, wave, halo, left, right, *rest):
    acc_in, rest = (rest[0], rest[1:]) if len(rest) == 8 else (None, rest)
    acc, src_high, src_low, lbuf, rbuf, sem, t_hl = rest
    terms = right.shape[0]
    block = left.shape[-1]
    core = info[0]
    first = core * half if first_at else 0

    def near(t):
        return jnp.logical_or(cls[t] == 0, cls[t] >= 3)

    for t in range(terms):

        @pl.when(near(t))
        def _():
            for copy in copies(left, right, first, half, t, t, lbuf, rbuf, sem):
                copy.start()

    acc[...] = jnp.zeros_like(acc) if acc_in is None else acc_in[...]
    at_halo = (half + 1) * core
    for s in range(half + 1):
        sector = core * (half - 1) + s
        rows = wave[pl.ds(pl.multiple_of(sector * block, block), block), :]
        at = pl.ds(pl.multiple_of((s + 1 - core) * block, block), block)
        src_high[at, :], src_low[at, :] = split(masked(rows, rows_ref[sector]))
    at = pl.ds(pl.multiple_of(at_halo * block, block), block)
    src_high[at, :], src_low[at, :] = split(halo[...])

    @pl.loop(0, terms)
    def _(t):
        @pl.when(near(t))
        def _():
            for copy in copies(left, right, first, half, t, t, lbuf, rbuf, sem):
                copy.wait()
            offset = jnp.where(cls[t] == 0, block, jnp.where(cls[t] == 3, 2 * block, 0))
            add_term(acc, src_high, src_low, offset, lbuf.at[t], rbuf.at[t], t_hl.at[0], t_hl.at[1])


def far_kernel(shift, merged, chunk_first, info, rows_ref, cls, cls_pair, wave, mine, other,
               left, right, left_pair, right_pair, acc_in, acc, sums, src_high, src_low,
               lbuf, rbuf, sem, t_hl):
    terms = right.shape[0]
    block = left.shape[-1]
    rows = acc.shape[0]
    count = rows // block
    core, side, sec, secs = info[0], info[1], info[2], info[3]
    half = left_pair.shape[0]
    own = (cls, left, right, core * half + chunk_first)
    pair = (cls_pair, left_pair, right_pair, chunk_first)

    def far(c):
        above = jnp.logical_and(c == 1, sec + shift < secs)
        return jnp.logical_or(above, jnp.logical_and(c == 2, sec >= shift))

    for g, (c, l, r, first) in enumerate((own, pair)):
        for t in range(terms):

            @pl.when(far(c[t]))
            def _(g=g, c=c, l=l, r=r, first=first, t=t):
                for copy in copies(l, r, first, count, t, g * terms + t, lbuf, rbuf, sem):
                    copy.start()

    part = rows // 2
    for k in range(mine.shape[0]):
        for ref, x in ((mine, side), (other, 1 - side)):
            at = pl.ds(pl.multiple_of(k * rows + x * part, part), part)
            src_high[at, :], src_low[at, :] = split(ref[k])
    acc[...] = acc_in[pl.ds(chunk_first * block, rows), :]

    for g, (c, l, r, first) in enumerate((own, pair)):

        @pl.loop(0, terms)
        def _(t, g=g, c=c, l=l, r=r, first=first):
            @pl.when(far(c[t]))
            def _():
                slot = g * terms + t
                for copy in copies(l, r, first, count, t, slot, lbuf, rbuf, sem):
                    copy.wait()
                offset = 0 if merged else jnp.where(c[t] == 1, 0, rows)
                add_term(acc, src_high, src_low, offset, lbuf.at[slot], rbuf.at[slot], t_hl.at[0], t_hl.at[1])

    cols = wave.shape[1]
    cross = jnp.zeros((8, cols), F32)
    square = jnp.zeros((8, cols), F32)
    for s in range(count):
        sector = core * half + chunk_first + s
        live = wave[pl.ds(pl.multiple_of(sector * block, block), block), :]
        live = masked(live, rows_ref[sector])
        part_sum = live * acc[pl.ds(s * block, block), :]
        cross += jnp.sum(part_sum.reshape(block // 8, 8, cols), axis=0)
        square += jnp.sum((live * live).reshape(block // 8, 8, cols), axis=0)
    fold = lambda v: sum(v[:, i : i + 128] for i in range(0, cols, 128))
    sums[0:8, :] = fold(cross)
    sums[8:16, :] = fold(square)


def final_kernel(sides, info, rows_ref, sums, wave, total, total_pair, applied, correction, buf, sem):
    core = info[0]
    block = wave.shape[0] // rows_ref.shape[0]
    half = total.shape[0] // block
    rayleigh = jnp.sum(sums[0:8, :]) / (jnp.sum(sums[8:16, :]) * (1.0 / sides))
    for part, (ref, c) in enumerate(((total, core), (total_pair, 1 - core))):
        for s in range(half):
            sector = c * half + s
            at = pl.ds(pl.multiple_of(sector * block, block), block)
            rows = masked(ref[pl.ds(s * block, block), :], rows_ref[sector])
            here = part * half + s
            buf[0, here] = rows
            buf[1, here] = rows - rayleigh * masked(wave[at, :], rows_ref[sector])
            pltpu.make_async_copy(buf.at[0, here], applied.at[at, :], sem.at[0, here]).start()
            pltpu.make_async_copy(buf.at[1, here], correction.at[at, :], sem.at[1, here]).start()
    for here in range(2 * half):
        pltpu.make_async_copy(buf.at[0, here], applied.at[pl.ds(0, block), :], sem.at[0, here]).wait()
        pltpu.make_async_copy(buf.at[1, here], correction.at[pl.ds(0, block), :], sem.at[1, here]).wait()


def params(limit):
    return pltpu.CompilerParams(vmem_limit_bytes=limit * 2**20)


def cost(flops, moved):
    return pl.CostEstimate(flops=int(flops), bytes_accessed=int(moved), transcendentals=0)


def swap(array, axis, bit):
    pairs = [(i, i ^ bit) for i in range(lax.axis_size(axis))]
    return lax.ppermute(array, axis, pairs)


def local(wavefunction, left_blocks, right_blocks, block_rows, term_charge):
    sector_count = block_rows.shape[0]
    block = left_blocks.shape[2]
    terms = left_blocks.shape[1]
    cols = wavefunction.shape[1]
    secs, mpos, reps = (lax.axis_size(a) for a in ("sec", "mpo", "rep"))
    sec, mpo = lax.axis_index("sec"), lax.axis_index("mpo")
    core, side = mpo % 2, mpo // 2 % 2
    half = sector_count // 2
    shift = QD // sector_count
    merged = secs <= 2 * shift
    info = jnp.stack([core, side, sec, jnp.int32(secs)]).astype(jnp.int32)

    whole = wavefunction
    if reps > 1:
        whole = lax.all_gather(wavefunction, "rep", axis=1, tiled=True)
    wide = whole.shape[1]
    index = jnp.arange(sector_count * block, dtype=jnp.int32)

    def live_rows(start, length):
        row = start + jnp.arange(length, dtype=jnp.int32)
        live = row % block < block_rows[row // block]
        return jnp.where(live[:, None], lax.dynamic_slice_in_dim(whole, start, length, 0), 0.0)

    chunk = half * block
    mine = live_rows(core * chunk + side * (chunk // 2), chunk // 2)
    up = [(i, i - shift) for i in range(shift, secs)]
    down = [(i, i + shift) for i in range(secs - shift)]
    if merged:
        mine = lax.ppermute(mine, "sec", up + down)[None]
    else:
        mine = jnp.stack([lax.ppermute(mine, "sec", p) for p in (up, down)])
    halo = live_rows((1 - core) * (sector_count - 1) * block, block)
    pairs = []
    for m in range(mpos):
        for z in range(secs):
            to = z + 1 if m % 2 == 0 else z - 1
            if 0 <= to < secs:
                pairs.append((z * mpos + m, to * mpos + m))
    halo = lax.ppermute(halo, ("sec", "mpo"), pairs)
    right_pair = swap(right_blocks, "mpo", 1)
    left_pair = swap(lax.dynamic_slice_in_dim(left_blocks, (1 - core) * half, half, 0), "mpo", 1)
    cls_pair = swap(term_charge, "mpo", 1)

    scratch = [
        pltpu.VMEM((half * block + 2 * block, wide), BF16),
        pltpu.VMEM((half * block + 2 * block, wide), BF16),
        pltpu.VMEM((terms, half, block, block), F32),
        pltpu.VMEM((terms, wide, cols), F32),
        pltpu.SemaphoreType.DMA((2, terms)),
        pltpu.VMEM((2, half * block, cols), BF16),
    ]
    term_flops = 6 * half * block * cols * (wide + block)
    acc = None
    for at, cls, left, right in (
        (True, term_charge, left_blocks, right_blocks),
        (False, cls_pair, left_pair, right_pair),
    ):
        args = (info, block_rows, cls, whole, halo, left, right)
        specs = [SMEM, SMEM, SMEM, VMEM, VMEM, ANY, ANY]
        if acc is not None:
            args, specs = args + (acc,), specs + [VMEM]
        acc = pl.pallas_call(
            functools.partial(near_kernel, half, at),
            out_shape=jax.ShapeDtypeStruct((half * block, cols), F32),
            in_specs=specs,
            out_specs=VMEM,
            scratch_shapes=scratch,
            compiler_params=params(32),
            cost_estimate=cost(terms * term_flops, 4 * terms * (half * block * block + wide * cols)),
            name="near_terms",
        )(*args)

    other = swap(mine, "mpo", 2)
    parts = 1 if merged else 2
    partial, sums = pl.pallas_call(
        functools.partial(far_kernel, shift, merged, 0),
        out_shape=(
            jax.ShapeDtypeStruct((half * block, cols), F32),
            jax.ShapeDtypeStruct((16, 128), F32),
        ),
        in_specs=[SMEM] * 4 + [VMEM] * 3 + [ANY] * 4 + [VMEM],
        out_specs=(VMEM, VMEM),
        scratch_shapes=[
            pltpu.VMEM((parts * half * block, wide), BF16),
            pltpu.VMEM((parts * half * block, wide), BF16),
            pltpu.VMEM((2 * terms, half, block, block), F32),
            pltpu.VMEM((2 * terms, wide, cols), F32),
            pltpu.SemaphoreType.DMA((2, 2 * terms)),
            pltpu.VMEM((2, half * block, cols), BF16),
        ],
        compiler_params=params(32),
        cost_estimate=cost(4 * term_flops, 4 * 4 * (half * block * block + wide * cols)),
        name="far_terms",
    )(info, block_rows, term_charge, cls_pair, wavefunction, mine, other,
      left_blocks, right_blocks, left_pair, right_pair, acc)

    recv = swap(partial, "mpo", 2)
    if secs & (secs - 1) == 0 and secs <= 4:
        bit = 1
        while bit < secs:
            sums = sums + swap(sums, "sec", bit)
            bit *= 2
    else:
        sums = lax.psum(sums, "sec")
    if reps > 1:
        sums = lax.psum(sums, "rep")
    sums = sums + swap(sums, "mpo", 2)
    sums = sums + swap(sums, "mpo", 1)
    total = partial + recv
    total_pair = swap(total, "mpo", 1)

    out = jax.ShapeDtypeStruct((sector_count * block, cols), F32)
    return pl.pallas_call(
        functools.partial(final_kernel, mpos // 2),
        out_shape=(out, out),
        in_specs=[SMEM] * 2 + [VMEM] * 4,
        out_specs=(ANY, ANY),
        scratch_shapes=[
            pltpu.VMEM((2, sector_count, block, cols), F32),
            pltpu.SemaphoreType.DMA((2, sector_count)),
        ],
        compiler_params=params(32),
        cost_estimate=cost(8 * sector_count * block * cols, 12 * sector_count * block * cols),
        name="residual",
    )(info, block_rows, sums, wavefunction, total, total_pair)


def solution(mesh):
    in_specs = (
        P(("runs", "sec"), "rep"),
        P(("runs", "sec"), "mpo", None, None),
        P(("runs", "mpo"), None, "rep"),
        P(("runs", "sec")),
        P("mpo"),
    )
    out_specs = (P(("runs", "sec"), "rep"), P(("runs", "sec"), "rep"))
    return jax.shard_map(local, mesh=mesh, in_specs=in_specs, out_specs=out_specs, check_vma=False)
```

```python
import functools

import jax
import jax.numpy as jnp
from jax import lax
from jax.experimental import pallas as pl
from jax.experimental.pallas import tpu as pltpu
from jax.sharding import PartitionSpec as P

QD = 16
F32 = jnp.float32
BF16 = jnp.bfloat16
VMEM = pl.BlockSpec(memory_space=pltpu.VMEM)
SMEM = pl.BlockSpec(memory_space=pltpu.SMEM)
HBM = pl.BlockSpec(memory_space=pltpu.HBM)
ANY = pl.BlockSpec(memory_space=pl.ANY)


def split(x):
    high = x.astype(BF16)
    return high, (x - high.astype(F32)).astype(BF16)


def masked(rows, live):
    index = lax.broadcasted_iota(jnp.int32, rows.shape, 0)
    return jnp.where(index < live, rows, 0.0)


GROUP = 2


def place():
    mpo = lax.axis_index("mpo")
    return lax.rem(mpo, 2), lax.rem(lax.div(mpo, 2), 2), lax.axis_index("sec")


def sector_rows(wave, sector, block):
    return wave.at[pl.ds(pl.multiple_of(sector * block, block), block), :]


def source_kernel(half, rows_ref, wave, mine, halo, sem):
    core, side, _ = place()
    block = mine.shape[0]
    count = rows_ref.shape[0]
    wanted = ((core * half + side, mine), ((1 - core) * (count - 1), halo))
    moves = [
        pltpu.make_async_copy(sector_rows(wave, sector, block), ref, sem.at[i])
        for i, (sector, ref) in enumerate(wanted)
    ]
    for move in moves:
        move.start()
    for move, (sector, ref) in zip(moves, wanted):
        move.wait()
        ref[...] = masked(ref[...], rows_ref[sector])


def pair_kernel(half, rows_ref, wave, left, mine, left_send, sem):
    core, side, _ = place()
    block = mine.shape[0]
    sector = core * half + half // 2 + side
    send = pltpu.make_async_copy(left.at[pl.ds((1 - core) * half, half)], left_send, sem.at[0])
    send.start()
    move = pltpu.make_async_copy(sector_rows(wave, sector, block), mine, sem.at[1])
    move.start()
    move.wait()
    mine[...] = masked(mine[...], rows_ref[sector])
    send.wait()


def terms_kernel(spec, *refs):
    refs = list(refs)
    take = lambda n: [refs.pop(0) for _ in range(n)]
    rows_hbm, wave = take(2)
    groups = [take(3) for _ in spec["groups"]]
    halo = take(1)[0] if spec["near"] else None
    mine, other = take(2) if spec["far"] else (None, None)
    acc_in = take(1)[0] if spec["acc"] is not None else None
    sums_in = take(1)[0] if spec["sums_in"] else None
    acc = take(1)[0]
    sums = take(1)[0] if spec["sums"] else None
    src, tbuf, rows_ref, cls_ref, order, offsets, sem = refs

    half, lo, secs, shift = (spec[k] for k in ("half", "lo", "secs", "shift"))
    rows, cols = acc.shape
    block = rows // spec["count"]
    count = spec["count"]
    core, side, sec = place()
    merged = secs <= 2 * shift
    far_at = (count + 2) * block if spec["near"] else 0
    below_at = far_at if merged else far_at + rows

    moves = [pltpu.make_async_copy(rows_hbm, rows_ref, sem.at[0])]
    for i, (cls, _, _) in enumerate(groups):
        moves.append(pltpu.make_async_copy(cls, cls_ref.at[i], sem.at[i + 1]))
    for move in moves:
        move.start()
    if acc_in is None:
        acc[...] = jnp.zeros_like(acc)
    else:
        acc[...] = acc_in[pl.ds(spec["acc"] * block, rows), :]

    def put(at, value):
        wide = value.shape[1]
        high, low = split(value)
        here = pl.ds(pl.multiple_of(at, block // 2), value.shape[0])
        src[here, 0:wide] = high
        src[here, wide : 2 * wide] = low
        src[here, 2 * wide : 3 * wide] = high

    if spec["far"]:
        for k in range(mine.shape[0]):
            for ref, x in ((mine, side), (other, 1 - side)):
                put(far_at + k * rows + x * ref.shape[1], ref[k])
    for move in moves:
        move.wait()
    if spec["near"]:
        for i in range(count + 2):
            sector = core * half + lo - 1 + i
            inside = jnp.logical_and(sector >= 0, sector < rows_ref.shape[0])
            if 0 < i < count + 1:
                inside = True

            @pl.when(inside)
            def _(i=i, sector=sector):
                put(i * block, masked(sector_rows(wave, sector, block)[...], rows_ref[sector]))

            if inside is not True:

                @pl.when(jnp.logical_not(inside))
                def _(i=i):
                    put(i * block, halo[...])

    for g, ((_, left, right), own) in enumerate(zip(groups, spec["groups"])):
        n = jnp.int32(0)
        for t in range(right.shape[0]):
            c = cls_ref[g, t]
            near = jnp.logical_or(c == 0, c >= 3)
            above = jnp.logical_and(c == 1, sec + shift < secs)
            below = jnp.logical_and(c == 2, sec >= shift)
            far = jnp.logical_or(above, below)
            near_at = jnp.where(c == 0, block, jnp.where(c == 3, 2 * block, 0))
            far_off = jnp.where(c == 1, far_at, below_at)
            chosen, at = (near, near_at) if not spec["far"] else (far, far_off)
            if spec["near"] and spec["far"]:
                chosen, at = jnp.logical_or(near, far), jnp.where(near, near_at, far_off)

            @pl.when(chosen)
            def _(n=n, t=t, at=at):
                order[n] = t
                offsets[n] = at

            n = n + chosen.astype(jnp.int32)

        first = core * half + lo if own else lo

        @pl.loop(0, lax.div(n + GROUP - 1, GROUP))
        def _(i, n=n, left=left, right=right, first=first):
            terms, real = [], []
            for j in range(GROUP):
                k = jnp.minimum(i * GROUP + j, n - 1)
                real.append(i * GROUP + j < n)
                terms.append(order[k])
                at = pl.ds(pl.multiple_of(offsets[k], block), rows)
                high, low = split(right[terms[j]])
                wide = jnp.concatenate([high, high, low], 0)
                high, low = split(jnp.dot(src[at, :], wide, preferred_element_type=F32))
                for s in range(count):
                    here = slice(s * block, (s + 1) * block)
                    tbuf[s, j * block : (j + 1) * block, :] = high[here]
                    tbuf[s, (GROUP + j) * block : (GROUP + j + 1) * block, :] = low[here]
            for s in range(count):
                blocks = [left[first + s, terms[0]]]
                for j in range(1, GROUP):
                    blocks.append(jnp.where(real[j], left[first + s, terms[j]], 0.0))
                high, low = split(jnp.concatenate(blocks, 1))
                acc[s * block : (s + 1) * block, :] += jnp.dot(
                    jnp.concatenate([high, high, low], 1),
                    jnp.concatenate([tbuf[s], tbuf[s, 0 : GROUP * block]], 0),
                    preferred_element_type=F32,
                )

    if sums is None:
        return
    cross = jnp.zeros((8, cols), F32)
    square = jnp.zeros((8, cols), F32)
    for s in range(count):
        sector = core * half + lo + s
        live = masked(sector_rows(wave, sector, block)[...], rows_ref[sector])
        fold = lambda v: jnp.sum(v.reshape(block // 8, 8, cols), axis=0)
        cross += fold(live * acc[s * block : (s + 1) * block, :])
        square += fold(live * live)
    fold = lambda v: sum(v[:, i : i + 128] for i in range(0, cols, 128))
    cross, square = fold(cross), fold(square)
    if sums_in is not None:
        cross, square = cross + sums_in[0:8, :], square + sums_in[8:16, :]
    sums[0:8, :] = cross
    sums[8:16, :] = square


def final_kernel(sides, rows_ref, sums, wave, *refs):
    totals, (applied, correction, buf, sem) = refs[:-4], refs[-4:]
    core, _, _ = place()
    block = wave.shape[0] // rows_ref.shape[0]
    half = rows_ref.shape[0] // 2
    chunks = len(totals) // 2
    rows = totals[0].shape[0]
    count = rows // block
    rayleigh = jnp.sum(sums[0:8, :]) / (jnp.sum(sums[8:16, :]) * (1.0 / sides))
    moves = []
    for i, total in enumerate(totals):
        c = core if i < chunks else 1 - core
        first = c * half + i % chunks * count
        for s in range(count):
            live = rows_ref[first + s]
            here = pl.ds(s * block, block)
            total_rows = masked(total[here, :], live)
            buf[0, i, here, :] = total_rows
            wave_rows = sector_rows(wave, first + s, block)[...]
            buf[1, i, here, :] = total_rows - rayleigh * masked(wave_rows, live)
        at = pl.ds(pl.multiple_of(first * block, block), rows)
        moves.append(pltpu.make_async_copy(buf.at[0, i], applied.at[at, :], sem.at[0, i]))
        moves.append(pltpu.make_async_copy(buf.at[1, i], correction.at[at, :], sem.at[1, i]))
        for move in moves[-2:]:
            move.start()
    for move in moves:
        move.wait()


def params(limit):
    return pltpu.CompilerParams(vmem_limit_bytes=limit * 2**20)


def cost(flops, moved):
    return pl.CostEstimate(flops=int(flops), bytes_accessed=int(moved), transcendentals=0)


def shape(*dims):
    return jax.ShapeDtypeStruct(dims, F32)


def swap(array, axis, bit):
    pairs = [(i, i ^ bit) for i in range(lax.axis_size(axis))]
    return lax.ppermute(array, axis, pairs)


def after(array, *others):
    return lax.optimization_barrier((array, *others))[0]


def local(wavefunction, left_blocks, right_blocks, block_rows, term_charge):
    sector_count = block_rows.shape[0]
    block = left_blocks.shape[2]
    terms = left_blocks.shape[1]
    cols = wavefunction.shape[1]
    secs, mpos, reps = (lax.axis_size(a) for a in ("sec", "mpo", "rep"))
    half = sector_count // 2
    part = half // 2
    shift = QD // sector_count
    merged = secs <= 2 * shift
    whole = wavefunction
    if reps > 1:
        whole = lax.all_gather(wavefunction, "rep", axis=1, tiled=True)
    wide = whole.shape[1]

    up = [(i, i - shift) for i in range(shift, secs)]
    down = [(i, i + shift) for i in range(secs - shift)]

    def far(array):
        if merged:
            return lax.ppermute(array, "sec", up + down)[None]
        return jnp.stack([lax.ppermute(array, "sec", p) for p in (up, down)])

    halo_pairs = []
    for m in range(mpos):
        for z in range(secs):
            to = z + 1 if m % 2 == 0 else z - 1
            if 0 <= to < secs:
                halo_pairs.append((z * mpos + m, to * mpos + m))

    mine_a, halo = pl.pallas_call(
        functools.partial(source_kernel, half),
        out_shape=(shape(block, wide), shape(block, wide)),
        in_specs=[SMEM, HBM],
        out_specs=(VMEM, VMEM),
        scratch_shapes=[pltpu.SemaphoreType.DMA((2,))],
        compiler_params=params(16),
        cost_estimate=cost(1, 1),
        name="first_sources",
    )(block_rows, whole)
    far_a = far(mine_a)
    halo = lax.ppermute(halo, ("sec", "mpo"), halo_pairs)
    right_pair = swap(right_blocks, "mpo", 1)
    mine_b, left_send = pl.pallas_call(
        functools.partial(pair_kernel, half),
        out_shape=(shape(block, wide), shape(half, terms, block, block)),
        in_specs=[SMEM, HBM, HBM],
        out_specs=(VMEM, VMEM),
        scratch_shapes=[pltpu.SemaphoreType.DMA((2,))],
        compiler_params=params(58),
        cost_estimate=cost(1, 1),
        name="pair_blocks",
    )(block_rows, after(whole, halo), left_blocks)
    left_pair = swap(left_send, "mpo", 1)
    cls_pair = swap(term_charge, "mpo", 1)
    far_b = far(mine_b)

    own = (term_charge, left_blocks, right_blocks)
    pair = (cls_pair, left_pair, right_pair)

    def run(name, groups, lo, count, halo=None, far=None, acc=None, acc_lo=0, sums_in=None, sums=False):
        spec = dict(
            groups=[g is own for g in groups], near=halo is not None, far=far is not None, half=half, lo=lo,
            count=count, secs=secs, shift=shift, acc=None if acc is None else acc_lo, sums=sums,
            sums_in=sums_in is not None,
        )
        args, specs = [block_rows, whole if halo is not None else wavefunction], [ANY, VMEM]
        for g in groups:
            args += g
            specs += [ANY, VMEM, VMEM]
        for extra in ((halo,) if halo is not None else ()) + (far or ()):
            args.append(extra)
            specs.append(VMEM)
        for extra in (acc, sums_in):
            if extra is not None:
                args.append(extra)
                specs.append(VMEM)
        rows = count * block
        src_rows = (rows + 2 * block if halo is not None else 0) + (rows * (1 if merged else 2) if far else 0)
        out = pl.pallas_call(
            functools.partial(terms_kernel, spec),
            out_shape=(shape(rows, cols), shape(16, 128)) if sums else (shape(rows, cols),),
            in_specs=specs,
            out_specs=(VMEM,) * (2 if sums else 1),
            scratch_shapes=[
                pltpu.VMEM((src_rows, 3 * wide), BF16),
                pltpu.VMEM((count, 2 * GROUP * block, cols), BF16),
                pltpu.SMEM((sector_count,), jnp.int32),
                pltpu.SMEM((len(groups), terms), jnp.int32),
                pltpu.SMEM((terms,), jnp.int32),
                pltpu.SMEM((terms,), jnp.int32),
                pltpu.SemaphoreType.DMA((1 + len(groups),)),
            ],
            compiler_params=params(32),
            cost_estimate=cost(1, 1),
            name=name,
        )(*args)
        return out if sums else out[0]

    acc = run("own_near", (own,), 0, half, halo=halo)
    other_a = swap(after(far_a, acc), "mpo", 2)
    acc = run("pair_near", (pair,), 0, half, halo=halo, acc=acc)
    other_b = swap(after(far_b, acc), "mpo", 2)
    part_a, sums = run("far", (own, pair), 0, part, far=(far_a, other_a), acc=acc, sums=True)
    recv_a = swap(part_a, "mpo", 2)
    part_b, sums = run(
        "far", (own, pair), part, part, far=(far_b, other_b), acc=acc, acc_lo=part, sums_in=sums, sums=True
    )
    recv_b = swap(part_b, "mpo", 2)

    if secs & (secs - 1) == 0 and secs <= 4:
        bit = 1
        while bit < secs:
            sums = sums + swap(sums, "sec", bit)
            bit *= 2
    else:
        sums = lax.psum(sums, "sec")
    if reps > 1:
        sums = lax.psum(sums, "rep")
    sums = sums + swap(sums, "mpo", 2)
    sums = sums + swap(sums, "mpo", 1)
    totals = [part_a + recv_a, part_b + after(recv_b, sums)]
    totals += [swap(total, "mpo", 1) for total in totals]

    out = shape(sector_count * block, cols)
    return pl.pallas_call(
        functools.partial(final_kernel, mpos // 2),
        out_shape=(out, out),
        in_specs=[SMEM] + [VMEM] * 6,
        out_specs=(ANY, ANY),
        scratch_shapes=[
            pltpu.VMEM((2, len(totals), part * block, cols), F32),
            pltpu.SemaphoreType.DMA((2, len(totals))),
        ],
        compiler_params=params(32),
        cost_estimate=cost(8 * sector_count * block * cols, 12 * sector_count * block * cols),
        name="residual",
    )(block_rows, sums, wavefunction, *totals)


def solution(mesh):
    in_specs = (
        P(("runs", "sec"), "rep"),
        P(("runs", "sec"), "mpo", None, None),
        P(("runs", "mpo"), None, "rep"),
        P(("runs", "sec")),
        P("mpo"),
    )
    out_specs = (P(("runs", "sec"), "rep"), P(("runs", "sec"), "rep"))
    return jax.shard_map(local, mesh=mesh, in_specs=in_specs, out_specs=out_specs, check_vma=False)
```

```python
import functools

import jax
import jax.numpy as jnp
from jax import lax
from jax.experimental import pallas as pl
from jax.experimental.pallas import tpu as pltpu
from jax.sharding import PartitionSpec as P

QD = 16
F32 = jnp.float32
BF16 = jnp.bfloat16
VMEM = pl.BlockSpec(memory_space=pltpu.VMEM)
SMEM = pl.BlockSpec(memory_space=pltpu.SMEM)
HBM = pl.BlockSpec(memory_space=pltpu.HBM)
ANY = pl.BlockSpec(memory_space=pl.ANY)


def split(x):
    high = x.astype(BF16)
    return high, (x - high.astype(F32)).astype(BF16)


def masked(rows, live):
    index = lax.broadcasted_iota(jnp.int32, rows.shape, 0)
    return jnp.where(index < live, rows, 0.0)


OWN_VMEM, PAIR_VMEM = 46, 32
GROUP = 2


def place():
    mpo = lax.axis_index("mpo")
    return lax.rem(mpo, 2), lax.rem(lax.div(mpo, 2), 2), lax.axis_index("sec")


def sector_rows(wave, sector, block):
    return wave.at[pl.ds(pl.multiple_of(sector * block, block), block), :]


def prepare_kernel(half, rows_hbm, wave, left, mine_a, mine_b, halo, left_send, rows_ref, sem):
    core, side, _ = place()
    block = halo.shape[0]
    count = rows_ref.shape[0]
    part = half // 2
    wanted = (
        (core * half + side, mine_a),
        ((1 - core) * (count - 1), halo),
        (core * half + part + side, mine_b),
    )
    moves = [pltpu.make_async_copy(rows_hbm, rows_ref, sem.at[0])]
    for i, (sector, ref) in enumerate(wanted):
        moves.append(pltpu.make_async_copy(sector_rows(wave, sector, block), ref, sem.at[i + 1]))
    moves.append(pltpu.make_async_copy(left.at[pl.ds((1 - core) * half, half)], left_send, sem.at[4]))
    for move in moves:
        move.start()
    moves[0].wait()
    for move, (sector, ref) in zip(moves[1:], wanted):
        move.wait()
        ref[...] = masked(ref[...], rows_ref[sector])
    moves[-1].wait()


def put(src, at, value):
    wide = value.shape[1]
    high, low = split(value)
    here = pl.ds(at, value.shape[0])
    src[here, 0:wide] = high
    src[here, wide : 2 * wide] = low
    src[here, 2 * wide : 3 * wide] = high


def pack(cls_ref, choose, order, offsets):
    n = jnp.int32(0)
    for t in range(cls_ref.shape[0]):
        chosen, at = choose(cls_ref[t])

        @pl.when(chosen)
        def _(n=n, t=t, at=at):
            order[n] = t
            offsets[n] = at

        n = n + chosen.astype(jnp.int32)
    return n


def add_terms(n, order, offsets, src, left, right, first, acc, tbuf, ready=None):
    rows = acc.shape[0]
    block = left.shape[-1]
    count = rows // block

    @pl.loop(0, lax.div(n + GROUP - 1, GROUP))
    def _(i):
        terms, real = [], []
        for j in range(GROUP):
            k = jnp.minimum(i * GROUP + j, n - 1)
            real.append(i * GROUP + j < n)
            terms.append(order[k])
            if ready is not None:

                @pl.when(real[j])
                def _(j=j):
                    ready(terms[j])

            at = pl.ds(pl.multiple_of(offsets[k], block), rows)
            high, low = split(right[terms[j]])
            wide = jnp.concatenate([high, high, low], 0)
            high, low = split(jnp.dot(src[at, :], wide, preferred_element_type=F32))
            for s in range(count):
                here = slice(s * block, (s + 1) * block)
                tbuf[s, j * block : (j + 1) * block, :] = high[here]
                tbuf[s, (GROUP + j) * block : (GROUP + j + 1) * block, :] = low[here]
        for s in range(count):
            blocks = [left[first + s, terms[0]]]
            for j in range(1, GROUP):
                blocks.append(jnp.where(real[j], left[first + s, terms[j]], 0.0))
            high, low = split(jnp.concatenate(blocks, 1))
            acc[s * block : (s + 1) * block, :] += jnp.dot(
                jnp.concatenate([high, high, low], 1),
                jnp.concatenate([tbuf[s], tbuf[s, 0 : GROUP * block]], 0),
                preferred_element_type=F32,
            )


def near_kernel(own, *refs):
    if own:
        cls, left_hbm, right_hbm, rows_hbm, whole, wave, halo, acc, left, right, src, live, *rest = refs
        rows_ref = rest.pop(0)
    else:
        cls, left_hbm, right_hbm, src, acc_in, acc, left, right, *rest = refs
    tbuf, cls_ref, order, offsets, sem = rest
    half, terms, block, _ = left.shape
    core, _, _ = place()

    fetch_cls = pltpu.make_async_copy(cls, cls_ref, sem.at[0, terms])
    fetch_cls.start()
    if own:
        fetch_rows = pltpu.make_async_copy(rows_hbm, rows_ref, sem.at[1, terms])
        fetch_rows.start()
    first = core * half if own else 0

    def fetch(t):
        return (
            pltpu.make_async_copy(left_hbm.at[pl.ds(first, half), t], left.at[:, t], sem.at[0, t]),
            pltpu.make_async_copy(right_hbm.at[t], right.at[t], sem.at[1, t]),
        )

    for t in range(terms):
        for move in fetch(t):
            move.start()

    if own:
        acc[...] = jnp.zeros_like(acc)
        fetch_rows.wait()
        count = rows_ref.shape[0]
        for s in range(count):
            here = pl.ds(s * block, block)
            live[here, :] = masked(wave[here, :], rows_ref[s])
        for i in range(half + 2):
            sector = core * half - 1 + i
            inside = jnp.logical_and(sector >= 0, sector < count)
            at = i * block
            if 0 < i < half + 1:
                put(src, at, masked(sector_rows(whole, sector, block)[...], rows_ref[sector]))
                continue

            @pl.when(inside)
            def _(sector=sector, at=at):
                put(src, at, masked(sector_rows(whole, sector, block)[...], rows_ref[sector]))

            @pl.when(jnp.logical_not(inside))
            def _(at=at):
                put(src, at, halo[...])
    else:
        acc[...] = acc_in[...]

    fetch_cls.wait()

    def near(c):
        at = jnp.where(c == 0, block, jnp.where(c == 3, 2 * block, 0))
        return jnp.logical_or(c == 0, c >= 3), at

    def wait(t):
        for move in fetch(t):
            move.wait()

    n = pack(cls_ref, near, order, offsets)
    add_terms(n, order, offsets, src, left, right, 0, acc, tbuf, ready=wait)
    for t in range(terms):

        @pl.when(jnp.logical_not(near(cls_ref[t])[0]))
        def _(t=t):
            wait(t)


def far_kernel(lo, shift, secs, chained, *refs):
    refs = list(refs)
    cls, cls_pair, rows_hbm, left, right, left_pair, right_pair, live, mine, other, acc_in = refs[:11]
    sums_in = refs.pop(11) if chained else None
    acc, sums, src, tbuf, rows_ref, cls_ref, order, offsets, sem = refs[11:]
    rows, cols = acc.shape
    half, terms, block, _ = left.shape
    count = rows // block
    core, side, sec = place()
    merged = mine.shape[0] == 1

    moves = [
        pltpu.make_async_copy(rows_hbm, rows_ref, sem.at[0]),
        pltpu.make_async_copy(cls, cls_ref.at[0], sem.at[1]),
        pltpu.make_async_copy(cls_pair, cls_ref.at[1], sem.at[2]),
    ]
    for move in moves:
        move.start()
    acc[...] = acc_in[pl.ds(lo * block, rows), :]
    for k in range(mine.shape[0]):
        for ref, x in ((mine, side), (other, 1 - side)):
            part = ref.shape[1]
            put(src, pl.multiple_of(k * rows + x * part, part), ref[k])
    for move in moves:
        move.wait()

    def far(c):
        above = jnp.logical_and(c == 1, sec + shift < secs)
        below = jnp.logical_and(c == 2, sec >= shift)
        return jnp.logical_or(above, below), jnp.where(c == 1, 0, 0 if merged else rows)

    for g, (l, r) in enumerate(((left, right), (left_pair, right_pair))):
        n = pack(cls_ref.at[g], far, order, offsets)
        add_terms(n, order, offsets, src, l, r, lo, acc, tbuf)

    cross = jnp.zeros((8, cols), F32)
    square = jnp.zeros((8, cols), F32)
    for s in range(count):
        sector = core * half + lo + s
        here = pl.ds(s * block, block)
        total = masked(acc[here, :], rows_ref[sector])
        acc[here, :] = total
        value = sector_rows(live, sector, block)[...]
        fold = lambda v: jnp.sum(v.reshape(block // 8, 8, cols), axis=0)
        cross += fold(value * total)
        square += fold(value * value)
    fold = lambda v: sum(v[:, i : i + 128] for i in range(0, cols, 128))
    cross, square = fold(cross), fold(square)
    if chained:
        cross, square = cross + sums_in[0:8, :], square + sums_in[8:16, :]
    sums[0:8, :] = cross
    sums[8:16, :] = square


def final_kernel(sides, block, sums, live, *refs):
    totals, (applied, correction, buf, sem) = refs[:-4], refs[-4:]
    core, _, _ = place()
    half = live.shape[0] // 2
    chunks = len(totals) // 2
    rows = totals[0].shape[0]
    places = []
    moves = []
    for i, total in enumerate(totals):
        c = core if i < chunks else 1 - core
        places.append(pl.ds(pl.multiple_of(c * half + i % chunks * rows, rows), rows))
        moves.append(pltpu.make_async_copy(total, applied.at[places[i], :], sem.at[0, i]))
        moves[-1].start()
    rayleigh = jnp.sum(sums[0:8, :]) / (jnp.sum(sums[8:16, :]) * (1.0 / sides))
    for i, total in enumerate(totals):
        buf[i] = total[...] - rayleigh * live[places[i], :]
        moves.append(pltpu.make_async_copy(buf.at[i], correction.at[places[i], :], sem.at[1, i]))
        moves[-1].start()
    for move in moves:
        move.wait()


def params(limit):
    return pltpu.CompilerParams(vmem_limit_bytes=limit * 2**20)


def cost(flops, moved):
    return pl.CostEstimate(flops=int(flops), bytes_accessed=int(moved), transcendentals=0)


def shape(*dims):
    return jax.ShapeDtypeStruct(dims, F32)


def swap(array, axis, bit):
    pairs = [(i, i ^ bit) for i in range(lax.axis_size(axis))]
    return lax.ppermute(array, axis, pairs)


def after(array, *others):
    return lax.optimization_barrier((array, *others))[0]


def local(wavefunction, left_blocks, right_blocks, block_rows, term_charge):
    sector_count = block_rows.shape[0]
    block = left_blocks.shape[2]
    terms = left_blocks.shape[1]
    cols = wavefunction.shape[1]
    secs, mpos, reps = (lax.axis_size(a) for a in ("sec", "mpo", "rep"))
    half = sector_count // 2
    part = half // 2
    shift = QD // sector_count
    merged = secs <= 2 * shift
    whole = wavefunction
    if reps > 1:
        whole = lax.all_gather(wavefunction, "rep", axis=1, tiled=True)
    wide = whole.shape[1]

    up = [(i, i - shift) for i in range(shift, secs)]
    down = [(i, i + shift) for i in range(secs - shift)]

    def far(array):
        if merged:
            return lax.ppermute(array, "sec", up + down)[None]
        return jnp.stack([lax.ppermute(array, "sec", p) for p in (up, down)])

    halo_pairs = []
    for m in range(mpos):
        for z in range(secs):
            to = z + 1 if m % 2 == 0 else z - 1
            if 0 <= to < secs:
                halo_pairs.append((z * mpos + m, to * mpos + m))

    rows = part * block
    blocks = shape(half, terms, block, block)
    mine_a, mine_b, halo, left_send = pl.pallas_call(
        functools.partial(prepare_kernel, half),
        out_shape=(shape(block, wide),) * 3 + (blocks,),
        in_specs=[ANY] * 3,
        out_specs=(VMEM,) * 4,
        scratch_shapes=[pltpu.SMEM((sector_count,), jnp.int32), pltpu.SemaphoreType.DMA((5,))],
        compiler_params=params(58),
        cost_estimate=cost(1, 1),
        name="prepare",
    )(block_rows, whole, left_blocks)
    far_a = far(mine_a)
    halo = lax.ppermute(halo, ("sec", "mpo"), halo_pairs)
    right_pair = swap(right_blocks, "mpo", 1)
    left_pair = swap(left_send, "mpo", 1)
    cls_pair = swap(term_charge, "mpo", 1)
    far_b = far(after(mine_b, halo))

    lists = [pltpu.SMEM((terms,), jnp.int32)] * 2

    def near(own, *args):
        outs = [shape(half * block, cols), blocks, shape(terms, wide, cols)]
        specs = [ANY, ANY, ANY] + ([ANY] + [VMEM] * 3 if own else [VMEM] * 2)
        if own:
            outs += [jax.ShapeDtypeStruct(((half + 2) * block, 3 * wide), BF16), shape(sector_count * block, cols)]
        return pl.pallas_call(
            functools.partial(near_kernel, own),
            out_shape=tuple(outs),
            in_specs=specs,
            out_specs=(VMEM,) * len(outs),
            scratch_shapes=([pltpu.SMEM((sector_count,), jnp.int32)] if own else [])
            + [pltpu.VMEM((half, 2 * GROUP * block, cols), BF16), pltpu.SMEM((terms,), jnp.int32)]
            + lists
            + [pltpu.SemaphoreType.DMA((2, terms + 1))],
            compiler_params=params(OWN_VMEM if own else PAIR_VMEM),
            cost_estimate=cost(1, 1),
            name="own_near" if own else "pair_near",
        )(*args)

    def add_far(lo, far, acc, sums):
        extra = () if sums is None else (sums,)
        return pl.pallas_call(
            functools.partial(far_kernel, lo, shift, secs, sums is not None),
            out_shape=(shape(rows, cols), shape(16, 128)),
            in_specs=[ANY] * 3 + [VMEM] * (8 + len(extra)),
            out_specs=(VMEM, VMEM),
            scratch_shapes=[
                pltpu.VMEM((far[0].shape[0] * rows, 3 * wide), BF16),
                pltpu.VMEM((part, 2 * GROUP * block, cols), BF16),
                pltpu.SMEM((sector_count,), jnp.int32),
                pltpu.SMEM((2, terms), jnp.int32),
                *lists,
                pltpu.SemaphoreType.DMA((3,)),
            ],
            compiler_params=params(32),
            cost_estimate=cost(1, 1),
            name="far",
        )(term_charge, cls_pair, block_rows, left, right, left_pair, right_pair, live, *far, acc, *extra)

    acc, left, right, src, live = near(
        True, term_charge, left_blocks, right_blocks, block_rows, whole, wavefunction, halo
    )
    other_a = swap(after(far_a, acc), "mpo", 2)
    acc, left_pair, right_pair = near(False, cls_pair, left_pair, right_pair, src, acc)
    other_b = swap(after(far_b, acc), "mpo", 2)
    part_a, sums = add_far(0, (far_a, other_a), acc, None)
    recv_a = swap(part_a, "mpo", 2)
    part_b, sums = add_far(part, (far_b, other_b), acc, sums)
    recv_b = swap(part_b, "mpo", 2)

    turned = [lax.ppermute(sums, "sec", [(i, (i + by) % secs) for i in range(secs)]) for by in range(1, min(secs, 4))]
    sums = sum(turned, sums) if secs <= 4 else lax.psum(sums, "sec")
    if reps > 1:
        sums = lax.psum(sums, "rep")
    sums = sums + swap(sums, "mpo", 2)
    sums = sums + swap(sums, "mpo", 1)
    totals = [part_a + recv_a, part_b + after(recv_b, sums)]
    totals += [swap(total, "mpo", 1) for total in totals]

    out = shape(sector_count * block, cols)
    return pl.pallas_call(
        functools.partial(final_kernel, mpos // 2, block),
        out_shape=(out, out),
        in_specs=[VMEM] * (2 + len(totals)),
        out_specs=(ANY, ANY),
        scratch_shapes=[
            pltpu.VMEM((len(totals), rows, cols), F32),
            pltpu.SemaphoreType.DMA((2, len(totals))),
        ],
        compiler_params=params(32),
        cost_estimate=cost(1, 1),
        name="residual",
    )(sums, live, *totals)


def solution(mesh):
    in_specs = (
        P(("runs", "sec"), "rep"),
        P(("runs", "sec"), "mpo", None, None),
        P(("runs", "mpo"), None, "rep"),
        P(("runs", "sec")),
        P("mpo"),
    )
    out_specs = (P(("runs", "sec"), "rep"), P(("runs", "sec"), "rep"))
    return jax.shard_map(local, mesh=mesh, in_specs=in_specs, out_specs=out_specs, check_vma=False)
```

```python
import functools

import jax
import jax.numpy as jnp
from jax import lax
from jax.experimental import pallas as pl
from jax.experimental.pallas import tpu as pltpu
from jax.sharding import PartitionSpec as P

QD = 16
F32 = jnp.float32
BF16 = jnp.bfloat16
VMEM = pl.BlockSpec(memory_space=pltpu.VMEM)
SMEM = pl.BlockSpec(memory_space=pltpu.SMEM)
HBM = pl.BlockSpec(memory_space=pltpu.HBM)
ANY = pl.BlockSpec(memory_space=pl.ANY)


def split(x):
    high = x.astype(BF16)
    return high, (x - high.astype(F32)).astype(BF16)


def masked(rows, live):
    index = lax.broadcasted_iota(jnp.int32, rows.shape, 0)
    return jnp.where(index < live, rows, 0.0)


PREPARE_VMEM, OWN_VMEM, PAIR_VMEM = 46, 46, 32
GROUP = 2


def place():
    mpo = lax.axis_index("mpo")
    return lax.rem(mpo, 2), lax.rem(lax.div(mpo, 2), 2), lax.axis_index("sec")


def sector_rows(wave, sector, block):
    return wave.at[pl.ds(pl.multiple_of(sector * block, block), block), :]


def prepare_kernel(half, rows_hbm, whole, wave, left, mine_a, mine_b, halo, left_send, src, live, *rest):
    rows_ref, sem = rest
    core, side, _ = place()
    block = halo.shape[0]
    rows = pltpu.make_async_copy(rows_hbm, rows_ref, sem.at[0])
    rows.start()
    send = pltpu.make_async_copy(left.at[pl.ds((1 - core) * half, half)], left_send, sem.at[1])
    send.start()
    src[pl.ds(pl.multiple_of(core * (half + 1) * block, block), block), :] = jnp.zeros((block, src.shape[1]), BF16)
    rows.wait()

    def source(sector):
        return masked(sector_rows(whole, sector, block)[...], rows_ref[sector])

    mine_a[...] = source(core * half + side)
    mine_b[...] = source(core * half + half // 2 + side)
    halo[...] = source((1 - core) * (2 * half - 1))
    for s in range(2 * half):
        here = pl.ds(s * block, block)
        live[here, :] = masked(wave[here, :], rows_ref[s])
    for i in range(half + 1):
        put(src, pl.multiple_of((i + 1 - core) * block, block), source(core * (half - 1) + i))
    send.wait()


def put(src, at, value):
    wide = value.shape[1]
    high, low = split(value)
    here = pl.ds(at, value.shape[0])
    src[here, 0:wide] = high
    src[here, wide : 2 * wide] = low
    src[here, 2 * wide : 3 * wide] = high


def pack(cls_ref, choose, order, offsets):
    n = jnp.int32(0)
    for t in range(cls_ref.shape[0]):
        chosen, at = choose(cls_ref[t])

        @pl.when(chosen)
        def _(n=n, t=t, at=at):
            order[n] = t
            offsets[n] = at

        n = n + chosen.astype(jnp.int32)
    return n


def add_terms(n, order, offsets, src, left, right, first, acc, tbuf, ready=None):
    rows = acc.shape[0]
    block = left.shape[-1]
    count = rows // block

    @pl.loop(0, lax.div(n + GROUP - 1, GROUP))
    def _(i):
        terms, real = [], []
        for j in range(GROUP):
            k = jnp.minimum(i * GROUP + j, n - 1)
            real.append(i * GROUP + j < n)
            terms.append(order[k])
            if ready is not None:

                @pl.when(real[j])
                def _(j=j):
                    ready(terms[j])

            at = pl.ds(pl.multiple_of(offsets[k], block), rows)
            high, low = split(right[terms[j]])
            wide = jnp.concatenate([high, high, low], 0)
            high, low = split(jnp.dot(src[at, :], wide, preferred_element_type=F32))
            for s in range(count):
                here = slice(s * block, (s + 1) * block)
                tbuf[s, j * block : (j + 1) * block, :] = high[here]
                tbuf[s, (GROUP + j) * block : (GROUP + j + 1) * block, :] = low[here]
        for s in range(count):
            blocks = [left[first + s, terms[0]]]
            for j in range(1, GROUP):
                blocks.append(jnp.where(real[j], left[first + s, terms[j]], 0.0))
            high, low = split(jnp.concatenate(blocks, 1))
            acc[s * block : (s + 1) * block, :] += jnp.dot(
                jnp.concatenate([high, high, low], 1),
                jnp.concatenate([tbuf[s], tbuf[s, 0 : GROUP * block]], 0),
                preferred_element_type=F32,
            )


def near_kernel(own, *refs):
    if own:
        cls, left_hbm, right_hbm, src, acc, left, right, *rest = refs
    else:
        cls, left_hbm, right_hbm, cls_own, left_own, right_own, halo, src_in, acc_in, acc, left, right, *rest = refs
        src, *rest = rest
    tbuf, cls_ref, order, offsets, sem = rest
    half, terms, block, _ = left.shape
    core, _, _ = place()

    fetch_cls = [pltpu.make_async_copy(cls, cls_ref.at[0], sem.at[0, terms])]
    if not own:
        fetch_cls.append(pltpu.make_async_copy(cls_own, cls_ref.at[1], sem.at[1, terms]))
    for move in fetch_cls:
        move.start()
    first = core * half if own else 0

    def fetch(t):
        return (
            pltpu.make_async_copy(left_hbm.at[pl.ds(first, half), t], left.at[:, t], sem.at[0, t]),
            pltpu.make_async_copy(right_hbm.at[t], right.at[t], sem.at[1, t]),
        )

    for t in range(terms):
        for move in fetch(t):
            move.start()

    halo_at = pl.multiple_of(core * (half + 1) * block, block)
    if own:
        acc[...] = jnp.zeros_like(acc)
    else:
        acc[...] = acc_in[...]
        src[...] = src_in[...]
        put(src, halo_at, halo[...])
    for move in fetch_cls:
        move.wait()

    def near(c):
        at = jnp.where(c == 0, block, jnp.where(c == 3, 2 * block, 0))
        return jnp.logical_or(c == 0, c >= 3), at

    def wait(t):
        for move in fetch(t):
            move.wait()

    if not own:
        edge = core * (half - 1)
        n = pack(cls_ref.at[1], lambda c: (c == 4 - core, halo_at), order, offsets)
        part = acc.at[pl.ds(pl.multiple_of(edge * block, block), block), :]
        add_terms(n, order, offsets, src, left_own, right_own, edge, part, tbuf)
    n = pack(cls_ref.at[0], near, order, offsets)
    add_terms(n, order, offsets, src, left, right, 0, acc, tbuf, ready=wait)
    for t in range(terms):

        @pl.when(jnp.logical_not(near(cls_ref[0, t])[0]))
        def _(t=t):
            wait(t)


def far_kernel(lo, shift, secs, chained, *refs):
    refs = list(refs)
    cls, cls_pair, rows_hbm, left, right, left_pair, right_pair, live, mine, other, acc_in = refs[:11]
    sums_in = refs.pop(11) if chained else None
    acc, sums, src, tbuf, rows_ref, cls_ref, order, offsets, sem = refs[11:]
    rows, cols = acc.shape
    half, terms, block, _ = left.shape
    count = rows // block
    core, side, sec = place()
    merged = mine.shape[0] == 1

    moves = [
        pltpu.make_async_copy(rows_hbm, rows_ref, sem.at[0]),
        pltpu.make_async_copy(cls, cls_ref.at[0], sem.at[1]),
        pltpu.make_async_copy(cls_pair, cls_ref.at[1], sem.at[2]),
    ]
    for move in moves:
        move.start()
    acc[...] = acc_in[pl.ds(lo * block, rows), :]
    for k in range(mine.shape[0]):
        for ref, x in ((mine, side), (other, 1 - side)):
            part = ref.shape[1]
            put(src, pl.multiple_of(k * rows + x * part, part), ref[k])
    for move in moves:
        move.wait()

    def far(c):
        above = jnp.logical_and(c == 1, sec + shift < secs)
        below = jnp.logical_and(c == 2, sec >= shift)
        return jnp.logical_or(above, below), jnp.where(c == 1, 0, 0 if merged else rows)

    for g, (l, r) in enumerate(((left, right), (left_pair, right_pair))):
        n = pack(cls_ref.at[g], far, order, offsets)
        add_terms(n, order, offsets, src, l, r, lo, acc, tbuf)

    cross = jnp.zeros((8, cols), F32)
    square = jnp.zeros((8, cols), F32)
    for s in range(count):
        sector = core * half + lo + s
        here = pl.ds(s * block, block)
        total = masked(acc[here, :], rows_ref[sector])
        acc[here, :] = total
        value = sector_rows(live, sector, block)[...]
        fold = lambda v: jnp.sum(v.reshape(block // 8, 8, cols), axis=0)
        cross += fold(value * total)
        square += fold(value * value)
    fold = lambda v: sum(v[:, i : i + 128] for i in range(0, cols, 128))
    cross, square = fold(cross), fold(square)
    if chained:
        cross, square = cross + sums_in[0:8, :], square + sums_in[8:16, :]
    sums[0:8, :] = cross
    sums[8:16, :] = square


def final_kernel(sides, block, sums, live, *refs):
    totals, (applied, correction, buf, sem) = refs[:-4], refs[-4:]
    core, _, _ = place()
    half = live.shape[0] // 2
    chunks = len(totals) // 2
    rows = totals[0].shape[0]
    places = []
    moves = []
    for i, total in enumerate(totals):
        c = core if i < chunks else 1 - core
        places.append(pl.ds(pl.multiple_of(c * half + i % chunks * rows, rows), rows))
        moves.append(pltpu.make_async_copy(total, applied.at[places[i], :], sem.at[0, i]))
        moves[-1].start()
    rayleigh = jnp.sum(sums[0:8, :]) / (jnp.sum(sums[8:16, :]) * (1.0 / sides))
    for i, total in enumerate(totals):
        buf[i] = total[...] - rayleigh * live[places[i], :]
        moves.append(pltpu.make_async_copy(buf.at[i], correction.at[places[i], :], sem.at[1, i]))
        moves[-1].start()
    for move in moves:
        move.wait()


def params(limit):
    return pltpu.CompilerParams(vmem_limit_bytes=limit * 2**20)


def cost(flops, moved):
    return pl.CostEstimate(flops=int(flops), bytes_accessed=int(moved), transcendentals=0)


def shape(*dims):
    return jax.ShapeDtypeStruct(dims, F32)


def swap(array, axis, bit):
    pairs = [(i, i ^ bit) for i in range(lax.axis_size(axis))]
    return lax.ppermute(array, axis, pairs)


def everyone(array, axis):
    return (array + swap(array, axis, 1)) + (swap(array, axis, 2) + swap(array, axis, 3))


def after(array, *others):
    return lax.optimization_barrier((array, *others))[0]


def local(wavefunction, left_blocks, right_blocks, block_rows, term_charge):
    sector_count = block_rows.shape[0]
    block = left_blocks.shape[2]
    terms = left_blocks.shape[1]
    cols = wavefunction.shape[1]
    secs, mpos, reps = (lax.axis_size(a) for a in ("sec", "mpo", "rep"))
    half = sector_count // 2
    part = half // 2
    shift = QD // sector_count
    merged = secs <= 2 * shift
    whole = wavefunction
    if reps > 1:
        whole = lax.all_gather(wavefunction, "rep", axis=1, tiled=True)
    wide = whole.shape[1]

    up = [(i, i - shift) for i in range(shift, secs)]
    down = [(i, i + shift) for i in range(secs - shift)]

    def far(array):
        if merged:
            return lax.ppermute(array, "sec", up + down)[None]
        return jnp.stack([lax.ppermute(array, "sec", p) for p in (up, down)])

    halo_pairs = []
    for m in range(mpos):
        for z in range(secs):
            to = z + 1 if m % 2 == 0 else z - 1
            if 0 <= to < secs:
                halo_pairs.append((z * mpos + m, to * mpos + m))

    rows = part * block
    blocks = shape(half, terms, block, block)
    source_shape = ((half + 2) * block, 3 * wide)
    mine_a, mine_b, halo, left_send, src, live = pl.pallas_call(
        functools.partial(prepare_kernel, half),
        out_shape=(shape(block, wide),) * 3
        + (blocks, jax.ShapeDtypeStruct(source_shape, BF16), shape(sector_count * block, cols)),
        in_specs=[ANY, VMEM, VMEM, ANY],
        out_specs=(VMEM,) * 6,
        scratch_shapes=[pltpu.SMEM((sector_count,), jnp.int32), pltpu.SemaphoreType.DMA((2,))],
        compiler_params=params(PREPARE_VMEM),
        cost_estimate=cost(1, 1),
        name="prepare",
    )(block_rows, whole, wavefunction, left_blocks)
    far_a = far(mine_a)
    halo = lax.ppermute(halo, ("sec", "mpo"), halo_pairs)
    right_pair = swap(right_blocks, "mpo", 1)
    cls_pair = swap(term_charge, "mpo", 1)
    left_pair = swap(left_send, "mpo", 1)
    far_b = far(after(mine_b, right_pair, cls_pair))

    lists = [pltpu.SMEM((terms,), jnp.int32)] * 2

    def near(own, *args):
        outs = [shape(half * block, cols), blocks, shape(terms, wide, cols)]
        return pl.pallas_call(
            functools.partial(near_kernel, own),
            out_shape=tuple(outs),
            in_specs=[ANY] * 3 + ([VMEM] if own else [ANY] + [VMEM] * 5),
            out_specs=(VMEM,) * len(outs),
            scratch_shapes=([] if own else [pltpu.VMEM(source_shape, BF16)])
            + [pltpu.VMEM((half, 2 * GROUP * block, cols), BF16), pltpu.SMEM((2, terms), jnp.int32)]
            + lists
            + [pltpu.SemaphoreType.DMA((2, terms + 1))],
            compiler_params=params(OWN_VMEM if own else PAIR_VMEM),
            cost_estimate=cost(1, 1),
            name="own_near" if own else "pair_near",
        )(*args)

    def add_far(lo, far, acc, sums):
        extra = () if sums is None else (sums,)
        return pl.pallas_call(
            functools.partial(far_kernel, lo, shift, secs, sums is not None),
            out_shape=(shape(rows, cols), shape(16, 128)),
            in_specs=[ANY] * 3 + [VMEM] * (8 + len(extra)),
            out_specs=(VMEM, VMEM),
            scratch_shapes=[
                pltpu.VMEM((far[0].shape[0] * rows, 3 * wide), BF16),
                pltpu.VMEM((part, 2 * GROUP * block, cols), BF16),
                pltpu.SMEM((sector_count,), jnp.int32),
                pltpu.SMEM((2, terms), jnp.int32),
                *lists,
                pltpu.SemaphoreType.DMA((3,)),
            ],
            compiler_params=params(32),
            cost_estimate=cost(1, 1),
            name="far",
        )(term_charge, cls_pair, block_rows, left, right, left_pair, right_pair, live, *far, acc, *extra)

    acc, left, right = near(True, term_charge, left_blocks, right_blocks, src)
    other_a = swap(after(far_a, acc), "mpo", 2)
    acc, left_pair, right_pair = near(
        False, cls_pair, left_pair, right_pair, term_charge, left, right, halo, src, acc
    )
    other_b = swap(after(far_b, acc), "mpo", 2)
    part_a, sums = add_far(0, (far_a, other_a), acc, None)
    recv_a = swap(part_a, "mpo", 2)
    part_b, sums = add_far(part, (far_b, other_b), acc, sums)
    recv_b = swap(part_b, "mpo", 2)

    if secs == 4:
        sums = everyone(sums, "sec")
    else:
        sums = lax.psum(sums, "sec")
    if reps > 1:
        sums = lax.psum(sums, "rep")
    sums = everyone(sums, "mpo")
    totals = [part_a + recv_a, part_b + after(recv_b, sums)]
    totals += [swap(total, "mpo", 1) for total in totals]

    out = shape(sector_count * block, cols)
    return pl.pallas_call(
        functools.partial(final_kernel, mpos // 2, block),
        out_shape=(out, out),
        in_specs=[VMEM] * (2 + len(totals)),
        out_specs=(ANY, ANY),
        scratch_shapes=[
            pltpu.VMEM((len(totals), rows, cols), F32),
            pltpu.SemaphoreType.DMA((2, len(totals))),
        ],
        compiler_params=params(32),
        cost_estimate=cost(1, 1),
        name="residual",
    )(sums, live, *totals)


def solution(mesh):
    in_specs = (
        P(("runs", "sec"), "rep"),
        P(("runs", "sec"), "mpo", None, None),
        P(("runs", "mpo"), None, "rep"),
        P(("runs", "sec")),
        P("mpo"),
    )
    out_specs = (P(("runs", "sec"), "rep"), P(("runs", "sec"), "rep"))
    return jax.shard_map(local, mesh=mesh, in_specs=in_specs, out_specs=out_specs, check_vma=False)
```

```python
import functools

import jax
import jax.numpy as jnp
from jax import lax
from jax.experimental import pallas as pl
from jax.experimental.pallas import tpu as pltpu
from jax.sharding import PartitionSpec as P

QD = 16
F32 = jnp.float32
BF16 = jnp.bfloat16
VMEM = pl.BlockSpec(memory_space=pltpu.VMEM)
SMEM = pl.BlockSpec(memory_space=pltpu.SMEM)
HBM = pl.BlockSpec(memory_space=pltpu.HBM)
ANY = pl.BlockSpec(memory_space=pl.ANY)


def split(x):
    high = x.astype(BF16)
    return high, (x - high.astype(F32)).astype(BF16)


def masked(rows, live):
    index = lax.broadcasted_iota(jnp.int32, rows.shape, 0)
    return jnp.where(index < live, rows, 0.0)


PREPARE_VMEM, NEAR_VMEM = 46, 32
GROUP = 2


def place():
    mpo = lax.axis_index("mpo")
    return lax.rem(mpo, 2), lax.rem(lax.div(mpo, 2), 2), lax.axis_index("sec")


def sector_rows(wave, sector, block):
    return wave.at[pl.ds(pl.multiple_of(sector * block, block), block), :]


def prepare_kernel(half, rows_hbm, whole, wave, left, mine_a, mine_b, halo, left_send, src, live, *rest):
    rows_ref, sem = rest
    core, side, _ = place()
    block = halo.shape[0]
    rows = pltpu.make_async_copy(rows_hbm, rows_ref, sem.at[0])
    rows.start()
    send = pltpu.make_async_copy(left.at[pl.ds((1 - core) * half, half)], left_send, sem.at[1])
    send.start()
    src[pl.ds(pl.multiple_of(core * (half + 1) * block, block), block), :] = jnp.zeros((block, src.shape[1]), BF16)
    rows.wait()

    def source(sector):
        return masked(sector_rows(whole, sector, block)[...], rows_ref[sector])

    mine_a[...] = source(core * half + side)
    mine_b[...] = source(core * half + half // 2 + side)
    halo[...] = source((1 - core) * (2 * half - 1))
    for s in range(2 * half):
        here = pl.ds(s * block, block)
        live[here, :] = masked(wave[here, :], rows_ref[s])
    for i in range(half + 1):
        put(src, pl.multiple_of((i + 1 - core) * block, block), source(core * (half - 1) + i))
    send.wait()


def put(src, at, value):
    wide = value.shape[1]
    high, low = split(value)
    here = pl.ds(at, value.shape[0])
    src[here, 0:wide] = high
    src[here, wide : 2 * wide] = low
    src[here, 2 * wide : 3 * wide] = high


def pack(cls_ref, choose, order, offsets):
    n = jnp.int32(0)
    for t in range(cls_ref.shape[0]):
        chosen, at = choose(cls_ref[t])

        @pl.when(chosen)
        def _(n=n, t=t, at=at):
            order[n] = t
            offsets[n] = at

        n = n + chosen.astype(jnp.int32)
    return n


def add_terms(n, order, offsets, src, left, right, first, acc, tbuf):
    rows = acc.shape[0]
    block = left.shape[-1]
    count = rows // block

    @pl.loop(0, lax.div(n + GROUP - 1, GROUP))
    def _(i):
        terms, real = [], []
        for j in range(GROUP):
            k = jnp.minimum(i * GROUP + j, n - 1)
            real.append(i * GROUP + j < n)
            terms.append(order[k])
            at = pl.ds(pl.multiple_of(offsets[k], block), rows)
            high, low = split(right[terms[j]])
            wide = jnp.concatenate([high, high, low], 0)
            high, low = split(jnp.dot(src[at, :], wide, preferred_element_type=F32))
            for s in range(count):
                here = slice(s * block, (s + 1) * block)
                tbuf[s, j * block : (j + 1) * block, :] = high[here]
                tbuf[s, (GROUP + j) * block : (GROUP + j + 1) * block, :] = low[here]
        for s in range(count):
            blocks = [left[first + s, terms[0]]]
            for j in range(1, GROUP):
                blocks.append(jnp.where(real[j], left[first + s, terms[j]], 0.0))
            high, low = split(jnp.concatenate(blocks, 1))
            acc[s * block : (s + 1) * block, :] += jnp.dot(
                jnp.concatenate([high, high, low], 1),
                jnp.concatenate([tbuf[s], tbuf[s, 0 : GROUP * block]], 0),
                preferred_element_type=F32,
            )


def near_kernel(own, *refs):
    if own:
        cls, left, right, src, acc, *rest = refs
    else:
        cls, left, right, cls_own, left_own, right_own, halo, src_in, acc_in, acc, src, *rest = refs
    tbuf, cls_ref, order, offsets, sem = rest
    block = left.shape[-1]
    half = acc.shape[0] // block
    core, _, _ = place()

    fetch = [pltpu.make_async_copy(cls, cls_ref.at[0], sem.at[0])]
    if not own:
        fetch.append(pltpu.make_async_copy(cls_own, cls_ref.at[1], sem.at[1]))
    for move in fetch:
        move.start()
    halo_at = pl.multiple_of(core * (half + 1) * block, block)
    if own:
        acc[...] = jnp.zeros_like(acc)
    else:
        acc[...] = acc_in[...]
        src[...] = src_in[...]
        put(src, halo_at, halo[...])
    for move in fetch:
        move.wait()

    def near(c):
        at = jnp.where(c == 0, block, jnp.where(c == 3, 2 * block, 0))
        return jnp.logical_or(c == 0, c >= 3), at

    if not own:
        edge = core * (half - 1)
        n = pack(cls_ref.at[1], lambda c: (c == 4 - core, halo_at), order, offsets)
        part = acc.at[pl.ds(pl.multiple_of(edge * block, block), block), :]
        add_terms(n, order, offsets, src, left_own, right_own, core * half + edge, part, tbuf)
    n = pack(cls_ref.at[0], near, order, offsets)
    add_terms(n, order, offsets, src, left, right, core * half if own else 0, acc, tbuf)


def far_kernel(lo, shift, secs, chained, *refs):
    refs = list(refs)
    cls, cls_pair, rows_hbm, left, right, left_pair, right_pair, live, mine, other, acc_in = refs[:11]
    sums_in = refs.pop(11) if chained else None
    acc, sums, src, tbuf, rows_ref, cls_ref, order, offsets, sem = refs[11:]
    rows, cols = acc.shape
    half, _, block, _ = left_pair.shape
    count = rows // block
    core, side, sec = place()
    merged = mine.shape[0] == 1

    moves = [
        pltpu.make_async_copy(rows_hbm, rows_ref, sem.at[0]),
        pltpu.make_async_copy(cls, cls_ref.at[0], sem.at[1]),
        pltpu.make_async_copy(cls_pair, cls_ref.at[1], sem.at[2]),
    ]
    for move in moves:
        move.start()
    acc[...] = acc_in[pl.ds(lo * block, rows), :]
    for k in range(mine.shape[0]):
        for ref, x in ((mine, side), (other, 1 - side)):
            part = ref.shape[1]
            put(src, pl.multiple_of(k * rows + x * part, part), ref[k])
    for move in moves:
        move.wait()

    def far(c):
        above = jnp.logical_and(c == 1, sec + shift < secs)
        below = jnp.logical_and(c == 2, sec >= shift)
        return jnp.logical_or(above, below), jnp.where(c == 1, 0, 0 if merged else rows)

    for g, (l, r, first) in enumerate(((left, right, core * half + lo), (left_pair, right_pair, lo))):
        n = pack(cls_ref.at[g], far, order, offsets)
        add_terms(n, order, offsets, src, l, r, first, acc, tbuf)

    cross = jnp.zeros((8, cols), F32)
    square = jnp.zeros((8, cols), F32)
    for s in range(count):
        sector = core * half + lo + s
        here = pl.ds(s * block, block)
        total = masked(acc[here, :], rows_ref[sector])
        acc[here, :] = total
        value = sector_rows(live, sector, block)[...]
        fold = lambda v: jnp.sum(v.reshape(block // 8, 8, cols), axis=0)
        cross += fold(value * total)
        square += fold(value * value)
    fold = lambda v: sum(v[:, i : i + 128] for i in range(0, cols, 128))
    cross, square = fold(cross), fold(square)
    if chained:
        cross, square = cross + sums_in[0:8, :], square + sums_in[8:16, :]
    sums[0:8, :] = cross
    sums[8:16, :] = square


def final_kernel(sides, block, sums, live, *refs):
    totals, (applied, correction, buf, sem) = refs[:-4], refs[-4:]
    core, _, _ = place()
    half = live.shape[0] // 2
    chunks = len(totals) // 2
    rows = totals[0].shape[0]
    places = []
    moves = []
    for i, total in enumerate(totals):
        c = core if i < chunks else 1 - core
        places.append(pl.ds(pl.multiple_of(c * half + i % chunks * rows, rows), rows))
        moves.append(pltpu.make_async_copy(total, applied.at[places[i], :], sem.at[0, i]))
        moves[-1].start()
    rayleigh = jnp.sum(sums[0:8, :]) / (jnp.sum(sums[8:16, :]) * (1.0 / sides))
    for i, total in enumerate(totals):
        buf[i] = total[...] - rayleigh * live[places[i], :]
        moves.append(pltpu.make_async_copy(buf.at[i], correction.at[places[i], :], sem.at[1, i]))
        moves[-1].start()
    for move in moves:
        move.wait()


def params(limit):
    return pltpu.CompilerParams(vmem_limit_bytes=limit * 2**20)


def cost(flops, moved):
    return pl.CostEstimate(flops=int(flops), bytes_accessed=int(moved), transcendentals=0)


def shape(*dims):
    return jax.ShapeDtypeStruct(dims, F32)


def swap(array, axis, bit):
    pairs = [(i, i ^ bit) for i in range(lax.axis_size(axis))]
    return lax.ppermute(array, axis, pairs)


def everyone(array, axis):
    return (array + swap(array, axis, 1)) + (swap(array, axis, 2) + swap(array, axis, 3))


def after(array, *others):
    return lax.optimization_barrier((array, *others))[0]


def local(wavefunction, left_blocks, right_blocks, block_rows, term_charge):
    sector_count = block_rows.shape[0]
    block = left_blocks.shape[2]
    terms = left_blocks.shape[1]
    cols = wavefunction.shape[1]
    secs, mpos, reps = (lax.axis_size(a) for a in ("sec", "mpo", "rep"))
    half = sector_count // 2
    part = half // 2
    shift = QD // sector_count
    merged = secs <= 2 * shift
    whole = wavefunction
    if reps > 1:
        whole = lax.all_gather(wavefunction, "rep", axis=1, tiled=True)
    wide = whole.shape[1]

    up = [(i, i - shift) for i in range(shift, secs)]
    down = [(i, i + shift) for i in range(secs - shift)]

    def far(array):
        if merged:
            return lax.ppermute(array, "sec", up + down)[None]
        return jnp.stack([lax.ppermute(array, "sec", p) for p in (up, down)])

    halo_pairs = []
    for m in range(mpos):
        for z in range(secs):
            to = z + 1 if m % 2 == 0 else z - 1
            if 0 <= to < secs:
                halo_pairs.append((z * mpos + m, to * mpos + m))

    rows = part * block
    blocks = shape(half, terms, block, block)
    source_shape = ((half + 2) * block, 3 * wide)
    mine_a, mine_b, halo, left_send, src, live = pl.pallas_call(
        functools.partial(prepare_kernel, half),
        out_shape=(shape(block, wide),) * 3
        + (blocks, jax.ShapeDtypeStruct(source_shape, BF16), shape(sector_count * block, cols)),
        in_specs=[ANY, VMEM, VMEM, ANY],
        out_specs=(VMEM,) * 6,
        scratch_shapes=[pltpu.SMEM((sector_count,), jnp.int32), pltpu.SemaphoreType.DMA((2,))],
        compiler_params=params(PREPARE_VMEM),
        cost_estimate=cost(1, 1),
        name="prepare",
    )(block_rows, whole, wavefunction, left_blocks)
    far_a = far(mine_a)
    halo = lax.ppermute(halo, ("sec", "mpo"), halo_pairs)
    right_pair = swap(right_blocks, "mpo", 1)
    cls_pair = swap(term_charge, "mpo", 1)
    left_pair = swap(left_send, "mpo", 1)
    far_b = far(after(mine_b, right_pair, cls_pair))

    lists = [pltpu.SMEM((terms,), jnp.int32)] * 2

    def near(own, *args):
        return pl.pallas_call(
            functools.partial(near_kernel, own),
            out_shape=shape(half * block, cols),
            in_specs=[ANY] + [VMEM] * 3 if own else [ANY, VMEM, VMEM] * 2 + [VMEM] * 3,
            out_specs=VMEM,
            scratch_shapes=([] if own else [pltpu.VMEM(source_shape, BF16)])
            + [pltpu.VMEM((half, 2 * GROUP * block, cols), BF16), pltpu.SMEM((2, terms), jnp.int32)]
            + lists
            + [pltpu.SemaphoreType.DMA((2,))],
            compiler_params=params(NEAR_VMEM),
            cost_estimate=cost(1, 1),
            name="own_near" if own else "pair_near",
        )(*args)

    def add_far(lo, far, acc, sums):
        extra = () if sums is None else (sums,)
        return pl.pallas_call(
            functools.partial(far_kernel, lo, shift, secs, sums is not None),
            out_shape=(shape(rows, cols), shape(16, 128)),
            in_specs=[ANY] * 3 + [VMEM] * (8 + len(extra)),
            out_specs=(VMEM, VMEM),
            scratch_shapes=[
                pltpu.VMEM((far[0].shape[0] * rows, 3 * wide), BF16),
                pltpu.VMEM((part, 2 * GROUP * block, cols), BF16),
                pltpu.SMEM((sector_count,), jnp.int32),
                pltpu.SMEM((2, terms), jnp.int32),
                *lists,
                pltpu.SemaphoreType.DMA((3,)),
            ],
            compiler_params=params(32),
            cost_estimate=cost(1, 1),
            name="far",
        )(term_charge, cls_pair, block_rows, left_blocks, right_blocks, left_pair, right_pair, live, *far, acc, *extra)

    acc = near(True, term_charge, left_blocks, right_blocks, src)
    other_a = swap(after(far_a, acc), "mpo", 2)
    acc = near(False, cls_pair, left_pair, right_pair, term_charge, left_blocks, right_blocks, halo, src, acc)
    other_b = swap(after(far_b, acc), "mpo", 2)
    part_a, sums = add_far(0, (far_a, other_a), acc, None)
    recv_a = swap(part_a, "mpo", 2)
    part_b, sums = add_far(part, (far_b, other_b), acc, sums)
    recv_b = swap(part_b, "mpo", 2)

    if secs == 4:
        sums = everyone(sums, "sec")
    else:
        sums = lax.psum(sums, "sec")
    if reps > 1:
        sums = lax.psum(sums, "rep")
    sums = everyone(sums, "mpo")
    totals = [part_a + recv_a, part_b + after(recv_b, sums)]
    totals += [swap(total, "mpo", 1) for total in totals]

    out = shape(sector_count * block, cols)
    return pl.pallas_call(
        functools.partial(final_kernel, mpos // 2, block),
        out_shape=(out, out),
        in_specs=[VMEM] * (2 + len(totals)),
        out_specs=(ANY, ANY),
        scratch_shapes=[
            pltpu.VMEM((len(totals), rows, cols), F32),
            pltpu.SemaphoreType.DMA((2, len(totals))),
        ],
        compiler_params=params(32),
        cost_estimate=cost(1, 1),
        name="residual",
    )(sums, live, *totals)


def solution(mesh):
    in_specs = (
        P(("runs", "sec"), "rep"),
        P(("runs", "sec"), "mpo", None, None),
        P(("runs", "mpo"), None, "rep"),
        P(("runs", "sec")),
        P("mpo"),
    )
    out_specs = (P(("runs", "sec"), "rep"), P(("runs", "sec"), "rep"))
    return jax.shard_map(local, mesh=mesh, in_specs=in_specs, out_specs=out_specs, check_vma=False)
```

```python
import functools

import jax
import jax.numpy as jnp
from jax import lax
from jax.experimental import pallas as pl
from jax.experimental.pallas import tpu as pltpu
from jax.sharding import PartitionSpec as P

QD = 16
F32 = jnp.float32
BF16 = jnp.bfloat16
VMEM = pl.BlockSpec(memory_space=pltpu.VMEM)
SMEM = pl.BlockSpec(memory_space=pltpu.SMEM)
HBM = pl.BlockSpec(memory_space=pltpu.HBM)
ANY = pl.BlockSpec(memory_space=pl.ANY)


def split(x):
    high = x.astype(BF16)
    return high, (x - high.astype(F32)).astype(BF16)


def masked(rows, live):
    index = lax.broadcasted_iota(jnp.int32, rows.shape, 0)
    return jnp.where(index < live, rows, 0.0)


PREPARE_VMEM, NEAR_VMEM = 46, 32
GROUP = 2


def place():
    mpo = lax.axis_index("mpo")
    return lax.rem(mpo, 2), lax.rem(lax.div(mpo, 2), 2), lax.axis_index("sec")


def sector_rows(wave, sector, block):
    return wave.at[pl.ds(pl.multiple_of(sector * block, block), block), :]


def prepare_kernel(half, live, left, mine_a, mine_b, halo, left_send, src, sem):
    core, side, _ = place()
    block = halo.shape[0]
    send = pltpu.make_async_copy(left.at[pl.ds((1 - core) * half, half)], left_send, sem.at[0])
    send.start()
    mine_a[...] = sector_rows(live, core * half + side, block)[...]
    mine_b[...] = sector_rows(live, core * half + half // 2 + side, block)[...]
    halo[...] = sector_rows(live, (1 - core) * (2 * half - 1), block)[...]
    src[pl.ds(pl.multiple_of(core * (half + 1) * block, block), block), :] = jnp.zeros((block, src.shape[1]), BF16)
    for i in range(half + 1):
        rows = sector_rows(live, core * (half - 1) + i, block)[...]
        put(src, pl.multiple_of((i + 1 - core) * block, block), rows)
    send.wait()


def put(src, at, value):
    wide = value.shape[1]
    high, low = split(value)
    here = pl.ds(at, value.shape[0])
    src[here, 0:wide] = high
    src[here, wide : 2 * wide] = low
    src[here, 2 * wide : 3 * wide] = high


def pack(cls_ref, choose, order, offsets):
    n = jnp.int32(0)
    for t in range(cls_ref.shape[0]):
        chosen, at = choose(cls_ref[t])

        @pl.when(chosen)
        def _(n=n, t=t, at=at):
            order[n] = t
            offsets[n] = at

        n = n + chosen.astype(jnp.int32)
    return n


def add_terms(n, order, offsets, src, left, right, first, acc, tbuf):
    rows = acc.shape[0]
    block = left.shape[-1]
    count = rows // block

    @pl.loop(0, lax.div(n + GROUP - 1, GROUP))
    def _(i):
        terms, real = [], []
        for j in range(GROUP):
            k = jnp.minimum(i * GROUP + j, n - 1)
            real.append(i * GROUP + j < n)
            terms.append(order[k])
            at = pl.ds(pl.multiple_of(offsets[k], block), rows)
            high, low = split(right[terms[j]])
            wide = jnp.concatenate([high, high, low], 0)
            high, low = split(jnp.dot(src[at, :], wide, preferred_element_type=F32))
            for s in range(count):
                here = slice(s * block, (s + 1) * block)
                tbuf[s, j * block : (j + 1) * block, :] = high[here]
                tbuf[s, (GROUP + j) * block : (GROUP + j + 1) * block, :] = low[here]
        for s in range(count):
            blocks = [left[first + s, terms[0]]]
            for j in range(1, GROUP):
                blocks.append(jnp.where(real[j], left[first + s, terms[j]], 0.0))
            high, low = split(jnp.concatenate(blocks, 1))
            acc[s * block : (s + 1) * block, :] += jnp.dot(
                jnp.concatenate([high, high, low], 1),
                jnp.concatenate([tbuf[s], tbuf[s, 0 : GROUP * block]], 0),
                preferred_element_type=F32,
            )


def near_kernel(own, *refs):
    if own:
        cls, left, right, src, acc, *rest = refs
    else:
        cls, left, right, cls_own, left_own, right_own, halo, src_in, acc_in, acc, src, *rest = refs
    tbuf, cls_ref, order, offsets, sem = rest
    block = left.shape[-1]
    half = acc.shape[0] // block
    core, _, _ = place()

    fetch = [pltpu.make_async_copy(cls, cls_ref.at[0], sem.at[0])]
    if not own:
        fetch.append(pltpu.make_async_copy(cls_own, cls_ref.at[1], sem.at[1]))
    for move in fetch:
        move.start()
    halo_at = pl.multiple_of(core * (half + 1) * block, block)
    if own:
        acc[...] = jnp.zeros_like(acc)
    else:
        acc[...] = acc_in[...]
        src[...] = src_in[...]
        put(src, halo_at, halo[...])
    for move in fetch:
        move.wait()

    def near(c):
        at = jnp.where(c == 0, block, jnp.where(c == 3, 2 * block, 0))
        return jnp.logical_or(c == 0, c >= 3), at

    if not own:
        edge = core * (half - 1)
        n = pack(cls_ref.at[1], lambda c: (c == 4 - core, halo_at), order, offsets)
        part = acc.at[pl.ds(pl.multiple_of(edge * block, block), block), :]
        add_terms(n, order, offsets, src, left_own, right_own, core * half + edge, part, tbuf)
    n = pack(cls_ref.at[0], near, order, offsets)
    add_terms(n, order, offsets, src, left, right, core * half if own else 0, acc, tbuf)


def far_kernel(lo, shift, secs, chained, *refs):
    refs = list(refs)
    cls, cls_pair, rows_hbm, left, right, left_pair, right_pair, live, mine, other, acc_in = refs[:11]
    sums_in = refs.pop(11) if chained else None
    acc, sums, src, tbuf, rows_ref, cls_ref, order, offsets, sem = refs[11:]
    rows, cols = acc.shape
    half, _, block, _ = left_pair.shape
    count = rows // block
    core, side, sec = place()
    merged = mine.shape[0] == 1

    moves = [
        pltpu.make_async_copy(rows_hbm, rows_ref, sem.at[0]),
        pltpu.make_async_copy(cls, cls_ref.at[0], sem.at[1]),
        pltpu.make_async_copy(cls_pair, cls_ref.at[1], sem.at[2]),
    ]
    for move in moves:
        move.start()
    acc[...] = acc_in[pl.ds(lo * block, rows), :]
    for k in range(mine.shape[0]):
        for ref, x in ((mine, side), (other, 1 - side)):
            part = ref.shape[1]
            put(src, pl.multiple_of(k * rows + x * part, part), ref[k])
    for move in moves:
        move.wait()

    def far(c):
        above = jnp.logical_and(c == 1, sec + shift < secs)
        below = jnp.logical_and(c == 2, sec >= shift)
        return jnp.logical_or(above, below), jnp.where(c == 1, 0, 0 if merged else rows)

    for g, (l, r, first) in enumerate(((left, right, core * half + lo), (left_pair, right_pair, lo))):
        n = pack(cls_ref.at[g], far, order, offsets)
        add_terms(n, order, offsets, src, l, r, first, acc, tbuf)

    cross = jnp.zeros((8, cols), F32)
    square = jnp.zeros((8, cols), F32)
    for s in range(count):
        sector = core * half + lo + s
        here = pl.ds(s * block, block)
        total = masked(acc[here, :], rows_ref[sector])
        acc[here, :] = total
        value = sector_rows(live, sector, block)[...]
        fold = lambda v: jnp.sum(v.reshape(block // 8, 8, cols), axis=0)
        cross += fold(value * total)
        square += fold(value * value)
    fold = lambda v: sum(v[:, i : i + 128] for i in range(0, cols, 128))
    cross, square = fold(cross), fold(square)
    if chained:
        cross, square = cross + sums_in[0:8, :], square + sums_in[8:16, :]
    sums[0:8, :] = cross
    sums[8:16, :] = square


def final_kernel(sides, block, sums, live, *refs):
    totals, (applied, correction, buf, sem) = refs[:-4], refs[-4:]
    core, _, _ = place()
    half = live.shape[0] // 2
    chunks = len(totals) // 2
    rows = totals[0].shape[0]
    places = []
    moves = []
    for i, total in enumerate(totals):
        c = core if i < chunks else 1 - core
        places.append(pl.ds(pl.multiple_of(c * half + i % chunks * rows, rows), rows))
        moves.append(pltpu.make_async_copy(total, applied.at[places[i], :], sem.at[0, i]))
        moves[-1].start()
    rayleigh = jnp.sum(sums[0:8, :]) / (jnp.sum(sums[8:16, :]) * (1.0 / sides))
    for i, total in enumerate(totals):
        buf[i] = total[...] - rayleigh * live[places[i], :]
        moves.append(pltpu.make_async_copy(buf.at[i], correction.at[places[i], :], sem.at[1, i]))
        moves[-1].start()
    for move in moves:
        move.wait()


def params(limit):
    return pltpu.CompilerParams(vmem_limit_bytes=limit * 2**20)


def cost(flops, moved):
    return pl.CostEstimate(flops=int(flops), bytes_accessed=int(moved), transcendentals=0)


def shape(*dims):
    return jax.ShapeDtypeStruct(dims, F32)


def swap(array, axis, bit):
    pairs = [(i, i ^ bit) for i in range(lax.axis_size(axis))]
    return lax.ppermute(array, axis, pairs)


def everyone(array, axis):
    return (array + swap(array, axis, 1)) + (swap(array, axis, 2) + swap(array, axis, 3))


def after(array, *others):
    return lax.optimization_barrier((array, *others))[0]


def local(wavefunction, left_blocks, right_blocks, block_rows, term_charge):
    sector_count = block_rows.shape[0]
    block = left_blocks.shape[2]
    terms = left_blocks.shape[1]
    cols = wavefunction.shape[1]
    secs, mpos, reps = (lax.axis_size(a) for a in ("sec", "mpo", "rep"))
    half = sector_count // 2
    part = half // 2
    shift = QD // sector_count
    merged = secs <= 2 * shift
    row = jnp.arange(block, dtype=jnp.int32)
    live = jnp.where((row < block_rows[:, None])[:, :, None], wavefunction.reshape(sector_count, block, cols), 0.0)
    live = live.reshape(sector_count * block, cols)
    whole = live
    if reps > 1:
        whole = lax.all_gather(live, "rep", axis=1, tiled=True)
    wide = whole.shape[1]

    up = [(i, i - shift) for i in range(shift, secs)]
    down = [(i, i + shift) for i in range(secs - shift)]

    def far(array):
        if merged:
            return lax.ppermute(array, "sec", up + down)[None]
        return jnp.stack([lax.ppermute(array, "sec", p) for p in (up, down)])

    halo_pairs = []
    for m in range(mpos):
        for z in range(secs):
            to = z + 1 if m % 2 == 0 else z - 1
            if 0 <= to < secs:
                halo_pairs.append((z * mpos + m, to * mpos + m))

    rows = part * block
    blocks = shape(half, terms, block, block)
    source_shape = ((half + 2) * block, 3 * wide)
    cls_pair = swap(term_charge, "mpo", 1)
    mine_a, mine_b, halo, left_send, src = pl.pallas_call(
        functools.partial(prepare_kernel, half),
        out_shape=(shape(block, wide),) * 3 + (blocks, jax.ShapeDtypeStruct(source_shape, BF16)),
        in_specs=[VMEM, ANY],
        out_specs=(VMEM,) * 5,
        scratch_shapes=[pltpu.SemaphoreType.DMA((1,))],
        compiler_params=params(PREPARE_VMEM),
        cost_estimate=cost(1, 1),
        name="prepare",
    )(after(whole, cls_pair), left_blocks)
    far_a = far(mine_a)
    halo = lax.ppermute(halo, ("sec", "mpo"), halo_pairs)
    right_pair = swap(right_blocks, "mpo", 1)
    left_pair = swap(left_send, "mpo", 1)

    lists = [pltpu.SMEM((terms,), jnp.int32)] * 2

    def near(own, *args):
        return pl.pallas_call(
            functools.partial(near_kernel, own),
            out_shape=shape(half * block, cols),
            in_specs=[ANY] + [VMEM] * 3 if own else [ANY, VMEM, VMEM] * 2 + [VMEM] * 3,
            out_specs=VMEM,
            scratch_shapes=([] if own else [pltpu.VMEM(source_shape, BF16)])
            + [pltpu.VMEM((half, 2 * GROUP * block, cols), BF16), pltpu.SMEM((2, terms), jnp.int32)]
            + lists
            + [pltpu.SemaphoreType.DMA((2,))],
            compiler_params=params(NEAR_VMEM),
            cost_estimate=cost(1, 1),
            name="own_near" if own else "pair_near",
        )(*args)

    def add_far(lo, far, acc, sums):
        extra = () if sums is None else (sums,)
        return pl.pallas_call(
            functools.partial(far_kernel, lo, shift, secs, sums is not None),
            out_shape=(shape(rows, cols), shape(16, 128)),
            in_specs=[ANY] * 3 + [VMEM] * (8 + len(extra)),
            out_specs=(VMEM, VMEM),
            scratch_shapes=[
                pltpu.VMEM((far[0].shape[0] * rows, 3 * wide), BF16),
                pltpu.VMEM((part, 2 * GROUP * block, cols), BF16),
                pltpu.SMEM((sector_count,), jnp.int32),
                pltpu.SMEM((2, terms), jnp.int32),
                *lists,
                pltpu.SemaphoreType.DMA((3,)),
            ],
            compiler_params=params(32),
            cost_estimate=cost(1, 1),
            name="far",
        )(term_charge, cls_pair, block_rows, left_blocks, right_blocks, left_pair, right_pair, live, *far, acc, *extra)

    acc = near(True, term_charge, left_blocks, right_blocks, src)
    far_b = far(after(mine_b, acc))
    acc = near(False, cls_pair, left_pair, right_pair, term_charge, left_blocks, right_blocks, halo, src, acc)
    other_a = swap(after(far_a, acc), "mpo", 2)
    other_b = swap(after(far_b, acc), "mpo", 2)
    part_a, sums = add_far(0, (far_a, other_a), acc, None)
    recv_a = swap(part_a, "mpo", 2)
    part_b, sums = add_far(part, (far_b, other_b), acc, sums)
    recv_b = swap(part_b, "mpo", 2)

    if secs == 4:
        sums = everyone(sums, "sec")
    else:
        sums = lax.psum(sums, "sec")
    if reps > 1:
        sums = lax.psum(sums, "rep")
    sums = everyone(after(sums, recv_a), "mpo")
    totals = [part_a + recv_a, part_b + after(recv_b, sums)]
    totals += [swap(total, "mpo", 1) for total in totals]

    out = shape(sector_count * block, cols)
    return pl.pallas_call(
        functools.partial(final_kernel, mpos // 2, block),
        out_shape=(out, out),
        in_specs=[VMEM] * (2 + len(totals)),
        out_specs=(ANY, ANY),
        scratch_shapes=[
            pltpu.VMEM((len(totals), rows, cols), F32),
            pltpu.SemaphoreType.DMA((2, len(totals))),
        ],
        compiler_params=params(32),
        cost_estimate=cost(1, 1),
        name="residual",
    )(sums, live, *totals)


def solution(mesh):
    in_specs = (
        P(("runs", "sec"), "rep"),
        P(("runs", "sec"), "mpo", None, None),
        P(("runs", "mpo"), None, "rep"),
        P(("runs", "sec")),
        P("mpo"),
    )
    out_specs = (P(("runs", "sec"), "rep"), P(("runs", "sec"), "rep"))
    return jax.shard_map(local, mesh=mesh, in_specs=in_specs, out_specs=out_specs, check_vma=False)
```

```python
import functools

import jax
import jax.numpy as jnp
from jax import lax
from jax.experimental import pallas as pl
from jax.experimental.pallas import tpu as pltpu
from jax.sharding import PartitionSpec as P

QD = 16
F32 = jnp.float32
BF16 = jnp.bfloat16
VMEM = pl.BlockSpec(memory_space=pltpu.VMEM)
SMEM = pl.BlockSpec(memory_space=pltpu.SMEM)
HBM = pl.BlockSpec(memory_space=pltpu.HBM)
ANY = pl.BlockSpec(memory_space=pl.ANY)


def split(x):
    high = x.astype(BF16)
    return high, (x - high.astype(F32)).astype(BF16)


def masked(rows, live):
    index = lax.broadcasted_iota(jnp.int32, rows.shape, 0)
    return jnp.where(index < live, rows, 0.0)


PREPARE_VMEM, OWN_VMEM, NEAR_VMEM = 62, 46, 32
GROUP = 2


def place():
    mpo = lax.axis_index("mpo")
    return lax.rem(mpo, 2), lax.rem(lax.div(mpo, 2), 2), lax.axis_index("sec")


def sector_rows(wave, sector, block):
    return wave.at[pl.ds(pl.multiple_of(sector * block, block), block), :]


def prepare_kernel(half, rows_hbm, wave, left, mine_a, mine_b, halo, left_send, stage, rows_ref, sem, stage_sem):
    core, side, _ = place()
    block = halo.shape[0]
    rows = pltpu.make_async_copy(rows_hbm, rows_ref, sem.at[0])
    rows.start()
    wanted = (
        (core * half + side, mine_a),
        (core * half + half // 2 + side, mine_b),
        ((1 - core) * (2 * half - 1), halo),
    )
    reads = [
        pltpu.make_async_copy(sector_rows(wave, sector, block), ref, sem.at[i + 1])
        for i, (sector, ref) in enumerate(wanted)
    ]
    pieces = [
        (
            pltpu.make_async_copy(left.at[(1 - core) * half + s], stage.at[s], stage_sem.at[0, s]),
            pltpu.make_async_copy(stage.at[s], left_send.at[s], stage_sem.at[1, s]),
        )
        for s in range(half)
    ]
    for move in reads + [piece[0] for piece in pieces]:
        move.start()
    rows.wait()
    for move, (sector, ref) in zip(reads, wanted):
        move.wait()
        ref[...] = masked(ref[...], rows_ref[sector])
    for read, write in pieces:
        read.wait()
        write.start()
    for _, write in pieces:
        write.wait()


def put(src, at, value):
    wide = value.shape[1]
    high, low = split(value)
    here = pl.ds(at, value.shape[0])
    src[here, 0:wide] = high
    src[here, wide : 2 * wide] = low
    src[here, 2 * wide : 3 * wide] = high


def pack(cls_ref, choose, order, offsets):
    n = jnp.int32(0)
    for t in range(cls_ref.shape[0]):
        chosen, at = choose(cls_ref[t])

        @pl.when(chosen)
        def _(n=n, t=t, at=at):
            order[n] = t
            offsets[n] = at

        n = n + chosen.astype(jnp.int32)
    return n


def add_terms(n, order, offsets, src, left, right, first, acc, tbuf, right_ready=None, left_ready=None):
    rows = acc.shape[0]
    block = left.shape[-1]
    count = rows // block

    @pl.loop(0, lax.div(n + GROUP - 1, GROUP))
    def _(i):
        terms, real = [], []
        for j in range(GROUP):
            k = jnp.minimum(i * GROUP + j, n - 1)
            real.append(i * GROUP + j < n)
            terms.append(order[k])
            if right_ready is not None:

                @pl.when(real[j])
                def _(j=j):
                    right_ready(terms[j])

            at = pl.ds(pl.multiple_of(offsets[k], block), rows)
            high, low = split(right[terms[j]])
            wide = jnp.concatenate([high, high, low], 0)
            high, low = split(jnp.dot(src[at, :], wide, preferred_element_type=F32))
            for s in range(count):
                here = slice(s * block, (s + 1) * block)
                tbuf[s, j * block : (j + 1) * block, :] = high[here]
                tbuf[s, (GROUP + j) * block : (GROUP + j + 1) * block, :] = low[here]
        if left_ready is not None:
            pl.when(i == 0)(left_ready)
        for s in range(count):
            blocks = [left[first + s, terms[0]]]
            for j in range(1, GROUP):
                blocks.append(jnp.where(real[j], left[first + s, terms[j]], 0.0))
            high, low = split(jnp.concatenate(blocks, 1))
            acc[s * block : (s + 1) * block, :] += jnp.dot(
                jnp.concatenate([high, high, low], 1),
                jnp.concatenate([tbuf[s], tbuf[s, 0 : GROUP * block]], 0),
                preferred_element_type=F32,
            )


def near_kernel(own, *refs):
    if own:
        cls, left_hbm, right_hbm, rows_hbm, whole, wave, acc, left, right, src, live, rows_ref, load, *rest = refs
    else:
        cls, left, right, src, acc_in, acc, *rest = refs
    tbuf, cls_ref, order, offsets, sem = rest
    half, terms, block, _ = left.shape
    core, _, _ = place()

    fetch = [pltpu.make_async_copy(cls, cls_ref, sem.at[0])]
    if own:
        fetch.append(pltpu.make_async_copy(rows_hbm, rows_ref, sem.at[1]))
    for move in fetch:
        move.start()
    if own:
        left_move = pltpu.make_async_copy(left_hbm.at[pl.ds(core * half, half)], left, load.at[terms])
        right_moves = lambda t: pltpu.make_async_copy(right_hbm.at[t], right.at[t], load.at[t])
        for t in range(terms):
            right_moves(t).start()
            if t == 1:
                left_move.start()
        acc[...] = jnp.zeros_like(acc)
        halo_at = pl.multiple_of(core * (half + 1) * block, block)
        src[pl.ds(halo_at, block), :] = jnp.zeros((block, src.shape[1]), BF16)
    else:
        acc[...] = acc_in[...]
    for move in fetch:
        move.wait()
    if own:
        for s in range(2 * half):
            here = pl.ds(s * block, block)
            live[here, :] = masked(wave[here, :], rows_ref[s])
        for i in range(half + 1):
            sector = core * (half - 1) + i
            rows = masked(sector_rows(whole, sector, block)[...], rows_ref[sector])
            put(src, pl.multiple_of((i + 1 - core) * block, block), rows)

    def near(c):
        at = jnp.where(c == 0, block, jnp.where(c == 3, 2 * block, 0))
        return jnp.logical_or(c == 0, c >= 3), at

    n = pack(cls_ref, near, order, offsets)
    if not own:
        add_terms(n, order, offsets, src, left, right, 0, acc, tbuf)
        return
    add_terms(n, order, offsets, src, left, right, 0, acc, tbuf, lambda t: right_moves(t).wait(), left_move.wait)
    for t in range(terms):

        @pl.when(jnp.logical_not(near(cls_ref[t])[0]))
        def _(t=t):
            right_moves(t).wait()

    @pl.when(n == 0)
    def _():
        left_move.wait()


def far_kernel(lo, shift, secs, chained, *refs):
    refs = list(refs)
    cls, cls_pair, rows_hbm, left, right, left_pair, right_pair, live, mine, other, halo, acc_in = refs[:12]
    sums_in = refs.pop(12) if chained else None
    acc, sums, src, tbuf, rows_ref, cls_ref, order, offsets, sem = refs[12:]
    rows, cols = acc.shape
    half, _, block, _ = left.shape
    count = rows // block
    core, side, sec = place()
    merged = mine.shape[0] == 1

    moves = [
        pltpu.make_async_copy(rows_hbm, rows_ref, sem.at[0]),
        pltpu.make_async_copy(cls, cls_ref.at[0], sem.at[1]),
        pltpu.make_async_copy(cls_pair, cls_ref.at[1], sem.at[2]),
    ]
    for move in moves:
        move.start()
    acc[...] = acc_in[pl.ds(lo * block, rows), :]
    for k in range(mine.shape[0]):
        for ref, x in ((mine, side), (other, 1 - side)):
            part = ref.shape[1]
            put(src, pl.multiple_of(k * rows + x * part, part), ref[k])
    halo_at = mine.shape[0] * rows
    put(src, halo_at, halo[...])
    for move in moves:
        move.wait()

    def far(c):
        above = jnp.logical_and(c == 1, sec + shift < secs)
        below = jnp.logical_and(c == 2, sec >= shift)
        return jnp.logical_or(above, below), jnp.where(c == 1, 0, 0 if merged else rows)

    for g, (l, r) in enumerate(((left, right), (left_pair, right_pair))):
        n = pack(cls_ref.at[g], far, order, offsets)
        add_terms(n, order, offsets, src, l, r, lo, acc, tbuf)
        n = pack(cls_ref.at[g], lambda c: (c == 4 - core, halo_at), order, offsets)
        n = jnp.where(core == (0 if lo == 0 else 1), n, 0)
        edge = core * (count - 1)
        part = acc.at[pl.ds(pl.multiple_of(edge * block, block), block), :]
        add_terms(n, order, offsets, src, l, r, lo + edge, part, tbuf)

    cross = jnp.zeros((8, cols), F32)
    square = jnp.zeros((8, cols), F32)
    for s in range(count):
        sector = core * half + lo + s
        here = pl.ds(s * block, block)
        total = masked(acc[here, :], rows_ref[sector])
        acc[here, :] = total
        value = sector_rows(live, sector, block)[...]
        fold = lambda v: jnp.sum(v.reshape(block // 8, 8, cols), axis=0)
        cross += fold(value * total)
        square += fold(value * value)
    fold = lambda v: sum(v[:, i : i + 128] for i in range(0, cols, 128))
    cross, square = fold(cross), fold(square)
    if chained:
        cross, square = cross + sums_in[0:8, :], square + sums_in[8:16, :]
    sums[0:8, :] = cross
    sums[8:16, :] = square


def final_kernel(sides, block, sums, live, *refs):
    totals, (applied, correction, buf, sem) = refs[:-4], refs[-4:]
    core, _, _ = place()
    half = live.shape[0] // 2
    chunks = len(totals) // 2
    rows = totals[0].shape[0]
    places = []
    moves = []
    for i, total in enumerate(totals):
        c = core if i < chunks else 1 - core
        places.append(pl.ds(pl.multiple_of(c * half + i % chunks * rows, rows), rows))
        moves.append(pltpu.make_async_copy(total, applied.at[places[i], :], sem.at[0, i]))
        moves[-1].start()
    rayleigh = jnp.sum(sums[0:8, :]) / (jnp.sum(sums[8:16, :]) * (1.0 / sides))
    for i, total in enumerate(totals):
        buf[i] = total[...] - rayleigh * live[places[i], :]
        moves.append(pltpu.make_async_copy(buf.at[i], correction.at[places[i], :], sem.at[1, i]))
        moves[-1].start()
    for move in moves:
        move.wait()


def params(limit):
    return pltpu.CompilerParams(vmem_limit_bytes=limit * 2**20)


def cost(flops, moved):
    return pl.CostEstimate(flops=int(flops), bytes_accessed=int(moved), transcendentals=0)


def shape(*dims):
    return jax.ShapeDtypeStruct(dims, F32)


def swap(array, axis, bit):
    pairs = [(i, i ^ bit) for i in range(lax.axis_size(axis))]
    return lax.ppermute(array, axis, pairs)


def everyone(array, axis):
    return (array + swap(array, axis, 1)) + (swap(array, axis, 2) + swap(array, axis, 3))


def after(array, *others):
    return lax.optimization_barrier((array, *others))[0]


def local(wavefunction, left_blocks, right_blocks, block_rows, term_charge):
    sector_count = block_rows.shape[0]
    block = left_blocks.shape[2]
    terms = left_blocks.shape[1]
    cols = wavefunction.shape[1]
    secs, mpos, reps = (lax.axis_size(a) for a in ("sec", "mpo", "rep"))
    half = sector_count // 2
    part = half // 2
    shift = QD // sector_count
    merged = secs <= 2 * shift
    whole = wavefunction
    if reps > 1:
        whole = lax.all_gather(wavefunction, "rep", axis=1, tiled=True)
    wide = whole.shape[1]

    up = [(i, i - shift) for i in range(shift, secs)]
    down = [(i, i + shift) for i in range(secs - shift)]

    def far(array):
        if merged:
            return lax.ppermute(array, "sec", up + down)[None]
        return jnp.stack([lax.ppermute(array, "sec", p) for p in (up, down)])

    halo_pairs = []
    for m in range(mpos):
        for z in range(secs):
            to = z + 1 if m % 2 == 0 else z - 1
            if 0 <= to < secs:
                halo_pairs.append((z * mpos + m, to * mpos + m))

    rows = part * block
    blocks = shape(half, terms, block, block)
    source_shape = ((half + 2) * block, 3 * wide)
    cls_pair = swap(term_charge, "mpo", 1)
    mine_a, mine_b, halo, left_send = pl.pallas_call(
        functools.partial(prepare_kernel, half),
        out_shape=(shape(block, wide),) * 3 + (blocks,),
        in_specs=[ANY] * 3,
        out_specs=(VMEM,) * 3 + (ANY,),
        scratch_shapes=[
            pltpu.VMEM(blocks.shape, F32),
            pltpu.SMEM((sector_count,), jnp.int32),
            pltpu.SemaphoreType.DMA((4,)),
            pltpu.SemaphoreType.DMA((2, half)),
        ],
        compiler_params=params(PREPARE_VMEM),
        cost_estimate=cost(1, 1),
        name="prepare",
    )(after(block_rows, cls_pair), whole, left_blocks)
    far_a = far(mine_a)
    right_pair = swap(after(right_blocks, mine_a), "mpo", 1)
    left_pair = swap(left_send, "mpo", 1)

    lists = [pltpu.SMEM((terms,), jnp.int32)] * 2

    def near(own, *args):
        outs = [shape(half * block, cols)]
        scratch = []
        if own:
            outs += [blocks, shape(terms, wide, cols)]
            outs += [jax.ShapeDtypeStruct(source_shape, BF16), shape(sector_count * block, cols)]
            scratch = [pltpu.SMEM((sector_count,), jnp.int32), pltpu.SemaphoreType.DMA((terms + 1,))]
        return pl.pallas_call(
            functools.partial(near_kernel, own),
            out_shape=tuple(outs),
            in_specs=[ANY] * 4 + [VMEM] * 2 if own else [ANY] + [VMEM] * 4,
            out_specs=(VMEM,) * len(outs),
            scratch_shapes=scratch
            + [pltpu.VMEM((half, 2 * GROUP * block, cols), BF16), pltpu.SMEM((terms,), jnp.int32)]
            + lists
            + [pltpu.SemaphoreType.DMA((2,))],
            compiler_params=params(OWN_VMEM if own else NEAR_VMEM),
            cost_estimate=cost(1, 1),
            name="own_near" if own else "pair_near",
        )(*args)

    def add_far(lo, far, acc, sums):
        extra = () if sums is None else (sums,)
        return pl.pallas_call(
            functools.partial(far_kernel, lo, shift, secs, sums is not None),
            out_shape=(shape(rows, cols), shape(16, 128)),
            in_specs=[ANY] * 3 + [VMEM] * (9 + len(extra)),
            out_specs=(VMEM, VMEM),
            scratch_shapes=[
                pltpu.VMEM((far[0].shape[0] * rows + block, 3 * wide), BF16),
                pltpu.VMEM((part, 2 * GROUP * block, cols), BF16),
                pltpu.SMEM((sector_count,), jnp.int32),
                pltpu.SMEM((2, terms), jnp.int32),
                *lists,
                pltpu.SemaphoreType.DMA((3,)),
            ],
            compiler_params=params(32),
            cost_estimate=cost(1, 1),
            name="far",
        )(term_charge, cls_pair, block_rows, left, right, left_pair, right_pair, live, *far, halo, acc, *extra)

    acc, left, right, src, live = near(
        True, term_charge, left_blocks, right_blocks, after(block_rows, mine_a), whole, wavefunction
    )
    far_b = far(after(mine_b, acc))
    halo = lax.ppermute(after(halo, acc), ("sec", "mpo"), halo_pairs)
    (acc,) = near(False, cls_pair, left_pair, right_pair, src, acc)
    other_a = swap(after(far_a, acc), "mpo", 2)
    other_b = swap(after(far_b, acc), "mpo", 2)
    part_a, sums = add_far(0, (far_a, other_a), acc, None)
    recv_a = swap(part_a, "mpo", 2)
    part_b, sums = add_far(part, (far_b, other_b), acc, sums)
    recv_b = swap(part_b, "mpo", 2)

    if secs == 4:
        sums = everyone(sums, "sec")
    else:
        sums = lax.psum(sums, "sec")
    if reps > 1:
        sums = lax.psum(sums, "rep")
    sums = everyone(after(sums, recv_a), "mpo")
    totals = [part_a + recv_a, part_b + after(recv_b, sums)]
    totals += [swap(total, "mpo", 1) for total in totals]

    out = shape(sector_count * block, cols)
    return pl.pallas_call(
        functools.partial(final_kernel, mpos // 2, block),
        out_shape=(out, out),
        in_specs=[VMEM] * (2 + len(totals)),
        out_specs=(ANY, ANY),
        scratch_shapes=[
            pltpu.VMEM((len(totals), rows, cols), F32),
            pltpu.SemaphoreType.DMA((2, len(totals))),
        ],
        compiler_params=params(32),
        cost_estimate=cost(1, 1),
        name="residual",
    )(sums, live, *totals)


def solution(mesh):
    in_specs = (
        P(("runs", "sec"), "rep"),
        P(("runs", "sec"), "mpo", None, None),
        P(("runs", "mpo"), None, "rep"),
        P(("runs", "sec")),
        P("mpo"),
    )
    out_specs = (P(("runs", "sec"), "rep"), P(("runs", "sec"), "rep"))
    return jax.shard_map(local, mesh=mesh, in_specs=in_specs, out_specs=out_specs, check_vma=False)
```

```python
import functools

import jax
import jax.numpy as jnp
from jax import lax
from jax.experimental import pallas as pl
from jax.experimental.pallas import tpu as pltpu
from jax.sharding import PartitionSpec as P

QD = 16
F32 = jnp.float32
BF16 = jnp.bfloat16
VMEM = pl.BlockSpec(memory_space=pltpu.VMEM)
SMEM = pl.BlockSpec(memory_space=pltpu.SMEM)
HBM = pl.BlockSpec(memory_space=pltpu.HBM)
ANY = pl.BlockSpec(memory_space=pl.ANY)


def split(x):
    high = x.astype(BF16)
    return high, (x - high.astype(F32)).astype(BF16)


def masked(rows, live):
    index = lax.broadcasted_iota(jnp.int32, rows.shape, 0)
    return jnp.where(index < live, rows, 0.0)


PREPARE_VMEM, CUT_VMEM, OWN_VMEM, NEAR_VMEM = 62, 50, 46, 32
GROUP = 2


def place():
    mpo = lax.axis_index("mpo")
    return lax.rem(mpo, 2), lax.rem(lax.div(mpo, 2), 2), lax.axis_index("sec")


def sector_rows(wave, sector, block):
    return wave.at[pl.ds(pl.multiple_of(sector * block, block), block), :]


def prepare_kernel(half, rows_hbm, wave, *refs):
    *sends, halo, rows_ref, sem = refs
    core, side, _ = place()
    block = halo.shape[0]
    piece = block // 2
    rows = pltpu.make_async_copy(rows_hbm, rows_ref, sem.at[0])
    rows.start()
    wanted = [(halo, (1 - core) * (2 * half - 1) * block)]
    first = core * half * block
    for ref in sends:
        wanted.append((ref, first + side * ref.shape[0]))
        first += 2 * ref.shape[0]
    reads = []
    for i, (ref, first) in enumerate(wanted):
        source = wave.at[pl.ds(pl.multiple_of(first, piece), ref.shape[0]), :]
        reads.append(pltpu.make_async_copy(source, ref, sem.at[i + 1]))
        reads[i].start()
    rows.wait()
    for read, (ref, first) in zip(reads, wanted):
        read.wait()
        for at in range(0, ref.shape[0], piece):
            here = pl.ds(at, piece)
            live = rows_ref[lax.div(first + at, block)] - lax.rem(first + at, block)
            ref[here, :] = masked(ref[here, :], live)


def cut_kernel(half, left, left_send, sem):
    core, _, _ = place()
    move = pltpu.make_async_copy(left.at[pl.ds((1 - core) * half, half)], left_send, sem.at[0])
    move.start()
    move.wait()


def put(src, at, value):
    wide = value.shape[1]
    high, low = split(value)
    here = pl.ds(at, value.shape[0])
    src[here, 0:wide] = high
    src[here, wide : 2 * wide] = low
    src[here, 2 * wide : 3 * wide] = high


def pack(cls_ref, choose, order, offsets):
    n = jnp.int32(0)
    for t in range(cls_ref.shape[0]):
        chosen, at = choose(cls_ref[t])

        @pl.when(chosen)
        def _(n=n, t=t, at=at):
            order[n] = t
            offsets[n] = at

        n = n + chosen.astype(jnp.int32)
    return n


def add_terms(n, order, offsets, src, left, right, first, acc, tbuf, right_ready=None, left_ready=None):
    rows = acc.shape[0]
    block = left.shape[-1]
    count = rows // block

    @pl.loop(0, lax.div(n + GROUP - 1, GROUP))
    def _(i):
        terms, real = [], []
        for j in range(GROUP):
            k = jnp.minimum(i * GROUP + j, n - 1)
            real.append(i * GROUP + j < n)
            terms.append(order[k])
            if right_ready is not None:

                @pl.when(real[j])
                def _(j=j):
                    right_ready(terms[j])

            at = pl.ds(pl.multiple_of(offsets[k], block), rows)
            high, low = split(right[terms[j]])
            wide = jnp.concatenate([high, high, low], 0)
            high, low = split(jnp.dot(src[at, :], wide, preferred_element_type=F32))
            for s in range(count):
                here = slice(s * block, (s + 1) * block)
                tbuf[s, j * block : (j + 1) * block, :] = high[here]
                tbuf[s, (GROUP + j) * block : (GROUP + j + 1) * block, :] = low[here]
        if left_ready is not None:
            pl.when(i == 0)(left_ready)
        for s in range(count):
            blocks = [left[first + s, terms[0]]]
            for j in range(1, GROUP):
                blocks.append(jnp.where(real[j], left[first + s, terms[j]], 0.0))
            high, low = split(jnp.concatenate(blocks, 1))
            acc[s * block : (s + 1) * block, :] += jnp.dot(
                jnp.concatenate([high, high, low], 1),
                jnp.concatenate([tbuf[s], tbuf[s, 0 : GROUP * block]], 0),
                preferred_element_type=F32,
            )


def near_kernel(own, *refs):
    if own:
        cls, left_hbm, right_hbm, rows_hbm, whole, wave, acc, left, right, src, live, rows_ref, load, *rest = refs
    else:
        cls, left, right, src, acc_in, acc, *rest = refs
    tbuf, cls_ref, order, offsets, sem = rest
    half, terms, block, _ = left.shape
    core, _, _ = place()

    fetch = [pltpu.make_async_copy(cls, cls_ref, sem.at[0])]
    if own:
        fetch.append(pltpu.make_async_copy(rows_hbm, rows_ref, sem.at[1]))
    for move in fetch:
        move.start()
    if own:
        left_move = pltpu.make_async_copy(left_hbm.at[pl.ds(core * half, half)], left, load.at[terms])
        right_moves = lambda t: pltpu.make_async_copy(right_hbm.at[t], right.at[t], load.at[t])
        for t in range(terms):
            right_moves(t).start()
            if t == 1:
                left_move.start()
        acc[...] = jnp.zeros_like(acc)
        halo_at = pl.multiple_of(core * (half + 1) * block, block)
        src[pl.ds(halo_at, block), :] = jnp.zeros((block, src.shape[1]), BF16)
    else:
        acc[...] = acc_in[...]
    for move in fetch:
        move.wait()
    if own:
        for s in range(2 * half):
            here = pl.ds(s * block, block)
            live[here, :] = masked(wave[here, :], rows_ref[s])
        for i in range(half + 1):
            sector = core * (half - 1) + i
            rows = masked(sector_rows(whole, sector, block)[...], rows_ref[sector])
            put(src, pl.multiple_of((i + 1 - core) * block, block), rows)

    def near(c):
        at = jnp.where(c == 0, block, jnp.where(c == 3, 2 * block, 0))
        return jnp.logical_or(c == 0, c >= 3), at

    n = pack(cls_ref, near, order, offsets)
    if not own:
        add_terms(n, order, offsets, src, left, right, 0, acc, tbuf)
        return
    add_terms(n, order, offsets, src, left, right, 0, acc, tbuf, lambda t: right_moves(t).wait(), left_move.wait)
    for t in range(terms):

        @pl.when(jnp.logical_not(near(cls_ref[t])[0]))
        def _(t=t):
            right_moves(t).wait()

    @pl.when(n == 0)
    def _():
        left_move.wait()


def far_kernel(lo, shift, secs, chained, *refs):
    refs = list(refs)
    cls, cls_pair, rows_hbm, left, right, left_pair, right_pair, live, mine, other, halo, acc_in = refs[:12]
    sums_in = refs.pop(12) if chained else None
    acc, sums, src, tbuf, rows_ref, cls_ref, order, offsets, sem = refs[12:]
    rows, cols = acc.shape
    half, _, block, _ = left.shape
    count = rows // block
    core, side, sec = place()
    merged = mine.shape[0] == 1

    moves = [
        pltpu.make_async_copy(rows_hbm, rows_ref, sem.at[0]),
        pltpu.make_async_copy(cls, cls_ref.at[0], sem.at[1]),
        pltpu.make_async_copy(cls_pair, cls_ref.at[1], sem.at[2]),
    ]
    for move in moves:
        move.start()
    acc[...] = acc_in[pl.ds(lo * block, rows), :]
    for k in range(mine.shape[0]):
        for ref, x in ((mine, side), (other, 1 - side)):
            part = ref.shape[1]
            put(src, pl.multiple_of(k * rows + x * part, part), ref[k])
    halo_at = mine.shape[0] * rows
    put(src, halo_at, halo[...])
    for move in moves:
        move.wait()

    def far(c):
        above = jnp.logical_and(c == 1, sec + shift < secs)
        below = jnp.logical_and(c == 2, sec >= shift)
        return jnp.logical_or(above, below), jnp.where(c == 1, 0, 0 if merged else rows)

    for g, (l, r) in enumerate(((left, right), (left_pair, right_pair))):
        n = pack(cls_ref.at[g], far, order, offsets)
        add_terms(n, order, offsets, src, l, r, lo, acc, tbuf)
        n = pack(cls_ref.at[g], lambda c: (c == 4 - core, halo_at), order, offsets)
        n = jnp.where(core == (0 if lo == 0 else 1), n, 0)
        edge = core * (count - 1)
        part = acc.at[pl.ds(pl.multiple_of(edge * block, block), block), :]
        add_terms(n, order, offsets, src, l, r, lo + edge, part, tbuf)

    cross = jnp.zeros((8, cols), F32)
    square = jnp.zeros((8, cols), F32)
    for s in range(count):
        sector = core * half + lo + s
        here = pl.ds(s * block, block)
        total = masked(acc[here, :], rows_ref[sector])
        acc[here, :] = total
        value = sector_rows(live, sector, block)[...]
        fold = lambda v: jnp.sum(v.reshape(block // 8, 8, cols), axis=0)
        cross += fold(value * total)
        square += fold(value * value)
    fold = lambda v: sum(v[:, i : i + 128] for i in range(0, cols, 128))
    cross, square = fold(cross), fold(square)
    if chained:
        cross, square = cross + sums_in[0:8, :], square + sums_in[8:16, :]
    sums[0:8, :] = cross
    sums[8:16, :] = square


def final_kernel(sides, sums, live, *refs):
    totals, (applied, correction, buf, sem) = refs[:-4], refs[-4:]
    core, _, _ = place()
    half = live.shape[0] // 2
    chunks = len(totals) // 2
    places = []
    moves = []
    at = 0
    for i, total in enumerate(totals):
        rows = total.shape[0]
        first = (core if i < chunks else 1 - core) * half + at % half
        at += rows
        places.append(pl.ds(pl.multiple_of(first, 8), rows))
        moves.append(pltpu.make_async_copy(total, applied.at[places[i], :], sem.at[0, i]))
        moves[-1].start()
    rayleigh = jnp.sum(sums[0:8, :]) / (jnp.sum(sums[8:16, :]) * (1.0 / sides))
    for i, total in enumerate(totals):
        here = places[i]
        buf[here, :] = total[...] - rayleigh * live[here, :]
        moves.append(pltpu.make_async_copy(buf.at[here, :], correction.at[here, :], sem.at[1, i]))
        moves[-1].start()
    for move in moves:
        move.wait()


def params(limit):
    return pltpu.CompilerParams(vmem_limit_bytes=limit * 2**20)


def cost(flops, moved):
    return pl.CostEstimate(flops=int(flops), bytes_accessed=int(moved), transcendentals=0)


def shape(*dims):
    return jax.ShapeDtypeStruct(dims, F32)


def swap(array, axis, bit):
    pairs = [(i, i ^ bit) for i in range(lax.axis_size(axis))]
    return lax.ppermute(array, axis, pairs)


def everyone(array, axis):
    return (array + swap(array, axis, 1)) + (swap(array, axis, 2) + swap(array, axis, 3))


def after(array, *others):
    return lax.optimization_barrier((array, *others))[0]


def local(wavefunction, left_blocks, right_blocks, block_rows, term_charge):
    sector_count = block_rows.shape[0]
    block = left_blocks.shape[2]
    terms = left_blocks.shape[1]
    cols = wavefunction.shape[1]
    secs, mpos, reps = (lax.axis_size(a) for a in ("sec", "mpo", "rep"))
    half = sector_count // 2
    part = half // 2
    shift = QD // sector_count
    merged = secs <= 2 * shift
    whole = wavefunction
    if reps > 1:
        whole = lax.all_gather(wavefunction, "rep", axis=1, tiled=True)
    wide = whole.shape[1]

    up = [(i, i - shift) for i in range(shift, secs)]
    down = [(i, i + shift) for i in range(secs - shift)]

    def far(array):
        if merged:
            return lax.ppermute(array, "sec", up + down)[None]
        return jnp.stack([lax.ppermute(array, "sec", p) for p in (up, down)])

    halo_pairs = []
    for m in range(mpos):
        for z in range(secs):
            to = z + 1 if m % 2 == 0 else z - 1
            if 0 <= to < secs:
                halo_pairs.append((z * mpos + m, to * mpos + m))

    blocks = shape(half, terms, block, block)
    source_shape = ((half + 2) * block, 3 * wide)
    sizes = (half // 2, half // 2)
    cls_pair = swap(term_charge, "mpo", 1)
    mine_a, mine_b, halo = pl.pallas_call(
        functools.partial(prepare_kernel, half),
        out_shape=tuple(shape(size * block // 2, wide) for size in sizes) + (shape(block, wide),),
        in_specs=[ANY] * 2,
        out_specs=(VMEM,) * 3,
        scratch_shapes=[pltpu.SMEM((sector_count,), jnp.int32), pltpu.SemaphoreType.DMA((4,))],
        compiler_params=params(PREPARE_VMEM),
        cost_estimate=cost(1, 1),
        name="prepare",
    )(block_rows, whole)
    (left_send,) = pl.pallas_call(
        functools.partial(cut_kernel, half),
        out_shape=(blocks,),
        in_specs=[ANY],
        out_specs=(VMEM,),
        scratch_shapes=[pltpu.SemaphoreType.DMA((1,))],
        compiler_params=params(CUT_VMEM),
        cost_estimate=cost(1, 1),
        name="pair_blocks",
    )(after(left_blocks, mine_a, cls_pair))
    left_pair = swap(left_send, "mpo", 1)
    far_a = far(mine_a)
    right_pair = swap(after(right_blocks, mine_a), "mpo", 1)

    lists = [pltpu.SMEM((terms,), jnp.int32)] * 2

    def near(own, *args):
        outs = [shape(half * block, cols)]
        scratch = []
        if own:
            outs += [blocks, shape(terms, wide, cols)]
            outs += [jax.ShapeDtypeStruct(source_shape, BF16), shape(sector_count * block, cols)]
            scratch = [pltpu.SMEM((sector_count,), jnp.int32), pltpu.SemaphoreType.DMA((terms + 1,))]
        return pl.pallas_call(
            functools.partial(near_kernel, own),
            out_shape=tuple(outs),
            in_specs=[ANY] * 4 + [VMEM] * 2 if own else [ANY] + [VMEM] * 4,
            out_specs=(VMEM,) * len(outs),
            scratch_shapes=scratch
            + [pltpu.VMEM((half, 2 * GROUP * block, cols), BF16), pltpu.SMEM((terms,), jnp.int32)]
            + lists
            + [pltpu.SemaphoreType.DMA((2,))],
            compiler_params=params(OWN_VMEM if own else NEAR_VMEM),
            cost_estimate=cost(1, 1),
            name="own_near" if own else "pair_near",
        )(*args)

    def add_far(lo, count, far, acc, sums):
        rows = count * block
        extra = () if sums is None else (sums,)
        return pl.pallas_call(
            functools.partial(far_kernel, lo, shift, secs, sums is not None),
            out_shape=(shape(rows, cols), shape(16, 128)),
            in_specs=[ANY] * 3 + [VMEM] * (9 + len(extra)),
            out_specs=(VMEM, VMEM),
            scratch_shapes=[
                pltpu.VMEM((far[0].shape[0] * rows + block, 3 * wide), BF16),
                pltpu.VMEM((count, 2 * GROUP * block, cols), BF16),
                pltpu.SMEM((sector_count,), jnp.int32),
                pltpu.SMEM((2, terms), jnp.int32),
                *lists,
                pltpu.SemaphoreType.DMA((3,)),
            ],
            compiler_params=params(32),
            cost_estimate=cost(1, 1),
            name="far",
        )(term_charge, cls_pair, block_rows, left, right, left_pair, right_pair, live, *far, halo, acc, *extra)

    acc, left, right, src, live = near(
        True, term_charge, left_blocks, right_blocks, after(block_rows, mine_a), whole, wavefunction
    )
    far_b = far(mine_b)
    halo = lax.ppermute(after(halo, acc), ("sec", "mpo"), halo_pairs)
    other_a = swap(after(far_a, acc), "mpo", 2)
    (acc,) = near(False, cls_pair, left_pair, right_pair, src, acc)
    other_b = swap(after(far_b, acc), "mpo", 2)
    part_a, sums = add_far(0, sizes[0], (far_a, other_a), acc, None)
    recv_a = swap(part_a, "mpo", 2)
    part_b, sums = add_far(sizes[0], sizes[1], (far_b, other_b), acc, sums)
    recv_b = swap(part_b, "mpo", 2)

    if secs == 4:
        sums = everyone(sums, "sec")
    else:
        sums = lax.psum(sums, "sec")
    if reps > 1:
        sums = lax.psum(sums, "rep")
    sums = everyone(after(sums, recv_a), "mpo")
    totals = [part_a + recv_a, part_b + recv_b]
    totals += [swap(total, "mpo", 1) for total in totals]

    out = shape(sector_count * block, cols)
    return pl.pallas_call(
        functools.partial(final_kernel, mpos // 2),
        out_shape=(out, out),
        in_specs=[VMEM] * (2 + len(totals)),
        out_specs=(ANY, ANY),
        scratch_shapes=[
            pltpu.VMEM((sector_count * block, cols), F32),
            pltpu.SemaphoreType.DMA((2, len(totals))),
        ],
        compiler_params=params(32),
        cost_estimate=cost(1, 1),
        name="residual",
    )(sums, live, *totals)


def solution(mesh):
    in_specs = (
        P(("runs", "sec"), "rep"),
        P(("runs", "sec"), "mpo", None, None),
        P(("runs", "mpo"), None, "rep"),
        P(("runs", "sec")),
        P("mpo"),
    )
    out_specs = (P(("runs", "sec"), "rep"), P(("runs", "sec"), "rep"))
    return jax.shard_map(local, mesh=mesh, in_specs=in_specs, out_specs=out_specs, check_vma=False)
```

```python
import functools

import jax
import jax.numpy as jnp
from jax import lax
from jax.experimental import pallas as pl
from jax.experimental.pallas import tpu as pltpu
from jax.sharding import PartitionSpec as P

QD = 16
F32 = jnp.float32
BF16 = jnp.bfloat16
VMEM = pl.BlockSpec(memory_space=pltpu.VMEM)
SMEM = pl.BlockSpec(memory_space=pltpu.SMEM)
HBM = pl.BlockSpec(memory_space=pltpu.HBM)
ANY = pl.BlockSpec(memory_space=pl.ANY)


def split(x):
    high = x.astype(BF16)
    return high, (x - high.astype(F32)).astype(BF16)


def masked(rows, live):
    index = lax.broadcasted_iota(jnp.int32, rows.shape, 0)
    return jnp.where(index < live, rows, 0.0)


PREPARE_VMEM, CUT_VMEM, OWN_VMEM, NEAR_VMEM = 62, 50, 46, 32
GROUPS = (4, 2)


def place():
    mpo = lax.axis_index("mpo")
    return lax.rem(mpo, 2), lax.rem(lax.div(mpo, 2), 2), lax.axis_index("sec")


def sector_rows(wave, sector, block):
    return wave.at[pl.ds(pl.multiple_of(sector * block, block), block), :]


def prepare_kernel(half, rows_hbm, wave, *refs):
    *sends, halo, rows_ref, sem = refs
    core, side, _ = place()
    block = halo.shape[0]
    piece = block // 2
    rows = pltpu.make_async_copy(rows_hbm, rows_ref, sem.at[0])
    rows.start()
    wanted = [(halo, (1 - core) * (2 * half - 1) * block)]
    first = core * half * block
    for ref in sends:
        wanted.append((ref, first + side * ref.shape[0]))
        first += 2 * ref.shape[0]
    reads = []
    for i, (ref, first) in enumerate(wanted):
        source = wave.at[pl.ds(pl.multiple_of(first, piece), ref.shape[0]), :]
        reads.append(pltpu.make_async_copy(source, ref, sem.at[i + 1]))
        reads[i].start()
    rows.wait()
    for read, (ref, first) in zip(reads, wanted):
        read.wait()
        for at in range(0, ref.shape[0], piece):
            here = pl.ds(at, piece)
            live = rows_ref[lax.div(first + at, block)] - lax.rem(first + at, block)
            ref[here, :] = masked(ref[here, :], live)


def cut_kernel(half, left, left_send, sem):
    core, _, _ = place()
    move = pltpu.make_async_copy(left.at[pl.ds((1 - core) * half, half)], left_send, sem.at[0])
    move.start()
    move.wait()


def put(src, at, value):
    wide = value.shape[1]
    high, low = split(value)
    here = pl.ds(at, value.shape[0])
    src[here, 0:wide] = high
    src[here, wide : 2 * wide] = low
    src[here, 2 * wide : 3 * wide] = high


def pack(classes, choose, order, offsets):
    n = jnp.int32(0)
    for t, c in enumerate(classes):
        chosen, at = choose(c)

        @pl.when(chosen)
        def _(n=n, t=t, at=at):
            order[n] = t
            offsets[n] = at

        n = n + chosen.astype(jnp.int32)
    return n


def add_terms(n, order, offsets, src, right_of, left_of, acc, tbuf):
    rows = acc.shape[0]
    block = tbuf.shape[1] // (2 * max(GROUPS))
    count = rows // block

    def add(begin, group):
        terms, real = [], []
        for j in range(group):
            k = jnp.minimum(begin + j, n - 1)
            real.append(begin + j < n)
            terms.append(order[k])
            at = pl.ds(pl.multiple_of(offsets[k], block), rows)
            high, low = split(right_of(terms[j]))
            wide = jnp.concatenate([high, high, low], 0)
            high, low = split(jnp.dot(src[at, :], wide, preferred_element_type=F32))
            for s in range(count):
                here = slice(s * block, (s + 1) * block)
                tbuf[s, j * block : (j + 1) * block, :] = high[here]
                tbuf[s, (group + j) * block : (group + j + 1) * block, :] = low[here]
        for s in range(count):
            blocks = [left_of(s, terms[0])]
            for j in range(1, group):
                blocks.append(jnp.where(real[j], left_of(s, terms[j]), 0.0))
            high, low = split(jnp.concatenate(blocks, 1))
            acc[s * block : (s + 1) * block, :] += jnp.dot(
                jnp.concatenate([high, high, low], 1),
                jnp.concatenate([tbuf[s, 0 : 2 * group * block], tbuf[s, 0 : group * block]], 0),
                preferred_element_type=F32,
            )

    large, small = GROUPS
    full = lax.div(n + large - small - 1, large)

    @pl.loop(0, full)
    def _(i):
        add(i * large, large)

    @pl.when(n > full * large)
    def _():
        add(full * large, small)


def load_kernel(left_hbm, right_hbm, rows_hbm, whole, wave, left, right, src, live, rows_ref, sem):
    half, terms, block, _ = left.shape
    core, _, _ = place()
    rows = pltpu.make_async_copy(rows_hbm, rows_ref, sem.at[0])
    moves = [
        pltpu.make_async_copy(left_hbm.at[pl.ds(core * half, half)], left, sem.at[1]),
        pltpu.make_async_copy(right_hbm, right, sem.at[2]),
    ]
    for move in [rows] + moves:
        move.start()
    halo_at = pl.multiple_of(core * (half + 1) * block, block)
    src[pl.ds(halo_at, block), :] = jnp.zeros((block, src.shape[1]), BF16)
    rows.wait()
    for s in range(2 * half):
        here = pl.ds(s * block, block)
        live[here, :] = masked(wave[here, :], rows_ref[s])
    for i in range(half + 1):
        sector = core * (half - 1) + i
        value = masked(sector_rows(whole, sector, block)[...], rows_ref[sector])
        put(src, pl.multiple_of((i + 1 - core) * block, block), value)
    for move in moves:
        move.wait()


def near_kernel(chained, cls, left, right, src, *refs):
    acc_in, refs = (refs[0], refs[1:]) if chained else (None, refs)
    acc, tbuf, cls_ref, order, offsets, sem = refs
    block = left.shape[-1]
    fetch = pltpu.make_async_copy(cls, cls_ref, sem.at[0])
    fetch.start()
    acc[...] = acc_in[...] if chained else jnp.zeros_like(acc)
    fetch.wait()

    def near(c):
        at = jnp.where(c == 0, block, jnp.where(c == 3, 2 * block, 0))
        return jnp.logical_or(c == 0, c >= 3), at

    n = pack([cls_ref[t] for t in range(right.shape[0])], near, order, offsets)
    add_terms(n, order, offsets, src, lambda t: right[t], lambda s, t: left[s, t], acc, tbuf)


def far_kernel(lo, shift, secs, chained, *refs):
    refs = list(refs)
    cls, cls_pair, rows_hbm, left, right, left_pair, right_pair, live, mine, other, halo, acc_in = refs[:12]
    sums_in = refs.pop(12) if chained else None
    acc, sums, src, tbuf, rows_ref, cls_ref, order, offsets, sem = refs[12:]
    rows, cols = acc.shape
    half, terms, block, _ = left.shape
    count = rows // block
    core, side, sec = place()
    merged = mine.shape[0] == 1

    moves = [
        pltpu.make_async_copy(rows_hbm, rows_ref, sem.at[0]),
        pltpu.make_async_copy(cls, cls_ref.at[0], sem.at[1]),
        pltpu.make_async_copy(cls_pair, cls_ref.at[1], sem.at[2]),
    ]
    for move in moves:
        move.start()
    acc[...] = acc_in[pl.ds(lo * block, rows), :]
    for k in range(mine.shape[0]):
        for ref, x in ((mine, side), (other, 1 - side)):
            part = ref.shape[1]
            put(src, pl.multiple_of(k * rows + x * part, part), ref[k])
    halo_at = mine.shape[0] * rows
    put(src, halo_at, halo[...])
    for move in moves:
        move.wait()

    def far(c):
        above = jnp.logical_and(c == 1, sec + shift < secs)
        below = jnp.logical_and(c == 2, sec >= shift)
        return jnp.logical_or(above, below), jnp.where(c == 1, 0, 0 if merged else rows)

    def either(own, pair, t, *index):
        here = index + (lax.rem(t, terms),)
        return jnp.where(t < terms, own[here], pair[here])

    classes = [cls_ref[g, t] for g in range(2) for t in range(terms)]
    right_of = functools.partial(either, right, right_pair)
    n = pack(classes, far, order, offsets)
    left_of = lambda s, t: either(left, left_pair, t, lo + s)
    add_terms(n, order, offsets, src, right_of, left_of, acc, tbuf)
    n = pack(classes, lambda c: (c == 4 - core, halo_at), order, offsets)
    n = jnp.where(core == (0 if lo == 0 else 1), n, 0)
    edge = core * (count - 1)
    left_of = lambda s, t: either(left, left_pair, t, lo + edge)
    add_terms(n, order, offsets, src, right_of, left_of, acc.at[pl.ds(pl.multiple_of(edge * block, block), block), :], tbuf)

    cross = jnp.zeros((8, cols), F32)
    square = jnp.zeros((8, cols), F32)
    for s in range(count):
        sector = core * half + lo + s
        here = pl.ds(s * block, block)
        total = masked(acc[here, :], rows_ref[sector])
        acc[here, :] = total
        value = sector_rows(live, sector, block)[...]
        fold = lambda v: jnp.sum(v.reshape(block // 8, 8, cols), axis=0)
        cross += fold(value * total)
        square += fold(value * value)
    fold = lambda v: sum(v[:, i : i + 128] for i in range(0, cols, 128))
    cross, square = fold(cross), fold(square)
    if chained:
        cross, square = cross + sums_in[0:8, :], square + sums_in[8:16, :]
    sums[0:8, :] = cross
    sums[8:16, :] = square


def final_kernel(sides, live, total, total_pair, applied, correction, buf, sem):
    core, _, _ = place()
    rows = live.shape[0] // 2
    pieces = sem.shape[1] // 2
    piece = rows // pieces
    moves = []

    def send(source, target, kind, i):
        moves.append(pltpu.make_async_copy(source, target, sem.at[kind, i]))
        moves[-1].start()

    for i, (ref, c) in enumerate(((total, core), (total_pair, 1 - core))):
        here = pl.ds(pl.multiple_of(c * rows, rows), rows)
        send(ref.at[pl.ds(0, rows), :], applied.at[here, :], 0, i)
    sums = total[rows : rows + 16, 0:128] + total_pair[rows : rows + 16, 0:128]
    rayleigh = jnp.sum(sums[0:8, :]) / (jnp.sum(sums[8:16, :]) * (1.0 / sides))
    for i, (ref, c) in enumerate(((total, core), (total_pair, 1 - core))):
        for p in range(pieces):
            here = pl.ds(pl.multiple_of(c * rows + p * piece, piece), piece)
            buf[here, :] = ref[pl.ds(p * piece, piece), :] - rayleigh * live[here, :]
            send(buf.at[here, :], correction.at[here, :], 1, i * pieces + p)
    for move in moves:
        move.wait()


def params(limit):
    return pltpu.CompilerParams(vmem_limit_bytes=limit * 2**20)


def cost(flops, moved):
    return pl.CostEstimate(flops=int(flops), bytes_accessed=int(moved), transcendentals=0)


def shape(*dims):
    return jax.ShapeDtypeStruct(dims, F32)


def swap(array, axis, bit):
    pairs = [(i, i ^ bit) for i in range(lax.axis_size(axis))]
    return lax.ppermute(array, axis, pairs)


def spread_sum(sums):
    sums = sums + swap(sums, "mpo", 1)
    parts = []
    for bit in range(4):
        pairs = [(4 * z + m, 4 * (z ^ bit) + (m ^ 2 if m % 2 else m)) for z in range(4) for m in range(4)]
        parts.append(lax.ppermute(sums, ("sec", "mpo"), [p for p in pairs if p[0] != p[1]]))
    parts[0] = jnp.where(lax.axis_index("mpo") % 2 == 0, sums, parts[0])
    return (parts[0] + parts[1]) + (parts[2] + parts[3])


def after(array, *others):
    return lax.optimization_barrier((array, *others))[0]


def local(wavefunction, left_blocks, right_blocks, block_rows, term_charge):
    sector_count = block_rows.shape[0]
    block = left_blocks.shape[2]
    terms = left_blocks.shape[1]
    cols = wavefunction.shape[1]
    secs, mpos, reps = (lax.axis_size(a) for a in ("sec", "mpo", "rep"))
    half = sector_count // 2
    part = half // 2
    shift = QD // sector_count
    merged = secs <= 2 * shift
    whole = wavefunction
    if reps > 1:
        whole = lax.all_gather(wavefunction, "rep", axis=1, tiled=True)
    wide = whole.shape[1]

    up = [(i, i - shift) for i in range(shift, secs)]
    down = [(i, i + shift) for i in range(secs - shift)]

    def far(array):
        if merged:
            return lax.ppermute(array, "sec", up + down)[None]
        return jnp.stack([lax.ppermute(array, "sec", p) for p in (up, down)])

    halo_pairs = []
    for m in range(mpos):
        for z in range(secs):
            to = z + 1 if m % 2 == 0 else z - 1
            if 0 <= to < secs:
                halo_pairs.append((z * mpos + m, to * mpos + m))

    blocks = shape(half, terms, block, block)
    source_shape = ((half + 2) * block, 3 * wide)
    sizes = (half // 2, half // 2)
    cls_pair = swap(term_charge, "mpo", 1)
    mine_a, mine_b, halo = pl.pallas_call(
        functools.partial(prepare_kernel, half),
        out_shape=tuple(shape(size * block // 2, wide) for size in sizes) + (shape(block, wide),),
        in_specs=[ANY] * 2,
        out_specs=(VMEM,) * 3,
        scratch_shapes=[pltpu.SMEM((sector_count,), jnp.int32), pltpu.SemaphoreType.DMA((4,))],
        compiler_params=params(PREPARE_VMEM),
        cost_estimate=cost(1, 1),
        name="prepare",
    )(block_rows, whole)
    (left_send,) = pl.pallas_call(
        functools.partial(cut_kernel, half),
        out_shape=(blocks,),
        in_specs=[ANY],
        out_specs=(VMEM,),
        scratch_shapes=[pltpu.SemaphoreType.DMA((1,))],
        compiler_params=params(CUT_VMEM),
        cost_estimate=cost(1, 1),
        name="pair_blocks",
    )(after(left_blocks, mine_a, cls_pair))
    left_pair = swap(left_send, "mpo", 1)
    far_a = far(mine_a)
    right_pair = swap(after(right_blocks, mine_a), "mpo", 1)

    lists = [pltpu.SMEM((2 * terms,), jnp.int32)] * 2

    def near(name, *args):
        chained = len(args) == 5
        return pl.pallas_call(
            functools.partial(near_kernel, chained),
            out_shape=shape(half * block, cols),
            in_specs=[ANY] + [VMEM] * (len(args) - 1),
            out_specs=VMEM,
            scratch_shapes=[pltpu.VMEM((half, 2 * GROUPS[0] * block, cols), BF16), pltpu.SMEM((terms,), jnp.int32)]
            + lists
            + [pltpu.SemaphoreType.DMA((1,))],
            compiler_params=params(NEAR_VMEM),
            cost_estimate=cost(1, 1),
            name=name,
        )(*args)

    def add_far(lo, count, far, acc, sums):
        rows = count * block
        extra = () if sums is None else (sums,)
        return pl.pallas_call(
            functools.partial(far_kernel, lo, shift, secs, sums is not None),
            out_shape=(shape(rows, cols), shape(16, 128)),
            in_specs=[ANY] * 3 + [VMEM] * (9 + len(extra)),
            out_specs=(VMEM, VMEM),
            scratch_shapes=[
                pltpu.VMEM((far[0].shape[0] * rows + block, 3 * wide), BF16),
                pltpu.VMEM((count, 2 * GROUPS[0] * block, cols), BF16),
                pltpu.SMEM((sector_count,), jnp.int32),
                pltpu.SMEM((2, terms), jnp.int32),
                *lists,
                pltpu.SemaphoreType.DMA((3,)),
            ],
            compiler_params=params(32),
            cost_estimate=cost(1, 1),
            name="far",
        )(term_charge, cls_pair, block_rows, left, right, left_pair, right_pair, live, *far, halo, acc, *extra)

    left, right, src, live = pl.pallas_call(
        load_kernel,
        out_shape=(
            blocks,
            shape(terms, wide, cols),
            jax.ShapeDtypeStruct(source_shape, BF16),
            shape(sector_count * block, cols),
        ),
        in_specs=[ANY] * 3 + [VMEM] * 2,
        out_specs=(VMEM,) * 4,
        scratch_shapes=[pltpu.SMEM((sector_count,), jnp.int32), pltpu.SemaphoreType.DMA((3,))],
        compiler_params=params(OWN_VMEM),
        cost_estimate=cost(1, 1),
        name="own_terms",
    )(left_blocks, right_blocks, after(block_rows, mine_a), whole, wavefunction)
    far_b = far(after(mine_b, src))
    acc = near("own_near", term_charge, left, right, src)
    halo = lax.ppermute(after(halo, acc), ("sec", "mpo"), halo_pairs)
    other_a = swap(after(far_a, acc), "mpo", 2)
    acc = near("pair_near", cls_pair, left_pair, right_pair, src, acc)
    other_b = swap(after(far_b, acc), "mpo", 2)
    part_a, sums = add_far(0, sizes[0], (far_a, other_a), acc, None)
    recv_a = swap(part_a, "mpo", 2)
    part_b, sums = add_far(sizes[0], sizes[1], (far_b, other_b), acc, sums)
    recv_b = swap(part_b, "mpo", 2)

    if secs == 4 and mpos == 4 and reps == 1:
        sums = spread_sum(sums)
    else:
        sums = lax.psum(sums, ("sec", "rep"))
        sums = sums + swap(sums, "mpo", 2)
    sums = jnp.pad(sums, ((0, 0), (0, cols - sums.shape[1])))
    total = jnp.concatenate([part_a + recv_a, part_b + after(recv_b, sums), sums])
    total_pair = swap(total, "mpo", 1)

    out = shape(sector_count * block, cols)
    return pl.pallas_call(
        functools.partial(final_kernel, mpos // 2),
        out_shape=(out, out),
        in_specs=[VMEM] * 3,
        out_specs=(ANY, ANY),
        scratch_shapes=[pltpu.VMEM((sector_count * block, cols), F32), pltpu.SemaphoreType.DMA((2, 4))],
        compiler_params=params(32),
        cost_estimate=cost(1, 1),
        name="residual",
    )(live, total, total_pair)


def solution(mesh):
    in_specs = (
        P(("runs", "sec"), "rep"),
        P(("runs", "sec"), "mpo", None, None),
        P(("runs", "mpo"), None, "rep"),
        P(("runs", "sec")),
        P("mpo"),
    )
    out_specs = (P(("runs", "sec"), "rep"), P(("runs", "sec"), "rep"))
    return jax.shard_map(local, mesh=mesh, in_specs=in_specs, out_specs=out_specs, check_vma=False)
```

```python
import functools

import jax
import jax.numpy as jnp
from jax import lax
from jax.experimental import pallas as pl
from jax.experimental.pallas import tpu as pltpu
from jax.sharding import PartitionSpec as P

QD = 16
F32 = jnp.float32
BF16 = jnp.bfloat16
VMEM = pl.BlockSpec(memory_space=pltpu.VMEM)
SMEM = pl.BlockSpec(memory_space=pltpu.SMEM)
HBM = pl.BlockSpec(memory_space=pltpu.HBM)
ANY = pl.BlockSpec(memory_space=pl.ANY)


def split(x):
    high = x.astype(BF16)
    return high, (x - high.astype(F32)).astype(BF16)


def masked(rows, live):
    index = lax.broadcasted_iota(jnp.int32, rows.shape, 0)
    return jnp.where(index < live, rows, 0.0)


PREPARE_VMEM, CUT_VMEM, OWN_VMEM, NEAR_VMEM = 62, 50, 46, 32
GROUPS = (4, 2)


def place():
    mpo = lax.axis_index("mpo")
    return lax.rem(mpo, 2), lax.rem(lax.div(mpo, 2), 2), lax.axis_index("sec")


def chunk_start(chunk, core, half):
    return (1 - core if chunk else core) * (half // 2)


def sector_rows(wave, sector, block):
    return wave.at[pl.ds(pl.multiple_of(sector * block, block), block), :]


def prepare_kernel(half, rows_hbm, wave, *refs):
    *sends, halo, rows_ref, sem = refs
    core, side, _ = place()
    block = halo.shape[0]
    piece = block // 2
    rows = pltpu.make_async_copy(rows_hbm, rows_ref, sem.at[0])
    rows.start()
    wanted = [(halo, (1 - core) * (2 * half - 1) * block)]
    for i, ref in enumerate(sends):
        wanted.append((ref, (core * half + chunk_start(i, core, half)) * block + side * ref.shape[0]))
    reads = []
    for i, (ref, first) in enumerate(wanted):
        source = wave.at[pl.ds(pl.multiple_of(first, piece), ref.shape[0]), :]
        reads.append(pltpu.make_async_copy(source, ref, sem.at[i + 1]))
        reads[i].start()
    rows.wait()
    for read, (ref, first) in zip(reads, wanted):
        read.wait()
        for at in range(0, ref.shape[0], piece):
            here = pl.ds(at, piece)
            live = rows_ref[lax.div(first + at, block)] - lax.rem(first + at, block)
            ref[here, :] = masked(ref[here, :], live)


def cut_kernel(half, left, left_send, sem):
    core, _, _ = place()
    move = pltpu.make_async_copy(left.at[pl.ds((1 - core) * half, half)], left_send, sem.at[0])
    move.start()
    move.wait()


def put(src, at, value):
    wide = value.shape[1]
    high, low = split(value)
    here = pl.ds(at, value.shape[0])
    src[here, 0:wide] = high
    src[here, wide : 2 * wide] = low
    src[here, 2 * wide : 3 * wide] = high


def pack(classes, choose, order, offsets):
    n = jnp.int32(0)
    for t, c in enumerate(classes):
        chosen, at = choose(c)

        @pl.when(chosen)
        def _(n=n, t=t, at=at):
            order[n] = t
            offsets[n] = at

        n = n + chosen.astype(jnp.int32)
    return n


def add_terms(n, order, offsets, src, right_of, left_of, acc, tbuf):
    rows = acc.shape[0]
    block = tbuf.shape[1] // (2 * max(GROUPS))
    count = rows // block

    def add(begin, group):
        terms, real = [], []
        for j in range(group):
            k = jnp.minimum(begin + j, n - 1)
            real.append(begin + j < n)
            terms.append(order[k])
            at = pl.ds(pl.multiple_of(offsets[k], block), rows)
            high, low = split(right_of(terms[j]))
            wide = jnp.concatenate([high, high, low], 0)
            high, low = split(jnp.dot(src[at, :], wide, preferred_element_type=F32))
            for s in range(count):
                here = slice(s * block, (s + 1) * block)
                tbuf[s, j * block : (j + 1) * block, :] = high[here]
                tbuf[s, (group + j) * block : (group + j + 1) * block, :] = low[here]
        for s in range(count):
            blocks = [left_of(s, terms[0])]
            for j in range(1, group):
                blocks.append(jnp.where(real[j], left_of(s, terms[j]), 0.0))
            high, low = split(jnp.concatenate(blocks, 1))
            acc[s * block : (s + 1) * block, :] += jnp.dot(
                jnp.concatenate([high, high, low], 1),
                jnp.concatenate([tbuf[s, 0 : 2 * group * block], tbuf[s, 0 : group * block]], 0),
                preferred_element_type=F32,
            )

    large, small = GROUPS
    full = lax.div(n + large - small - 1, large)

    @pl.loop(0, full)
    def _(i):
        add(i * large, large)

    @pl.when(n > full * large)
    def _():
        add(full * large, small)


def load_kernel(left_hbm, right_hbm, rows_hbm, whole, wave, left, right, src, live, rows_ref, sem):
    half, terms, block, _ = left.shape
    core, _, _ = place()
    rows = pltpu.make_async_copy(rows_hbm, rows_ref, sem.at[0])
    moves = [
        pltpu.make_async_copy(left_hbm.at[pl.ds(core * half, half)], left, sem.at[1]),
        pltpu.make_async_copy(right_hbm, right, sem.at[2]),
    ]
    for move in [rows] + moves:
        move.start()
    halo_at = pl.multiple_of(core * (half + 1) * block, block)
    src[pl.ds(halo_at, block), :] = jnp.zeros((block, src.shape[1]), BF16)
    rows.wait()
    for s in range(2 * half):
        here = pl.ds(s * block, block)
        live[here, :] = masked(wave[here, :], rows_ref[s])
    for i in range(half + 1):
        sector = core * (half - 1) + i
        value = masked(sector_rows(whole, sector, block)[...], rows_ref[sector])
        put(src, pl.multiple_of((i + 1 - core) * block, block), value)
    for move in moves:
        move.wait()


def near_kernel(chained, cls, left, right, src, *refs):
    acc_in, refs = (refs[0], refs[1:]) if chained else (None, refs)
    acc, tbuf, cls_ref, order, offsets, sem = refs
    block = left.shape[-1]
    fetch = pltpu.make_async_copy(cls, cls_ref, sem.at[0])
    fetch.start()
    acc[...] = acc_in[...] if chained else jnp.zeros_like(acc)
    fetch.wait()

    def near(c):
        at = jnp.where(c == 0, block, jnp.where(c == 3, 2 * block, 0))
        return jnp.logical_or(c == 0, c >= 3), at

    n = pack([cls_ref[t] for t in range(right.shape[0])], near, order, offsets)
    add_terms(n, order, offsets, src, lambda t: right[t], lambda s, t: left[s, t], acc, tbuf)


def far_kernel(chunk, shift, secs, *refs):
    refs = list(refs)
    cls, cls_pair, rows_hbm, left, right, left_pair, right_pair, live, mine, other, acc_in = refs[:11]
    halo, sums_in = (None, refs.pop(11)) if chunk else (refs.pop(11), None)
    acc, sums, src, tbuf, rows_ref, cls_ref, order, offsets, sem = refs[11:]
    rows, cols = acc.shape
    half, terms, block, _ = left.shape
    count = rows // block
    core, side, sec = place()
    lo = chunk_start(chunk, core, half)
    merged = mine.shape[0] == 1

    moves = [
        pltpu.make_async_copy(rows_hbm, rows_ref, sem.at[0]),
        pltpu.make_async_copy(cls, cls_ref.at[0], sem.at[1]),
        pltpu.make_async_copy(cls_pair, cls_ref.at[1], sem.at[2]),
    ]
    for move in moves:
        move.start()
    acc[...] = acc_in[pl.ds(pl.multiple_of(lo * block, block), rows), :]
    for k in range(mine.shape[0]):
        for ref, x in ((mine, side), (other, 1 - side)):
            part = ref.shape[1]
            put(src, pl.multiple_of(k * rows + x * part, part), ref[k])
    halo_at = mine.shape[0] * rows
    if not chunk:
        put(src, halo_at, halo[...])
    for move in moves:
        move.wait()

    def far(c):
        above = jnp.logical_and(c == 1, sec + shift < secs)
        below = jnp.logical_and(c == 2, sec >= shift)
        return jnp.logical_or(above, below), jnp.where(c == 1, 0, 0 if merged else rows)

    def either(own, pair, t, *index):
        here = index + (lax.rem(t, terms),)
        return jnp.where(t < terms, own[here], pair[here])

    classes = [cls_ref[g, t] for g in range(2) for t in range(terms)]
    right_of = functools.partial(either, right, right_pair)
    n = pack(classes, far, order, offsets)
    left_of = lambda s, t: either(left, left_pair, t, lo + s)
    add_terms(n, order, offsets, src, right_of, left_of, acc, tbuf)
    if not chunk:
        n = pack(classes, lambda c: (c == 4 - core, halo_at), order, offsets)
        edge = core * (count - 1)
        left_of = lambda s, t: either(left, left_pair, t, lo + edge)
        edge_rows = acc.at[pl.ds(pl.multiple_of(edge * block, block), block), :]
        add_terms(n, order, offsets, src, right_of, left_of, edge_rows, tbuf)

    cross = jnp.zeros((8, cols), F32)
    square = jnp.zeros((8, cols), F32)
    for s in range(count):
        sector = core * half + lo + s
        here = pl.ds(s * block, block)
        total = masked(acc[here, :], rows_ref[sector])
        acc[here, :] = total
        value = sector_rows(live, sector, block)[...]
        fold = lambda v: jnp.sum(v.reshape(block // 8, 8, cols), axis=0)
        cross += fold(value * total)
        square += fold(value * value)
    fold = lambda v: sum(v[:, i : i + 128] for i in range(0, cols, 128))
    cross, square = fold(cross), fold(square)
    if chunk:
        cross, square = cross + sums_in[0:8, :], square + sums_in[8:16, :]
    sums[0:8, :] = cross
    sums[8:16, :] = square


def final_kernel(sides, half, live, total, total_pair, applied, correction, buf, sem):
    core, _, _ = place()
    rows = live.shape[0] // 2
    block = rows // half
    part = rows // 2
    moves = []
    places = []

    def send(source, target, kind, i):
        moves.append(pltpu.make_async_copy(source, target, sem.at[kind, i]))
        moves[-1].start()

    for ref, c in ((total, core), (total_pair, 1 - core)):
        for chunk in range(2):
            first = (c * half + chunk_start(chunk, c, half)) * block
            here = pl.ds(pl.multiple_of(first, block), part)
            source = ref.at[pl.ds(chunk * part, part), :]
            places.append((source, here))
            send(source, applied.at[here, :], 0, len(places) - 1)
    sums = total[rows : rows + 16, 0:128] + total_pair[rows : rows + 16, 0:128]
    rayleigh = jnp.sum(sums[0:8, :]) / (jnp.sum(sums[8:16, :]) * (1.0 / sides))
    for i, (source, here) in enumerate(places):
        buf[here, :] = source[...] - rayleigh * live[here, :]
        send(buf.at[here, :], correction.at[here, :], 1, i)
    for move in moves:
        move.wait()


def params(limit):
    return pltpu.CompilerParams(vmem_limit_bytes=limit * 2**20)


def cost(flops, moved):
    return pl.CostEstimate(flops=int(flops), bytes_accessed=int(moved), transcendentals=0)


def shape(*dims):
    return jax.ShapeDtypeStruct(dims, F32)


def swap(array, axis, bit):
    pairs = [(i, i ^ bit) for i in range(lax.axis_size(axis))]
    return lax.ppermute(array, axis, pairs)


def spread_sum(sums):
    sums = sums + swap(sums, "mpo", 1)
    parts = []
    for bit in range(4):
        pairs = [(4 * z + m, 4 * (z ^ bit) + (m ^ 2 if m % 2 else m)) for z in range(4) for m in range(4)]
        parts.append(lax.ppermute(sums, ("sec", "mpo"), [p for p in pairs if p[0] != p[1]]))
    parts[0] = jnp.where(lax.axis_index("mpo") % 2 == 0, sums, parts[0])
    return (parts[0] + parts[1]) + (parts[2] + parts[3])


def after(array, *others):
    return lax.optimization_barrier((array, *others))[0]


def local(wavefunction, left_blocks, right_blocks, block_rows, term_charge):
    sector_count = block_rows.shape[0]
    block = left_blocks.shape[2]
    terms = left_blocks.shape[1]
    cols = wavefunction.shape[1]
    secs, mpos, reps = (lax.axis_size(a) for a in ("sec", "mpo", "rep"))
    half = sector_count // 2
    part = half // 2
    shift = QD // sector_count
    merged = secs <= 2 * shift
    whole = wavefunction
    if reps > 1:
        whole = lax.all_gather(wavefunction, "rep", axis=1, tiled=True)
    wide = whole.shape[1]

    up = [(i, i - shift) for i in range(shift, secs)]
    down = [(i, i + shift) for i in range(secs - shift)]

    def far(array):
        if merged:
            return lax.ppermute(array, "sec", up + down)[None]
        return jnp.stack([lax.ppermute(array, "sec", p) for p in (up, down)])

    halo_pairs = []
    for m in range(mpos):
        for z in range(secs):
            to = z + 1 if m % 2 == 0 else z - 1
            if 0 <= to < secs:
                halo_pairs.append((z * mpos + m, to * mpos + m))

    blocks = shape(half, terms, block, block)
    source_shape = ((half + 2) * block, 3 * wide)
    cls_pair = swap(term_charge, "mpo", 1)
    mine_a, mine_b, halo = pl.pallas_call(
        functools.partial(prepare_kernel, half),
        out_shape=(shape(part * block // 2, wide),) * 2 + (shape(block, wide),),
        in_specs=[ANY] * 2,
        out_specs=(VMEM,) * 3,
        scratch_shapes=[pltpu.SMEM((sector_count,), jnp.int32), pltpu.SemaphoreType.DMA((4,))],
        compiler_params=params(PREPARE_VMEM),
        cost_estimate=cost(1, 1),
        name="prepare",
    )(block_rows, whole)
    (left_send,) = pl.pallas_call(
        functools.partial(cut_kernel, half),
        out_shape=(blocks,),
        in_specs=[ANY],
        out_specs=(VMEM,),
        scratch_shapes=[pltpu.SemaphoreType.DMA((1,))],
        compiler_params=params(CUT_VMEM),
        cost_estimate=cost(1, 1),
        name="pair_blocks",
    )(after(left_blocks, mine_a, cls_pair))
    left_pair = swap(left_send, "mpo", 1)
    far_a = far(mine_a)
    right_pair = swap(after(right_blocks, left_send), "mpo", 1)

    lists = [pltpu.SMEM((2 * terms,), jnp.int32)] * 2

    def near(name, *args):
        chained = len(args) == 5
        return pl.pallas_call(
            functools.partial(near_kernel, chained),
            out_shape=shape(half * block, cols),
            in_specs=[ANY] + [VMEM] * (len(args) - 1),
            out_specs=VMEM,
            scratch_shapes=[pltpu.VMEM((half, 2 * GROUPS[0] * block, cols), BF16), pltpu.SMEM((terms,), jnp.int32)]
            + lists
            + [pltpu.SemaphoreType.DMA((1,))],
            compiler_params=params(NEAR_VMEM),
            cost_estimate=cost(1, 1),
            name=name,
        )(*args)

    def add_far(chunk, *args):
        rows = part * block
        return pl.pallas_call(
            functools.partial(far_kernel, chunk, shift, secs),
            out_shape=(shape(rows, cols), shape(16, 128)),
            in_specs=[ANY] * 3 + [VMEM] * (5 + len(args)),
            out_specs=(VMEM, VMEM),
            scratch_shapes=[
                pltpu.VMEM(((1 if merged else 2) * rows + block, 3 * wide), BF16),
                pltpu.VMEM((part, 2 * GROUPS[0] * block, cols), BF16),
                pltpu.SMEM((sector_count,), jnp.int32),
                pltpu.SMEM((2, terms), jnp.int32),
                *lists,
                pltpu.SemaphoreType.DMA((3,)),
            ],
            compiler_params=params(NEAR_VMEM),
            cost_estimate=cost(1, 1),
            name="far",
        )(term_charge, cls_pair, block_rows, left, right, left_pair, right_pair, live, *args)

    left, right, src, live = pl.pallas_call(
        load_kernel,
        out_shape=(
            blocks,
            shape(terms, wide, cols),
            jax.ShapeDtypeStruct(source_shape, BF16),
            shape(sector_count * block, cols),
        ),
        in_specs=[ANY] * 3 + [VMEM] * 2,
        out_specs=(VMEM,) * 4,
        scratch_shapes=[pltpu.SMEM((sector_count,), jnp.int32), pltpu.SemaphoreType.DMA((3,))],
        compiler_params=params(OWN_VMEM),
        cost_estimate=cost(1, 1),
        name="own_terms",
    )(left_blocks, right_blocks, after(block_rows, mine_a), whole, wavefunction)
    far_b = far(after(mine_b, src))
    acc = near("own_near", term_charge, left, right, src)
    halo = lax.ppermute(after(halo, acc), ("sec", "mpo"), halo_pairs)
    other_a = swap(after(far_a, acc), "mpo", 2)
    acc = near("pair_near", cls_pair, left_pair, right_pair, src, acc)
    other_b = swap(after(far_b, acc), "mpo", 2)
    part_a, sums = add_far(0, far_a, other_a, acc, halo)
    recv_a = swap(part_a, "mpo", 2)
    part_b, sums = add_far(1, far_b, other_b, acc, sums)
    recv_b = swap(part_b, "mpo", 2)

    if secs == 4 and mpos == 4 and reps == 1:
        sums = spread_sum(sums)
    else:
        sums = lax.psum(sums, ("sec", "rep"))
        sums = sums + swap(sums, "mpo", 2)
    sums = jnp.pad(sums, ((0, 0), (0, cols - sums.shape[1])))
    total = jnp.concatenate([part_a + recv_a, part_b + after(recv_b, sums), sums])
    total_pair = swap(total, "mpo", 1)

    out = shape(sector_count * block, cols)
    return pl.pallas_call(
        functools.partial(final_kernel, mpos // 2, half),
        out_shape=(out, out),
        in_specs=[VMEM] * 3,
        out_specs=(ANY, ANY),
        scratch_shapes=[pltpu.VMEM((sector_count * block, cols), F32), pltpu.SemaphoreType.DMA((2, 4))],
        compiler_params=params(32),
        cost_estimate=cost(1, 1),
        name="residual",
    )(live, total, total_pair)


def solution(mesh):
    in_specs = (
        P(("runs", "sec"), "rep"),
        P(("runs", "sec"), "mpo", None, None),
        P(("runs", "mpo"), None, "rep"),
        P(("runs", "sec")),
        P("mpo"),
    )
    out_specs = (P(("runs", "sec"), "rep"), P(("runs", "sec"), "rep"))
    return jax.shard_map(local, mesh=mesh, in_specs=in_specs, out_specs=out_specs, check_vma=False)
```

```python
import functools

import jax
import jax.numpy as jnp
from jax import lax
from jax.experimental import pallas as pl
from jax.experimental.pallas import tpu as pltpu
from jax.sharding import PartitionSpec as P

QD = 16
F32 = jnp.float32
BF16 = jnp.bfloat16
VMEM = pl.BlockSpec(memory_space=pltpu.VMEM)
SMEM = pl.BlockSpec(memory_space=pltpu.SMEM)
HBM = pl.BlockSpec(memory_space=pltpu.HBM)
ANY = pl.BlockSpec(memory_space=pl.ANY)


def split(x):
    high = x.astype(BF16)
    return high, (x - high.astype(F32)).astype(BF16)


def masked(rows, live):
    index = lax.broadcasted_iota(jnp.int32, rows.shape, 0)
    return jnp.where(index < live, rows, 0.0)


PREPARE_VMEM, CUT_VMEM, OWN_VMEM, NEAR_VMEM = 62, 50, 46, 32
GROUPS = (4, 2)


def place():
    mpo = lax.axis_index("mpo")
    return lax.rem(mpo, 2), lax.rem(lax.div(mpo, 2), 2), lax.axis_index("sec")


def chunk_start(chunk, core, half):
    return (1 - core if chunk else core) * (half // 2)


def sector_rows(wave, sector, block):
    return wave.at[pl.ds(pl.multiple_of(sector * block, block), block), :]


def prepare_kernel(half, rows_hbm, wave, *refs):
    *sends, halo, rows_ref, sem = refs
    core, side, _ = place()
    block = halo.shape[0]
    piece = block // 2
    rows = pltpu.make_async_copy(rows_hbm, rows_ref, sem.at[0])
    rows.start()
    wanted = [(halo, (1 - core) * (2 * half - 1) * block)]
    for i, ref in enumerate(sends):
        wanted.append((ref, (core * half + chunk_start(i, core, half)) * block + side * ref.shape[0]))
    reads = []
    for i, (ref, first) in enumerate(wanted):
        source = wave.at[pl.ds(pl.multiple_of(first, piece), ref.shape[0]), :]
        reads.append(pltpu.make_async_copy(source, ref, sem.at[i + 1]))
        reads[i].start()
    rows.wait()
    for read, (ref, first) in zip(reads, wanted):
        read.wait()
        for at in range(0, ref.shape[0], piece):
            here = pl.ds(at, piece)
            live = rows_ref[lax.div(first + at, block)] - lax.rem(first + at, block)
            ref[here, :] = masked(ref[here, :], live)


def cut_kernel(half, left, left_send, sem):
    core, _, _ = place()
    move = pltpu.make_async_copy(left.at[pl.ds((1 - core) * half, half)], left_send, sem.at[0])
    move.start()
    move.wait()


def put(src, at, value):
    wide = value.shape[1]
    high, low = split(value)
    here = pl.ds(at, value.shape[0])
    src[here, 0:wide] = high
    src[here, wide : 2 * wide] = low
    src[here, 2 * wide : 3 * wide] = high


def pack(classes, choose, order, offsets):
    n = jnp.int32(0)
    for t, c in enumerate(classes):
        chosen, at = choose(c)

        @pl.when(chosen)
        def _(n=n, t=t, at=at):
            order[n] = t
            offsets[n] = at

        n = n + chosen.astype(jnp.int32)
    return n


def add_terms(n, order, offsets, src, right_of, left_of, acc, tbuf):
    rows = acc.shape[0]
    block = tbuf.shape[1] // (2 * max(GROUPS))
    count = rows // block

    def add(begin, group):
        terms, real = [], []
        for j in range(group):
            k = jnp.minimum(begin + j, n - 1)
            real.append(begin + j < n)
            terms.append(order[k])
            at = pl.ds(pl.multiple_of(offsets[k], block), rows)
            high, low = split(right_of(terms[j]))
            wide = jnp.concatenate([high, high, low], 0)
            high, low = split(jnp.dot(src[at, :], wide, preferred_element_type=F32))
            for s in range(count):
                here = slice(s * block, (s + 1) * block)
                tbuf[s, j * block : (j + 1) * block, :] = high[here]
                tbuf[s, (group + j) * block : (group + j + 1) * block, :] = low[here]
        for s in range(count):
            blocks = [left_of(s, terms[0])]
            for j in range(1, group):
                blocks.append(jnp.where(real[j], left_of(s, terms[j]), 0.0))
            high, low = split(jnp.concatenate(blocks, 1))
            acc[s * block : (s + 1) * block, :] += jnp.dot(
                jnp.concatenate([high, high, low], 1),
                jnp.concatenate([tbuf[s, 0 : 2 * group * block], tbuf[s, 0 : group * block]], 0),
                preferred_element_type=F32,
            )

    large, small = GROUPS
    full = lax.div(n + large - small - 1, large)

    @pl.loop(0, full)
    def _(i):
        add(i * large, large)

    @pl.when(n > full * large)
    def _():
        add(full * large, small)


def load_kernel(left_hbm, right_hbm, rows_hbm, whole, wave, left, right, src, live, rows_ref, sem):
    half, terms, block, _ = left.shape
    core, _, _ = place()
    rows = pltpu.make_async_copy(rows_hbm, rows_ref, sem.at[0])
    moves = [
        pltpu.make_async_copy(left_hbm.at[pl.ds(core * half, half)], left, sem.at[1]),
        pltpu.make_async_copy(right_hbm, right, sem.at[2]),
    ]
    for move in [rows] + moves:
        move.start()
    halo_at = pl.multiple_of(core * (half + 1) * block, block)
    src[pl.ds(halo_at, block), :] = jnp.zeros((block, src.shape[1]), BF16)
    rows.wait()
    for s in range(2 * half):
        here = pl.ds(s * block, block)
        live[here, :] = masked(wave[here, :], rows_ref[s])
    for i in range(half + 1):
        sector = core * (half - 1) + i
        value = masked(sector_rows(whole, sector, block)[...], rows_ref[sector])
        put(src, pl.multiple_of((i + 1 - core) * block, block), value)
    for move in moves:
        move.wait()


def near_kernel(chained, cls, left, right, src, *refs):
    acc_in, refs = (refs[0], refs[1:]) if chained else (None, refs)
    acc, tbuf, cls_ref, order, offsets, sem = refs
    block = left.shape[-1]
    fetch = pltpu.make_async_copy(cls, cls_ref, sem.at[0])
    fetch.start()
    acc[...] = acc_in[...] if chained else jnp.zeros_like(acc)
    fetch.wait()

    def near(c):
        at = jnp.where(c == 0, block, jnp.where(c == 3, 2 * block, 0))
        return jnp.logical_or(c == 0, c >= 3), at

    n = pack([cls_ref[t] for t in range(right.shape[0])], near, order, offsets)
    add_terms(n, order, offsets, src, lambda t: right[t], lambda s, t: left[s, t], acc, tbuf)


def far_kernel(chunk, shift, secs, *refs):
    refs = list(refs)
    cls, cls_pair, rows_hbm, left, right, left_pair, right_pair, live, mine, other, acc_in = refs[:11]
    halo, sums_in = (None, refs.pop(11)) if chunk else (refs.pop(11), None)
    acc, sums, src, tbuf, rows_ref, cls_ref, order, offsets, sem = refs[11:]
    cols = acc.shape[1]
    half, terms, block, _ = left.shape
    rows = half // 2 * block
    whole, acc = acc, acc.at[pl.ds(0, rows), :]
    count = rows // block
    core, side, sec = place()
    lo = chunk_start(chunk, core, half)
    merged = mine.shape[0] == 1

    moves = [
        pltpu.make_async_copy(rows_hbm, rows_ref, sem.at[0]),
        pltpu.make_async_copy(cls, cls_ref.at[0], sem.at[1]),
        pltpu.make_async_copy(cls_pair, cls_ref.at[1], sem.at[2]),
    ]
    for move in moves:
        move.start()
    acc[...] = acc_in[pl.ds(pl.multiple_of(lo * block, block), rows), :]
    for k in range(mine.shape[0]):
        for ref, x in ((mine, side), (other, 1 - side)):
            part = ref.shape[1]
            put(src, pl.multiple_of(k * rows + x * part, part), ref[k])
    halo_at = mine.shape[0] * rows
    if not chunk:
        put(src, halo_at, halo[...])
    for move in moves:
        move.wait()

    def far(c):
        above = jnp.logical_and(c == 1, sec + shift < secs)
        below = jnp.logical_and(c == 2, sec >= shift)
        return jnp.logical_or(above, below), jnp.where(c == 1, 0, 0 if merged else rows)

    def either(own, pair, t, *index):
        here = index + (lax.rem(t, terms),)
        return jnp.where(t < terms, own[here], pair[here])

    classes = [cls_ref[g, t] for g in range(2) for t in range(terms)]
    right_of = functools.partial(either, right, right_pair)
    n = pack(classes, far, order, offsets)
    left_of = lambda s, t: either(left, left_pair, t, lo + s)
    add_terms(n, order, offsets, src, right_of, left_of, acc, tbuf)
    if not chunk:
        n = pack(classes, lambda c: (c == 4 - core, halo_at), order, offsets)
        edge = core * (count - 1)
        left_of = lambda s, t: either(left, left_pair, t, lo + edge)
        edge_rows = acc.at[pl.ds(pl.multiple_of(edge * block, block), block), :]
        add_terms(n, order, offsets, src, right_of, left_of, edge_rows, tbuf)

    cross = jnp.zeros((8, cols), F32)
    square = jnp.zeros((8, cols), F32)
    for s in range(count):
        sector = core * half + lo + s
        here = pl.ds(s * block, block)
        total = masked(acc[here, :], rows_ref[sector])
        acc[here, :] = total
        value = sector_rows(live, sector, block)[...]
        fold = lambda v: jnp.sum(v.reshape(block // 8, 8, cols), axis=0)
        cross += fold(value * total)
        square += fold(value * value)
    fold = lambda v: sum(v[:, i : i + 128] for i in range(0, cols, 128))
    cross, square = fold(cross), fold(square)
    if chunk:
        cross, square = cross + sums_in[0:8, :], square + sums_in[8:16, :]
    sums[0:8, :] = cross
    sums[8:16, :] = square
    if chunk:
        whole[rows:, :] = jnp.zeros((whole.shape[0] - rows, cols), F32)
        whole[rows : rows + 16, 0:128] = sums[...]


def add_kernel(part, recv, total):
    total[...] = part[...] + recv[...]


def combine_kernel(total_a, part_b, recv_b, sums, first, second, third, total):
    at = total_a.shape[0]
    rows = 2 * at
    even = place()[0] == 0
    total[0:at, :] = total_a[...]
    total[at:rows, :] = part_b[0:at, :] + recv_b[0:at, :]
    total[rows:, :] = jnp.zeros((total.shape[0] - rows, total.shape[1]), F32)
    rest = second[...] + third[...]
    total[rows : rows + 16, 0:128] = jnp.where(even, (sums[...] + first[...]) + rest, first[...])
    total[rows + 16 : rows + 32, 0:128] = jnp.where(even, 0.0, rest)
    total[rows + 32 : rows + 48, 0:128] = recv_b[at : at + 16, 0:128]


def final_kernel(sides, half, live, total, total_pair, applied, correction, buf, sem):
    core, _, _ = place()
    rows = live.shape[0] // 2
    block = rows // half
    part = rows // 2
    moves = []
    places = []

    def send(source, target, kind, i):
        moves.append(pltpu.make_async_copy(source, target, sem.at[kind, i]))
        moves[-1].start()

    for ref, c in ((total, core), (total_pair, 1 - core)):
        for chunk in range(2):
            first = (c * half + chunk_start(chunk, c, half)) * block
            here = pl.ds(pl.multiple_of(first, block), part)
            source = ref.at[pl.ds(chunk * part, part), :]
            places.append((source, here))
            send(source, applied.at[here, :], 0, len(places) - 1)
    either = lambda c, at: jnp.where(core == c, total[at : at + 16, 0:128], total_pair[at : at + 16, 0:128])
    nearest = total[rows + 32 : rows + 48, 0:128] + total_pair[rows + 32 : rows + 48, 0:128]
    sums = either(0, rows) + ((nearest + either(1, rows)) + either(1, rows + 16))
    rayleigh = jnp.sum(sums[0:8, :]) / (jnp.sum(sums[8:16, :]) * (1.0 / sides))
    for i, (source, here) in enumerate(places):
        buf[here, :] = source[...] - rayleigh * live[here, :]
        send(buf.at[here, :], correction.at[here, :], 1, i)
    for move in moves:
        move.wait()


def params(limit):
    return pltpu.CompilerParams(vmem_limit_bytes=limit * 2**20)


def cost(flops, moved):
    return pl.CostEstimate(flops=int(flops), bytes_accessed=int(moved), transcendentals=0)


def shape(*dims):
    return jax.ShapeDtypeStruct(dims, F32)


def swap(array, axis, bit):
    pairs = [(i, i ^ bit) for i in range(lax.axis_size(axis))]
    return lax.ppermute(array, axis, pairs)


def far_parts(sums):
    parts = []
    for bit in range(1, 4):
        pairs = [(4 * z + m, 4 * (z ^ bit) + (m ^ 2 if m % 2 else m)) for z in range(4) for m in range(4)]
        parts.append(lax.ppermute(sums, ("sec", "mpo"), pairs))
    return parts


def after(array, *others):
    return lax.optimization_barrier((array, *others))[0]


def local(wavefunction, left_blocks, right_blocks, block_rows, term_charge):
    sector_count = block_rows.shape[0]
    block = left_blocks.shape[2]
    terms = left_blocks.shape[1]
    cols = wavefunction.shape[1]
    secs, mpos, reps = (lax.axis_size(a) for a in ("sec", "mpo", "rep"))
    half = sector_count // 2
    part = half // 2
    shift = QD // sector_count
    merged = secs <= 2 * shift
    whole = wavefunction
    if reps > 1:
        whole = lax.all_gather(wavefunction, "rep", axis=1, tiled=True)
    wide = whole.shape[1]

    up = [(i, i - shift) for i in range(shift, secs)]
    down = [(i, i + shift) for i in range(secs - shift)]

    def far(array):
        if merged:
            return lax.ppermute(array, "sec", up + down)[None]
        return jnp.stack([lax.ppermute(array, "sec", p) for p in (up, down)])

    halo_pairs = []
    for m in range(mpos):
        for z in range(secs):
            to = z + 1 if m % 2 == 0 else z - 1
            if 0 <= to < secs:
                halo_pairs.append((z * mpos + m, to * mpos + m))

    blocks = shape(half, terms, block, block)
    source_shape = ((half + 2) * block, 3 * wide)
    cls_pair = swap(term_charge, "mpo", 1)
    mine_a, mine_b, halo = pl.pallas_call(
        functools.partial(prepare_kernel, half),
        out_shape=(shape(part * block // 2, wide),) * 2 + (shape(block, wide),),
        in_specs=[ANY] * 2,
        out_specs=(VMEM,) * 3,
        scratch_shapes=[pltpu.SMEM((sector_count,), jnp.int32), pltpu.SemaphoreType.DMA((4,))],
        compiler_params=params(PREPARE_VMEM),
        cost_estimate=cost(1, 1),
        name="prepare",
    )(block_rows, whole)
    (left_send,) = pl.pallas_call(
        functools.partial(cut_kernel, half),
        out_shape=(blocks,),
        in_specs=[ANY],
        out_specs=(VMEM,),
        scratch_shapes=[pltpu.SemaphoreType.DMA((1,))],
        compiler_params=params(CUT_VMEM),
        cost_estimate=cost(1, 1),
        name="pair_blocks",
    )(after(left_blocks, mine_a, cls_pair))
    left_pair = swap(left_send, "mpo", 1)
    far_a = far(mine_a)
    right_pair = swap(after(right_blocks, left_send), "mpo", 1)

    lists = [pltpu.SMEM((2 * terms,), jnp.int32)] * 2

    def near(name, *args):
        chained = len(args) == 5
        return pl.pallas_call(
            functools.partial(near_kernel, chained),
            out_shape=shape(half * block, cols),
            in_specs=[ANY] + [VMEM] * (len(args) - 1),
            out_specs=VMEM,
            scratch_shapes=[pltpu.VMEM((half, 2 * GROUPS[0] * block, cols), BF16), pltpu.SMEM((terms,), jnp.int32)]
            + lists
            + [pltpu.SemaphoreType.DMA((1,))],
            compiler_params=params(NEAR_VMEM),
            cost_estimate=cost(1, 1),
            name=name,
        )(*args)

    def add_far(chunk, *args):
        rows = part * block
        return pl.pallas_call(
            functools.partial(far_kernel, chunk, shift, secs),
            out_shape=(shape(rows + 16 * chunk, cols), shape(16, 128)),
            in_specs=[ANY] * 3 + [VMEM] * (5 + len(args)),
            out_specs=(VMEM, VMEM),
            scratch_shapes=[
                pltpu.VMEM(((1 if merged else 2) * rows + block, 3 * wide), BF16),
                pltpu.VMEM((part, 2 * GROUPS[0] * block, cols), BF16),
                pltpu.SMEM((sector_count,), jnp.int32),
                pltpu.SMEM((2, terms), jnp.int32),
                *lists,
                pltpu.SemaphoreType.DMA((3,)),
            ],
            compiler_params=params(NEAR_VMEM),
            cost_estimate=cost(1, 1),
            name="far",
        )(term_charge, cls_pair, block_rows, left, right, left_pair, right_pair, live, *args)

    left, right, src, live = pl.pallas_call(
        load_kernel,
        out_shape=(
            blocks,
            shape(terms, wide, cols),
            jax.ShapeDtypeStruct(source_shape, BF16),
            shape(sector_count * block, cols),
        ),
        in_specs=[ANY] * 3 + [VMEM] * 2,
        out_specs=(VMEM,) * 4,
        scratch_shapes=[pltpu.SMEM((sector_count,), jnp.int32), pltpu.SemaphoreType.DMA((3,))],
        compiler_params=params(OWN_VMEM),
        cost_estimate=cost(1, 1),
        name="own_terms",
    )(left_blocks, right_blocks, after(block_rows, mine_a), whole, wavefunction)
    far_b = far(after(mine_b, src))
    acc = near("own_near", term_charge, left, right, src)
    halo = lax.ppermute(after(halo, acc), ("sec", "mpo"), halo_pairs)
    other_a = swap(after(far_a, acc), "mpo", 2)
    acc = near("pair_near", cls_pair, left_pair, right_pair, src, acc)
    other_b = swap(after(far_b, acc), "mpo", 2)
    part_a, sums = add_far(0, far_a, other_a, acc, halo)
    recv_a = swap(part_a, "mpo", 2)
    part_b, sums = add_far(1, far_b, other_b, acc, sums)
    recv_b = swap(part_b, "mpo", 2)
    if secs == 4 and mpos == 4 and reps == 1:
        sums = sums + swap(sums, "mpo", 1)
        parts = far_parts(sums)
    else:
        own = sums
        sums = lax.psum(sums, ("sec", "rep", "mpo"))
        parts = [jnp.zeros_like(sums)] * 2 + [-swap(own, "mpo", 2)]
        parts[2] = parts[2] + swap(parts[2], "mpo", 1)
    total_a = pl.pallas_call(
        add_kernel,
        out_shape=shape(part * block, cols),
        in_specs=[VMEM] * 2,
        out_specs=VMEM,
        compiler_params=params(NEAR_VMEM),
        cost_estimate=cost(1e9, 1),
        name="first_total",
    )(part_a, recv_a)
    total = pl.pallas_call(
        combine_kernel,
        out_shape=shape(half * block + 48, cols),
        in_specs=[VMEM] * 7,
        out_specs=VMEM,
        compiler_params=params(NEAR_VMEM),
        cost_estimate=cost(1, 1),
        name="totals",
    )(total_a, part_b, recv_b, sums, *parts)
    total_pair = swap(total, "mpo", 1)

    out = shape(sector_count * block, cols)
    return pl.pallas_call(
        functools.partial(final_kernel, mpos // 2, half),
        out_shape=(out, out),
        in_specs=[VMEM] * 3,
        out_specs=(ANY, ANY),
        scratch_shapes=[pltpu.VMEM((sector_count * block, cols), F32), pltpu.SemaphoreType.DMA((2, 4))],
        compiler_params=params(32),
        cost_estimate=cost(1, 1),
        name="residual",
    )(live, total, total_pair)


def solution(mesh):
    in_specs = (
        P(("runs", "sec"), "rep"),
        P(("runs", "sec"), "mpo", None, None),
        P(("runs", "mpo"), None, "rep"),
        P(("runs", "sec")),
        P("mpo"),
    )
    out_specs = (P(("runs", "sec"), "rep"), P(("runs", "sec"), "rep"))
    return jax.shard_map(local, mesh=mesh, in_specs=in_specs, out_specs=out_specs, check_vma=False)
```

```python
import functools

import jax
import jax.numpy as jnp
from jax import lax
from jax.experimental import pallas as pl
from jax.experimental.pallas import tpu as pltpu
from jax.sharding import PartitionSpec as P

QD = 16
F32 = jnp.float32
BF16 = jnp.bfloat16
VMEM = pl.BlockSpec(memory_space=pltpu.VMEM)
SMEM = pl.BlockSpec(memory_space=pltpu.SMEM)
HBM = pl.BlockSpec(memory_space=pltpu.HBM)
ANY = pl.BlockSpec(memory_space=pl.ANY)


def split(x):
    high = x.astype(BF16)
    return high, (x - high.astype(F32)).astype(BF16)


def masked(rows, live):
    index = lax.broadcasted_iota(jnp.int32, rows.shape, 0)
    return jnp.where(index < live, rows, 0.0)


PREPARE_VMEM, CUT_VMEM, OWN_VMEM, NEAR_VMEM = 62, 50, 46, 32
GROUPS = (4, 2)


def place():
    mpo = lax.axis_index("mpo")
    return lax.rem(mpo, 2), lax.rem(lax.div(mpo, 2), 2), lax.axis_index("sec")


def chunk_start(chunk, core, half):
    return (1 - core if chunk else core) * (half // 2)


def sector_rows(wave, sector, block):
    return wave.at[pl.ds(pl.multiple_of(sector * block, block), block), :]


def prepare_kernel(half, rows_hbm, wave, *refs):
    *sends, halo, rows_ref, sem = refs
    core, side, _ = place()
    block = halo.shape[0]
    piece = block // 2
    rows = pltpu.make_async_copy(rows_hbm, rows_ref, sem.at[0])
    rows.start()
    wanted = [(halo, (1 - core) * (2 * half - 1) * block)]
    for i, ref in enumerate(sends):
        wanted.append((ref, (core * half + chunk_start(i, core, half)) * block + side * ref.shape[0]))
    reads = []
    for i, (ref, first) in enumerate(wanted):
        source = wave.at[pl.ds(pl.multiple_of(first, piece), ref.shape[0]), :]
        reads.append(pltpu.make_async_copy(source, ref, sem.at[i + 1]))
        reads[i].start()
    rows.wait()
    for read, (ref, first) in zip(reads, wanted):
        read.wait()
        for at in range(0, ref.shape[0], piece):
            here = pl.ds(at, piece)
            live = rows_ref[lax.div(first + at, block)] - lax.rem(first + at, block)
            ref[here, :] = masked(ref[here, :], live)


def cut_kernel(half, left, left_send, sem):
    core, _, _ = place()
    move = pltpu.make_async_copy(left.at[pl.ds((1 - core) * half, half)], left_send, sem.at[0])
    move.start()
    move.wait()


def put(src, at, value):
    wide = value.shape[1]
    high, low = split(value)
    here = pl.ds(at, value.shape[0])
    src[here, 0:wide] = high
    src[here, wide : 2 * wide] = low
    src[here, 2 * wide : 3 * wide] = high


def pack(classes, choose, order, offsets):
    n = jnp.int32(0)
    for t, c in enumerate(classes):
        chosen, at = choose(c)

        @pl.when(chosen)
        def _(n=n, t=t, at=at):
            order[n] = t
            offsets[n] = at

        n = n + chosen.astype(jnp.int32)
    return n


def add_terms(n, order, offsets, src, right_of, left_of, acc, tbuf):
    rows = acc.shape[0]
    block = tbuf.shape[1] // (2 * max(GROUPS))
    count = rows // block

    def add(begin, group):
        terms, real = [], []
        for j in range(group):
            k = jnp.minimum(begin + j, n - 1)
            real.append(begin + j < n)
            terms.append(order[k])
            at = pl.ds(pl.multiple_of(offsets[k], block), rows)
            high, low = split(right_of(terms[j]))
            wide = jnp.concatenate([high, high, low], 0)
            high, low = split(jnp.dot(src[at, :], wide, preferred_element_type=F32))
            for s in range(count):
                here = slice(s * block, (s + 1) * block)
                tbuf[s, j * block : (j + 1) * block, :] = high[here]
                tbuf[s, (group + j) * block : (group + j + 1) * block, :] = low[here]
        for s in range(count):
            blocks = [left_of(s, terms[0])]
            for j in range(1, group):
                blocks.append(jnp.where(real[j], left_of(s, terms[j]), 0.0))
            high, low = split(jnp.concatenate(blocks, 1))
            acc[s * block : (s + 1) * block, :] += jnp.dot(
                jnp.concatenate([high, high, low], 1),
                jnp.concatenate([tbuf[s, 0 : 2 * group * block], tbuf[s, 0 : group * block]], 0),
                preferred_element_type=F32,
            )

    large, small = GROUPS
    full = lax.div(n + large - small - 1, large)

    @pl.loop(0, full)
    def _(i):
        add(i * large, large)

    @pl.when(n > full * large)
    def _():
        add(full * large, small)


def load_kernel(left_hbm, right_hbm, rows_hbm, whole, wave, left, right, src, live, rows_ref, sem):
    half, terms, block, _ = left.shape
    core, _, _ = place()
    rows = pltpu.make_async_copy(rows_hbm, rows_ref, sem.at[0])
    moves = [
        pltpu.make_async_copy(left_hbm.at[pl.ds(core * half, half)], left, sem.at[1]),
        pltpu.make_async_copy(right_hbm, right, sem.at[2]),
    ]
    for move in [rows] + moves:
        move.start()
    halo_at = pl.multiple_of(core * (half + 1) * block, block)
    src[pl.ds(halo_at, block), :] = jnp.zeros((block, src.shape[1]), BF16)
    rows.wait()
    for s in range(2 * half):
        here = pl.ds(s * block, block)
        live[here, :] = masked(wave[here, :], rows_ref[s])
    for i in range(half + 1):
        sector = core * (half - 1) + i
        value = masked(sector_rows(whole, sector, block)[...], rows_ref[sector])
        put(src, pl.multiple_of((i + 1 - core) * block, block), value)
    for move in moves:
        move.wait()


def near_kernel(chained, cls, left, right, src, *refs):
    acc_in, refs = (refs[0], refs[1:]) if chained else (None, refs)
    acc, tbuf, cls_ref, order, offsets, sem = refs
    block = left.shape[-1]
    fetch = pltpu.make_async_copy(cls, cls_ref, sem.at[0])
    fetch.start()
    acc[...] = acc_in[...] if chained else jnp.zeros_like(acc)
    fetch.wait()

    def near(c):
        at = jnp.where(c == 0, block, jnp.where(c == 3, 2 * block, 0))
        return jnp.logical_or(c == 0, c >= 3), at

    n = pack([cls_ref[t] for t in range(right.shape[0])], near, order, offsets)
    add_terms(n, order, offsets, src, lambda t: right[t], lambda s, t: left[s, t], acc, tbuf)


def far_kernel(chunk, shift, secs, *refs):
    refs = list(refs)
    cls, cls_pair, rows_hbm, left, right, left_pair, right_pair, live, mine, other, acc_in = refs[:11]
    halo, sums_in = (None, refs.pop(11)) if chunk else (refs.pop(11), None)
    acc, sums, src, tbuf, rows_ref, cls_ref, order, offsets, sem = refs[11:]
    cols = acc.shape[1]
    half, terms, block, _ = left.shape
    rows = half // 2 * block
    whole, acc = acc, acc.at[pl.ds(0, rows), :]
    count = rows // block
    core, side, sec = place()
    lo = chunk_start(chunk, core, half)
    merged = mine.shape[0] == 1

    moves = [
        pltpu.make_async_copy(rows_hbm, rows_ref, sem.at[0]),
        pltpu.make_async_copy(cls, cls_ref.at[0], sem.at[1]),
        pltpu.make_async_copy(cls_pair, cls_ref.at[1], sem.at[2]),
    ]
    for move in moves:
        move.start()
    acc[...] = acc_in[pl.ds(pl.multiple_of(lo * block, block), rows), :]
    for k in range(mine.shape[0]):
        for ref, x in ((mine, side), (other, 1 - side)):
            part = ref.shape[1]
            put(src, pl.multiple_of(k * rows + x * part, part), ref[k])
    halo_at = mine.shape[0] * rows
    if not chunk:
        put(src, halo_at, halo[...])
    for move in moves:
        move.wait()

    def far(c):
        above = jnp.logical_and(c == 1, sec + shift < secs)
        below = jnp.logical_and(c == 2, sec >= shift)
        return jnp.logical_or(above, below), jnp.where(c == 1, 0, 0 if merged else rows)

    def either(own, pair, t, *index):
        here = index + (lax.rem(t, terms),)
        return jnp.where(t < terms, own[here], pair[here])

    classes = [cls_ref[g, t] for g in range(2) for t in range(terms)]
    right_of = functools.partial(either, right, right_pair)
    n = pack(classes, far, order, offsets)
    left_of = lambda s, t: either(left, left_pair, t, lo + s)
    add_terms(n, order, offsets, src, right_of, left_of, acc, tbuf)
    if not chunk:
        n = pack(classes, lambda c: (c == 4 - core, halo_at), order, offsets)
        edge = core * (count - 1)
        left_of = lambda s, t: either(left, left_pair, t, lo + edge)
        edge_rows = acc.at[pl.ds(pl.multiple_of(edge * block, block), block), :]
        add_terms(n, order, offsets, src, right_of, left_of, edge_rows, tbuf)

    cross = jnp.zeros((8, cols), F32)
    square = jnp.zeros((8, cols), F32)
    for s in range(count):
        sector = core * half + lo + s
        here = pl.ds(s * block, block)
        total = masked(acc[here, :], rows_ref[sector])
        acc[here, :] = total
        value = sector_rows(live, sector, block)[...]
        fold = lambda v: jnp.sum(v.reshape(block // 8, 8, cols), axis=0)
        cross += fold(value * total)
        square += fold(value * value)
    fold = lambda v: sum(v[:, i : i + 128] for i in range(0, cols, 128))
    cross, square = fold(cross), fold(square)
    if chunk:
        cross, square = cross + sums_in[0:8, :], square + sums_in[8:16, :]
    sums[0:8, :] = cross
    sums[8:16, :] = square
    if chunk:
        whole[rows:, :] = jnp.zeros((whole.shape[0] - rows, cols), F32)
        whole[rows : rows + 16, 0:128] = sums[...]


def add_kernel(part, recv, total):
    total[...] = part[...] + recv[...]


def pass_kernel(source, target):
    target[...] = source[...]


def combine_kernel(total_a, part_b, recv_b, sums, first, second, third, total):
    at = total_a.shape[0]
    rows = 2 * at
    even = place()[0] == 0
    total[0:at, :] = total_a[...]
    total[at:rows, :] = part_b[0:at, :] + recv_b[0:at, :]
    total[rows:, :] = jnp.zeros((total.shape[0] - rows, total.shape[1]), F32)
    rest = second[...] + third[...]
    total[rows : rows + 16, 0:128] = jnp.where(even, (sums[...] + first[...]) + rest, first[...])
    total[rows + 16 : rows + 32, 0:128] = jnp.where(even, 0.0, rest)
    total[rows + 32 : rows + 48, 0:128] = recv_b[at : at + 16, 0:128]


def final_kernel(sides, half, live, total, total_pair, applied, correction, buf, sem):
    core, _, _ = place()
    rows = live.shape[0] // 2
    block = rows // half
    part = rows // 2
    moves = []
    places = []

    def send(source, target, kind, i):
        moves.append(pltpu.make_async_copy(source, target, sem.at[kind, i]))
        moves[-1].start()

    for ref, c in ((total, core), (total_pair, 1 - core)):
        for chunk in range(2):
            first = (c * half + chunk_start(chunk, c, half)) * block
            here = pl.ds(pl.multiple_of(first, block), part)
            source = ref.at[pl.ds(chunk * part, part), :]
            places.append((source, here))
            send(source, applied.at[here, :], 0, len(places) - 1)
    either = lambda c, at: jnp.where(core == c, total[at : at + 16, 0:128], total_pair[at : at + 16, 0:128])
    nearest = total[rows + 32 : rows + 48, 0:128] + total_pair[rows + 32 : rows + 48, 0:128]
    sums = either(0, rows) + ((nearest + either(1, rows)) + either(1, rows + 16))
    rayleigh = jnp.sum(sums[0:8, :]) / (jnp.sum(sums[8:16, :]) * (1.0 / sides))
    for i, (source, here) in enumerate(places):
        buf[here, :] = source[...] - rayleigh * live[here, :]
        send(buf.at[here, :], correction.at[here, :], 1, i)
    for move in moves:
        move.wait()


def params(limit):
    return pltpu.CompilerParams(vmem_limit_bytes=limit * 2**20)


def cost(flops, moved):
    return pl.CostEstimate(flops=int(flops), bytes_accessed=int(moved), transcendentals=0)


def shape(*dims):
    return jax.ShapeDtypeStruct(dims, F32)


def swap(array, axis, bit):
    pairs = [(i, i ^ bit) for i in range(lax.axis_size(axis))]
    return lax.ppermute(array, axis, pairs)


def far_parts(sums):
    parts = []
    for bit in range(1, 4):
        pairs = [(4 * z + m, 4 * (z ^ bit) + (m ^ 2 if m % 2 else m)) for z in range(4) for m in range(4)]
        parts.append(lax.ppermute(sums, ("sec", "mpo"), pairs))
    return parts


def after(array, *others):
    return lax.optimization_barrier((array, *others))[0]


def local(wavefunction, left_blocks, right_blocks, block_rows, term_charge):
    sector_count = block_rows.shape[0]
    block = left_blocks.shape[2]
    terms = left_blocks.shape[1]
    cols = wavefunction.shape[1]
    secs, mpos, reps = (lax.axis_size(a) for a in ("sec", "mpo", "rep"))
    half = sector_count // 2
    part = half // 2
    shift = QD // sector_count
    merged = secs <= 2 * shift
    whole = wavefunction
    if reps > 1:
        whole = lax.all_gather(wavefunction, "rep", axis=1, tiled=True)
    wide = whole.shape[1]

    up = [(i, i - shift) for i in range(shift, secs)]
    down = [(i, i + shift) for i in range(secs - shift)]

    def far(array):
        if merged:
            return lax.ppermute(array, "sec", up + down)[None]
        return jnp.stack([lax.ppermute(array, "sec", p) for p in (up, down)])

    halo_pairs = []
    for m in range(mpos):
        for z in range(secs):
            to = z + 1 if m % 2 == 0 else z - 1
            if 0 <= to < secs:
                halo_pairs.append((z * mpos + m, to * mpos + m))

    blocks = shape(half, terms, block, block)
    source_shape = ((half + 2) * block, 3 * wide)
    cls_pair = swap(term_charge, "mpo", 1)
    mine_a, mine_b, halo = pl.pallas_call(
        functools.partial(prepare_kernel, half),
        out_shape=(shape(part * block // 2, wide),) * 2 + (shape(block, wide),),
        in_specs=[ANY] * 2,
        out_specs=(VMEM,) * 3,
        scratch_shapes=[pltpu.SMEM((sector_count,), jnp.int32), pltpu.SemaphoreType.DMA((4,))],
        compiler_params=params(PREPARE_VMEM),
        cost_estimate=cost(1, 1),
        name="prepare",
    )(block_rows, whole)
    (left_send,) = pl.pallas_call(
        functools.partial(cut_kernel, half),
        out_shape=(blocks,),
        in_specs=[ANY],
        out_specs=(VMEM,),
        scratch_shapes=[pltpu.SemaphoreType.DMA((1,))],
        compiler_params=params(CUT_VMEM),
        cost_estimate=cost(1, 1),
        name="pair_blocks",
    )(after(left_blocks, mine_a))
    left_pair = swap(after(left_send, cls_pair), "mpo", 1)
    far_a = far(mine_a)
    right_pair = swap(after(right_blocks, left_send, cls_pair), "mpo", 1)

    lists = [pltpu.SMEM((2 * terms,), jnp.int32)] * 2

    def near(name, *args):
        chained = len(args) == 5
        return pl.pallas_call(
            functools.partial(near_kernel, chained),
            out_shape=shape(half * block, cols),
            in_specs=[ANY] + [VMEM] * (len(args) - 1),
            out_specs=VMEM,
            scratch_shapes=[pltpu.VMEM((half, 2 * GROUPS[0] * block, cols), BF16), pltpu.SMEM((terms,), jnp.int32)]
            + lists
            + [pltpu.SemaphoreType.DMA((1,))],
            compiler_params=params(NEAR_VMEM),
            cost_estimate=cost(1, 1),
            name=name,
        )(*args)

    def add_far(chunk, *args):
        rows = part * block
        return pl.pallas_call(
            functools.partial(far_kernel, chunk, shift, secs),
            out_shape=(shape(rows + 16 * chunk, cols), shape(16, 128)),
            in_specs=[ANY] * 3 + [VMEM] * (5 + len(args)),
            out_specs=(VMEM, VMEM),
            scratch_shapes=[
                pltpu.VMEM(((1 if merged else 2) * rows + block, 3 * wide), BF16),
                pltpu.VMEM((part, 2 * GROUPS[0] * block, cols), BF16),
                pltpu.SMEM((sector_count,), jnp.int32),
                pltpu.SMEM((2, terms), jnp.int32),
                *lists,
                pltpu.SemaphoreType.DMA((3,)),
            ],
            compiler_params=params(NEAR_VMEM),
            cost_estimate=cost(1, 1),
            name="far",
        )(term_charge, cls_pair, block_rows, left, right, left_pair, right_pair, live, *args)

    left, right, src, live = pl.pallas_call(
        load_kernel,
        out_shape=(
            blocks,
            shape(terms, wide, cols),
            jax.ShapeDtypeStruct(source_shape, BF16),
            shape(sector_count * block, cols),
        ),
        in_specs=[ANY] * 3 + [VMEM] * 2,
        out_specs=(VMEM,) * 4,
        scratch_shapes=[pltpu.SMEM((sector_count,), jnp.int32), pltpu.SemaphoreType.DMA((3,))],
        compiler_params=params(OWN_VMEM),
        cost_estimate=cost(1, 1),
        name="own_terms",
    )(left_blocks, right_blocks, after(block_rows, mine_a, left_send, cls_pair), whole, wavefunction)
    far_b = far(after(mine_b, src))
    acc = near("own_near", term_charge, left, right, src)
    halo = lax.ppermute(after(halo, acc), ("sec", "mpo"), halo_pairs)
    far_a = pl.pallas_call(
        pass_kernel,
        out_shape=jax.ShapeDtypeStruct(far_a.shape, F32),
        in_specs=[VMEM],
        out_specs=VMEM,
        compiler_params=params(NEAR_VMEM),
        cost_estimate=cost(5e10, 1),
        name="first_far",
    )(after(far_a, acc))
    other_a = swap(far_a, "mpo", 2)
    acc = near("pair_near", cls_pair, left_pair, right_pair, src, acc)
    other_b = swap(after(far_b, acc), "mpo", 2)
    part_a, sums = add_far(0, far_a, other_a, acc, halo)
    recv_a = swap(part_a, "mpo", 2)
    part_b, sums = add_far(1, far_b, other_b, acc, sums)
    recv_b = swap(part_b, "mpo", 2)
    if secs == 4 and mpos == 4 and reps == 1:
        sums = sums + swap(sums, "mpo", 1)
        parts = far_parts(sums)
    else:
        own = sums
        sums = lax.psum(sums, ("sec", "rep", "mpo"))
        parts = [jnp.zeros_like(sums)] * 2 + [-swap(own, "mpo", 2)]
        parts[2] = parts[2] + swap(parts[2], "mpo", 1)
    total_a = pl.pallas_call(
        add_kernel,
        out_shape=shape(part * block, cols),
        in_specs=[VMEM] * 2,
        out_specs=VMEM,
        compiler_params=params(NEAR_VMEM),
        cost_estimate=cost(1e9, 1),
        name="first_total",
    )(part_a, recv_a)
    total = pl.pallas_call(
        combine_kernel,
        out_shape=shape(half * block + 48, cols),
        in_specs=[VMEM] * 7,
        out_specs=VMEM,
        compiler_params=params(NEAR_VMEM),
        cost_estimate=cost(1, 1),
        name="totals",
    )(total_a, part_b, recv_b, sums, *parts)
    total_pair = swap(total, "mpo", 1)

    out = shape(sector_count * block, cols)
    return pl.pallas_call(
        functools.partial(final_kernel, mpos // 2, half),
        out_shape=(out, out),
        in_specs=[VMEM] * 3,
        out_specs=(ANY, ANY),
        scratch_shapes=[pltpu.VMEM((sector_count * block, cols), F32), pltpu.SemaphoreType.DMA((2, 4))],
        compiler_params=params(32),
        cost_estimate=cost(1, 1),
        name="residual",
    )(live, total, total_pair)


def solution(mesh):
    in_specs = (
        P(("runs", "sec"), "rep"),
        P(("runs", "sec"), "mpo", None, None),
        P(("runs", "mpo"), None, "rep"),
        P(("runs", "sec")),
        P("mpo"),
    )
    out_specs = (P(("runs", "sec"), "rep"), P(("runs", "sec"), "rep"))
    return jax.shard_map(local, mesh=mesh, in_specs=in_specs, out_specs=out_specs, check_vma=False)
```
